32 devices in a mesh: cells: 8 (over z, core), genes: 4 (over y, x).
Axes of the slice: x: 2, y: 2, z: 4, core: 2. Of those that a mesh axis runs over, the one named last changes fastest.
Arguments:
- sketch: bfloat16 [8192, 256], P('cells'), may hold values from -6 to 6
- tiles: bfloat16 [3072, 128, 128], P(('cells', 'genes')), may hold values from -0.0546875 to 0.0546875
- tile_rows: int32 [3072], P(('cells', 'genes')), may hold values from 0 to 7, as said below
- tile_cols: int32 [3072], P(('cells', 'genes')), may hold values from 0 to 15
- tile_counts: int32 [32], P(('cells', 'genes')), may hold values from 16 to 96, as said below
Outputs:
- projected: float32 [8192, 256], P(('cells', 'genes'))
The draws below stay inside these ranges and needn't reach their ends.
Inputs may be any that keep to these rules, and one draw needn't show every extreme that they name: Within one device's slots the pairs (tile_rows, tile_cols) are distinct. `tile_counts`: some device holds 96 tiles and the device half the cells axis away from it holds 16.
All inputs are finite; a program needn't handle non-finite values.
Results may differ from the reference program's by a relative error of at most 0.0021.
Values may be sent and summed in bfloat16 or wider, within the bound.
No kernel may reach another device: no remote copies, remote signals or barrier semaphores. Data moves between devices by JAX's collectives and lax.ppermute only.
A program may use at most 128 MiB of HBM per device.

```python
import jax
import jax.numpy as jnp
from jax import lax

TILE = 128
RANK = 256
GENE_BLOCKS = 16
ROW_BLOCKS = 8
TMAX = 96
TMIN = 16
UNITS = 32
CELLS = 8192
N_CELLS = 8
N_GENES = 4


def place_slots(key):
    device_keys = jax.random.split(jax.random.fold_in(key, 11), UNITS)

    def one_device(device_key):
        return jax.random.permutation(device_key, ROW_BLOCKS * GENE_BLOCKS)[:TMAX]
    return jax.vmap(one_device)(device_keys).reshape(UNITS * TMAX).astype(jnp.int32)


def draw_tile_rows(key, part):
    return place_slots(key) // GENE_BLOCKS


def draw_tile_cols(key, part):
    return place_slots(key) % GENE_BLOCKS


def draw_tile_counts(key, part):
    first_draw = jax.random.randint(jax.random.fold_in(key, 1), (UNITS,), TMIN, TMAX + 1)
    second_draw = jax.random.randint(jax.random.fold_in(key, 2), (UNITS,), TMIN, TMAX + 1)
    third_draw = jax.random.randint(jax.random.fold_in(key, 3), (UNITS,), TMIN, TMAX + 1)
    counts = jnp.minimum(jnp.minimum(first_draw, second_draw), third_draw)
    counts = counts.at[0].set(TMAX).at[N_CELLS // 2 * N_GENES].set(TMIN)
    return counts.astype(jnp.int32)


def level_of(rng, shape, cuts, smallest, largest):
    loudness = 1.0
    for dim, blocks in cuts:
        heights = jax.random.uniform(jax.random.fold_in(jax.random.fold_in(rng, 6), dim), (blocks,), jnp.float32, smallest / len(cuts), largest / len(cuts))
        loudness = loudness * jnp.repeat(jnp.exp(heights), shape[dim] // blocks).reshape((-1,) + (1,) * (len(shape) - 1 - dim))
    return loudness


def bell_draw(key, extent, deviation, reach, shards=(), kind=jnp.bfloat16):
    array = deviation * jax.random.normal(key, extent, jnp.float32)
    if shards:
        array = array * level_of(key, extent, shards, -0.22, 0.18)
    return jnp.clip(array, -reach, reach).astype(kind)


def setup_inputs(seed: int = 0) -> dict:
    key_list = jax.random.split(jax.random.key(seed), 6)
    return {
        "sketch": bell_draw(key_list[0], (CELLS, RANK), 1.0, 6.0, ((0, 8),)),
        "tiles": bell_draw(key_list[1], (UNITS * TMAX, TILE, TILE), (TILE * TMAX) ** -0.5, 0.0546875, ((0, 32),)),
        "tile_rows": draw_tile_rows(jax.random.fold_in(key_list[5], 71), 0),
        "tile_cols": draw_tile_cols(jax.random.fold_in(key_list[5], 71), 0),
        "tile_counts": draw_tile_counts(jax.random.fold_in(key_list[5], 71), 0),
    }


def device_first(tile_set, row_ids, col_ids, count_one, sketch_rows):
    live_mask = (jnp.arange(TMAX, dtype=jnp.int32) < count_one).astype(jnp.float32)
    picked = sketch_rows[row_ids].astype(jnp.float32)
    contrib = jnp.einsum('ski,skr->sir', tile_set.astype(jnp.float32), picked)
    contrib = contrib * live_mask[:, None, None]
    return jnp.zeros((GENE_BLOCKS, TILE, RANK), jnp.float32).at[col_ids].add(contrib)


def device_second(tile_set, row_ids, col_ids, count_one, gene_rows):
    live_mask = (jnp.arange(TMAX, dtype=jnp.int32) < count_one).astype(jnp.float32)
    picked = gene_rows[col_ids].astype(jnp.float32)
    contrib = jnp.einsum('sik,skr->sir', tile_set.astype(jnp.float32), picked)
    contrib = contrib * live_mask[:, None, None]
    return jnp.zeros((ROW_BLOCKS, TILE, RANK), jnp.float32).at[row_ids].add(contrib)


def reference(sketch, tiles, tile_rows, tile_cols, tile_counts):
    tile_grid = tiles.reshape(N_CELLS, N_GENES, TMAX, TILE, TILE)
    row_grid = tile_rows.reshape(N_CELLS, N_GENES, TMAX)
    col_grid = tile_cols.reshape(N_CELLS, N_GENES, TMAX)
    count_grid = tile_counts.reshape(N_CELLS, N_GENES)
    sketch_grid = sketch.reshape(N_CELLS, ROW_BLOCKS, TILE, RANK)

    def gene_step(running, inputs):
        tile_set, row_ids, col_ids, count_row, sketch_rows = inputs
        partials = jax.vmap(device_first, in_axes=(0, 0, 0, 0, None))(tile_set, row_ids, col_ids, count_row, sketch_rows)
        return running + partials, None

    start_value = jnp.zeros((N_GENES, GENE_BLOCKS, TILE, RANK), jnp.float32)
    gene_side, _ = lax.scan(gene_step, start_value, (tile_grid, row_grid, col_grid, count_grid, sketch_grid))
    gene_cast = gene_side.astype(jnp.bfloat16)

    def cell_step(inputs):
        tile_set, row_ids, col_ids, count_row = inputs
        partials = jax.vmap(device_second)(tile_set, row_ids, col_ids, count_row, gene_cast)
        return jnp.sum(partials, axis=0)

    projected = lax.map(cell_step, (tile_grid, row_grid, col_grid, count_grid))
    return projected.reshape(N_CELLS * ROW_BLOCKS * TILE, RANK)
```

```python
import functools

import jax
import jax.numpy as jnp
from jax import lax
from jax.experimental import pallas as pl
from jax.experimental.pallas import tpu as pltpu
from jax.sharding import PartitionSpec as P

GENE_BLOCKS = 16
CORES = 2
MIB = 1 << 20

VMEM = pl.BlockSpec(memory_space=pltpu.VMEM)
SMEM = pl.BlockSpec(memory_space=pltpu.SMEM)
ANY = pl.BlockSpec(memory_space=pl.ANY)
f32, bf16, i16, i32 = jnp.float32, jnp.bfloat16, jnp.int16, jnp.int32


def encode(x, out, at=()):
    peak = jnp.max(jnp.abs(x), axis=0, keepdims=True)
    expo = jnp.ceil(jnp.log2(jnp.maximum(peak, 2.0**-100)))
    expo = jnp.clip(expo, -100.0, 126.0)
    code = jnp.round(x * jnp.exp2(14.0 - expo)).astype(i32)
    top = code[:16]
    row = lax.broadcasted_iota(i32, top.shape, 0)
    word = jnp.broadcast_to(expo.astype(i32) + 128, top.shape)
    marked = (top & ~1) | ((word >> jnp.minimum(row, 7)) & 1)
    top = jnp.where(row < 8, marked, top)
    out[at + (pl.ds(0, 16),)] = top.astype(i16)
    out[at + (pl.ds(16, x.shape[0] - 16),)] = code[16:].astype(i16)


def decode(code):
    code = code.astype(i32)
    head = code[:8]
    row = lax.broadcasted_iota(i32, head.shape, 0)
    word = jnp.sum((head & 1) << row, axis=0, keepdims=True)
    scale = jnp.exp2((word - (128 + 14)).astype(f32))
    return code.astype(f32) * scale


def core_and_chip():
    place = lax.axis_index("cells")
    return lax.rem(place, CORES), lax.div(place, CORES)


def call(body, outs, in_specs, scratch=(), mib=32, flops=0, nbytes=0):
    return pl.pallas_call(
        body,
        out_shape=outs,
        in_specs=in_specs,
        out_specs=jax.tree.map(lambda _: VMEM, outs),
        scratch_shapes=list(scratch),
        compiler_params=pltpu.CompilerParams(vmem_limit_bytes=mib * MIB),
        cost_estimate=pl.CostEstimate(flops=flops, bytes_accessed=nbytes, transcendentals=0),
    )


def dense_kernel(count, rows, cols, sketch, tiles, dense, turned, theirs, sems):
    tile = tiles.shape[1]
    core, _ = core_and_chip()

    def clear(i, _):
        dense[pl.ds(pl.multiple_of(i * 16, 16), 16), :] = jnp.zeros((16, dense.shape[1]), bf16)
        return 0

    lax.fori_loop(0, dense.shape[0] // 16, clear, 0)

    def copy(s):
        r = pl.multiple_of(rows[s] * tile, tile)
        c = pl.multiple_of(cols[s] * tile, tile)
        return pltpu.make_async_copy(tiles.at[s], dense.at[pl.ds(r, tile), pl.ds(c, tile)], sems.at[s])

    def start(s, _):
        copy(s).start()
        return 0

    def wait(s, _):
        copy(s).wait()
        return 0

    lax.fori_loop(0, count[0], start, 0)
    turned[...] = sketch[...].T
    lax.fori_loop(0, count[0], wait, 0)
    half = theirs.shape[0]
    left = turned[pl.ds(pl.multiple_of((1 - core) * half, half), half), :]
    width = 512
    for j in range(dense.shape[1] // width):
        part = jnp.dot(left, dense[:, j * width : (j + 1) * width], preferred_element_type=f32)
        encode_columns(part, theirs, j * width)


def encode_columns(x, out, at):
    encode(x, out.at[:, pl.ds(at, x.shape[1])])


def own_kernel(turned, dense, mine):
    core, _ = core_and_chip()
    half = mine.shape[0]
    left = turned[pl.ds(pl.multiple_of(core * half, half), half), :]
    mine[...] = jnp.dot(left, dense[...], preferred_element_type=f32)


def pair_kernel(mine, got, *outs):
    _, chip = core_and_chip()
    width = outs[0].shape[1]
    for k, out in enumerate(outs):
        cut = pl.ds(pl.multiple_of((chip ^ k) * width, width), width)
        total = mine[:, cut] + decode(got[:, cut])
        if k == 0:
            out[...] = total
        else:
            encode(total, out)


def gene_kernel(own, *refs):
    *got, out = refs
    total = own[...]
    for ref in got:
        total = total + decode(ref[...])
    out[...] = total.astype(bf16)


def cell_kernel(chips, dense, *refs):
    ours, theirs = refs[:chips], refs[chips : 2 * chips]
    outs, gene = refs[2 * chips : -1], refs[-1]
    core, chip = core_and_chip()
    half, width = ours[0].shape
    for k in range(chips):
        cut = pl.ds(pl.multiple_of((chip ^ k) * width, width), width)
        gene[pl.ds(pl.multiple_of(core * half, half), half), cut] = ours[k][...]
        gene[pl.ds(pl.multiple_of((1 - core) * half, half), half), cut] = theirs[k][...]
    me = lax.axis_index("genes")
    height = outs[0].shape[0]
    for k, out in enumerate(outs):
        left = dense[pl.ds(pl.multiple_of((me ^ k) * height, height), height), :]
        part = lax.dot_general(left, gene[...], (((1,), (1,)), ((), ())), preferred_element_type=f32)
        if k == 0:
            out[...] = part
        else:
            encode(part, out)


def last_kernel(own, *refs):
    *got, out = refs
    total = own[...]
    for ref in got:
        total = total + decode(ref[...])
    out[...] = total


def local(n_cells, n_genes, sketch, tiles, tile_rows, tile_cols, tile_counts):
    cells, rank = sketch.shape
    slots, tile, _ = tiles.shape
    genes = GENE_BLOCKS * tile
    chips = n_cells // CORES
    half = rank // CORES
    width = genes // chips
    height = cells // n_genes
    flops = 2 * cells * genes * rank
    shape = jax.ShapeDtypeStruct

    def to_core(x):
        return lax.ppermute(x, "cells", [(i, i ^ 1) for i in range(n_cells)])

    def to_chip(x, k):
        return lax.ppermute(x, "cells", [(i, i ^ (k * CORES)) for i in range(n_cells)])

    def to_gene(x, k):
        return lax.ppermute(x, "genes", [(i, i ^ k) for i in range(n_genes)])

    dense, turned, theirs = call(
        dense_kernel,
        (shape((cells, genes), bf16), shape((rank, cells), bf16), shape((half, genes), i16)),
        [SMEM, SMEM, SMEM, VMEM, ANY],
        scratch=[pltpu.SemaphoreType.DMA((slots,))],
        flops=flops // 2,
        nbytes=8 * MIB,
    )(tile_counts, tile_rows, tile_cols, sketch, tiles)
    got = to_core(theirs)
    mine = call(own_kernel, shape((half, genes), f32), [VMEM, VMEM], flops=flops // 2, nbytes=5 * MIB)(turned, dense)
    pieces = call(
        pair_kernel,
        (shape((half, width), f32),) + (shape((half, width), i16),) * (chips - 1),
        [VMEM, VMEM],
        nbytes=2 * MIB,
    )(mine, got)
    sums = [to_chip(pieces[k], k) for k in range(1, chips)]
    chunk = call(gene_kernel, shape((half, width), bf16), [VMEM] * chips, nbytes=MIB)(pieces[0], *sums)
    ours = [chunk] + [to_chip(chunk, k) for k in range(1, chips)]
    partners = [to_core(x) for x in ours]
    parts = call(
        functools.partial(cell_kernel, chips),
        (shape((height, rank), f32),) + (shape((height, rank), i16),) * (n_genes - 1),
        [VMEM] * (1 + 2 * chips),
        scratch=[pltpu.VMEM((rank, genes), bf16)],
        flops=flops,
        nbytes=6 * MIB,
    )(dense, *ours, *partners)
    rest = [to_gene(parts[k], k) for k in range(1, n_genes)]
    return call(last_kernel, shape((height, rank), f32), [VMEM] * n_genes, nbytes=MIB)(parts[0], *rest)


def solution(mesh):
    in_specs = (
        P("cells", None),
        P(("cells", "genes"), None, None),
        P(("cells", "genes")),
        P(("cells", "genes")),
        P(("cells", "genes")),
    )
    out_specs = P(("cells", "genes"), None)
    body = functools.partial(local, mesh.shape["cells"], mesh.shape["genes"])
    return jax.shard_map(body, mesh=mesh, in_specs=in_specs, out_specs=out_specs, check_vma=False)
```

```python
import functools

import jax
import jax.numpy as jnp
from jax import lax
from jax.experimental import pallas as pl
from jax.experimental.pallas import tpu as pltpu
from jax.sharding import PartitionSpec as P

GENE_BLOCKS = 16
CORES = 2
MIB = 1 << 20

VMEM = pl.BlockSpec(memory_space=pltpu.VMEM)
SMEM = pl.BlockSpec(memory_space=pltpu.SMEM)
HBM = pl.BlockSpec(memory_space=pltpu.HBM)
f32, bf16, i16, i32 = jnp.float32, jnp.bfloat16, jnp.int16, jnp.int32


def encode(x, out, at=()):
    peak = jnp.max(jnp.abs(x), axis=0, keepdims=True)
    expo = jnp.ceil(jnp.log2(jnp.maximum(peak, 2.0**-100)))
    expo = jnp.clip(expo, -100.0, 126.0)
    code = jnp.round(x * jnp.exp2(14.0 - expo)).astype(i32)
    top = code[:16]
    row = lax.broadcasted_iota(i32, top.shape, 0)
    word = jnp.broadcast_to(expo.astype(i32) + 128, top.shape)
    marked = (top & ~1) | ((word >> jnp.minimum(row, 7)) & 1)
    top = jnp.where(row < 8, marked, top)
    out[at + (pl.ds(0, 16),)] = top.astype(i16)
    out[at + (pl.ds(16, x.shape[0] - 16),)] = code[16:].astype(i16)


def decode(code):
    code = code.astype(i32)
    head = code[:8]
    row = lax.broadcasted_iota(i32, head.shape, 0)
    word = jnp.sum((head & 1) << row, axis=0, keepdims=True)
    scale = jnp.exp2((word - (128 + 14)).astype(f32))
    return code.astype(f32) * scale


def core_and_chip():
    place = lax.axis_index("cells")
    return lax.rem(place, CORES), lax.div(place, CORES)


def call(body, outs, in_specs, scratch=(), mib=32, flops=0, nbytes=0):
    return pl.pallas_call(
        body,
        out_shape=outs,
        in_specs=in_specs,
        out_specs=jax.tree.map(lambda _: VMEM, outs),
        scratch_shapes=list(scratch),
        compiler_params=pltpu.CompilerParams(vmem_limit_bytes=mib * MIB),
        cost_estimate=pl.CostEstimate(flops=flops, bytes_accessed=nbytes, transcendentals=0),
    )


def dense_kernel(count, rows, cols, sketch, tiles, dense, turned, theirs, place, sketch_here, load_sems, sems):
    tile = tiles.shape[1]
    core, _ = core_and_chip()
    rows_place, cols_place = place
    loads = [
        pltpu.make_async_copy(src, dst, load_sems.at[i])
        for i, (src, dst) in enumerate(((rows, rows_place), (cols, cols_place), (sketch, sketch_here)))
    ]
    for load in loads:
        load.start()

    def clear(i, _):
        dense[pl.ds(pl.multiple_of(i * 16, 16), 16), :] = jnp.zeros((16, dense.shape[1]), bf16)
        return 0

    lax.fori_loop(0, dense.shape[0] // 16, clear, 0)
    for load in loads[:2]:
        load.wait()

    def copy(s):
        r = pl.multiple_of(rows_place[s] * tile, tile)
        c = pl.multiple_of(cols_place[s] * tile, tile)
        return pltpu.make_async_copy(tiles.at[s], dense.at[pl.ds(r, tile), pl.ds(c, tile)], sems.at[s])

    def start(s, _):
        copy(s).start()
        return 0

    def wait(s, _):
        copy(s).wait()
        return 0

    lax.fori_loop(0, count[0], start, 0)
    loads[2].wait()
    turned[...] = sketch_here[...].T
    lax.fori_loop(0, count[0], wait, 0)
    half = theirs.shape[0]
    left = turned[pl.ds(pl.multiple_of((1 - core) * half, half), half), :]
    width = 512
    for j in range(dense.shape[1] // width):
        part = jnp.dot(left, dense[:, j * width : (j + 1) * width], preferred_element_type=f32)
        encode_columns(part, theirs, j * width)


def encode_columns(x, out, at):
    encode(x, out.at[:, pl.ds(at, x.shape[1])])


def own_kernel(turned, dense, mine):
    core, _ = core_and_chip()
    half = mine.shape[0]
    left = turned[pl.ds(pl.multiple_of(core * half, half), half), :]
    mine[...] = jnp.dot(left, dense[...], preferred_element_type=f32)


def pair_kernel(mine, got, out):
    width = out.shape[2]
    for j in range(out.shape[0]):
        cut = slice(j * width, (j + 1) * width)
        encode(mine[:, cut] + decode(got[:, cut]), out.at[j])


def gene_kernel(got, out):
    total = decode(got[0])
    for j in range(1, got.shape[0]):
        total = total + decode(got[j])
    for j in range(got.shape[0]):
        out[j] = total.astype(bf16)


def cell_kernel(dense, ours, theirs, out, gene):
    core, _ = core_and_chip()
    chips, half, width = ours.shape
    for j in range(chips):
        cut = slice(j * width, (j + 1) * width)
        gene[pl.ds(pl.multiple_of(core * half, half), half), cut] = ours[j]
        gene[pl.ds(pl.multiple_of((1 - core) * half, half), half), cut] = theirs[j]
    height = out.shape[1]
    for j in range(out.shape[0]):
        left = dense[j * height : (j + 1) * height, :]
        part = lax.dot_general(left, gene[...], (((1,), (1,)), ((), ())), preferred_element_type=f32)
        encode(part, out.at[j])


def last_kernel(got, out):
    total = decode(got[0])
    for j in range(1, got.shape[0]):
        total = total + decode(got[j])
    out[...] = total


def local(n_cells, n_genes, sketch, tiles, tile_rows, tile_cols, tile_counts):
    cells, rank = sketch.shape
    slots, tile, _ = tiles.shape
    genes = GENE_BLOCKS * tile
    chips = n_cells // CORES
    half = rank // CORES
    width = genes // chips
    height = cells // n_genes
    flops = 2 * cells * genes * rank
    shape = jax.ShapeDtypeStruct

    def to_core(x):
        return lax.ppermute(x, "cells", [(i, i ^ 1) for i in range(n_cells)])

    def over_chips(x):
        groups = [[chip * CORES + core for chip in range(chips)] for core in range(CORES)]
        return lax.all_to_all(x, "cells", 0, 0, axis_index_groups=groups, tiled=True)

    def over_genes(x):
        return lax.all_to_all(x, "genes", 0, 0, tiled=True)

    dense, turned, theirs = call(
        dense_kernel,
        (shape((cells, genes), bf16), shape((rank, cells), bf16), shape((half, genes), i16)),
        [SMEM] + [HBM] * 4,
        scratch=[
            (pltpu.SMEM((slots,), i32), pltpu.SMEM((slots,), i32)),
            pltpu.VMEM((cells, rank), bf16),
            pltpu.SemaphoreType.DMA((3,)),
            pltpu.SemaphoreType.DMA((slots,)),
        ],
        flops=flops // 2,
        nbytes=8 * MIB,
    )(tile_counts, *(pltpu.with_memory_space_constraint(x, pltpu.HBM) for x in (tile_rows, tile_cols, sketch, tiles)))
    got = to_core(theirs)
    mine = call(own_kernel, shape((half, genes), f32), [VMEM, VMEM], flops=flops // 2, nbytes=5 * MIB)(turned, dense)
    pieces = call(pair_kernel, shape((chips, half, width), i16), [VMEM, VMEM], nbytes=2 * MIB)(mine, got)
    chunks = call(gene_kernel, shape((chips, half, width), bf16), [VMEM], nbytes=MIB)(over_chips(pieces))
    ours = over_chips(chunks)
    theirs = to_core(ours)
    parts = call(
        cell_kernel,
        shape((n_genes, height, rank), i16),
        [VMEM] * 3,
        scratch=[pltpu.VMEM((rank, genes), bf16)],
        flops=flops,
        nbytes=6 * MIB,
    )(dense, ours, theirs)
    return call(last_kernel, shape((height, rank), f32), [VMEM], nbytes=MIB)(over_genes(parts))


def solution(mesh):
    in_specs = (
        P("cells", None),
        P(("cells", "genes"), None, None),
        P(("cells", "genes")),
        P(("cells", "genes")),
        P(("cells", "genes")),
    )
    out_specs = P(("cells", "genes"), None)
    body = functools.partial(local, mesh.shape["cells"], mesh.shape["genes"])
    return jax.shard_map(body, mesh=mesh, in_specs=in_specs, out_specs=out_specs, check_vma=False)
```

```python
import functools

import jax
import jax.numpy as jnp
from jax import lax
from jax.experimental import pallas as pl
from jax.experimental.pallas import tpu as pltpu
from jax.sharding import PartitionSpec as P

GENE_BLOCKS = 16
CORES = 2
STREAMS = 2
MIB = 1 << 20

VMEM = pl.BlockSpec(memory_space=pltpu.VMEM)
SMEM = pl.BlockSpec(memory_space=pltpu.SMEM)
HBM = pl.BlockSpec(memory_space=pltpu.HBM)
f32, bf16, i16, i32 = jnp.float32, jnp.bfloat16, jnp.int16, jnp.int32


def encode(x, out, at=()):
    peak = jnp.max(jnp.abs(x), axis=0, keepdims=True)
    expo = jnp.ceil(jnp.log2(jnp.maximum(peak, 2.0**-100)))
    expo = jnp.clip(expo, -100.0, 126.0)
    code = jnp.round(x * jnp.exp2(14.0 - expo)).astype(i32)
    top = code[:16]
    row = lax.broadcasted_iota(i32, top.shape, 0)
    word = jnp.broadcast_to(expo.astype(i32) + 128, top.shape)
    marked = (top & ~1) | ((word >> jnp.minimum(row, 7)) & 1)
    top = jnp.where(row < 8, marked, top)
    out[at + (pl.ds(0, 16),)] = top.astype(i16)
    out[at + (pl.ds(16, x.shape[0] - 16),)] = code[16:].astype(i16)


def decode(code):
    code = code.astype(i32)
    head = code[:8]
    row = lax.broadcasted_iota(i32, head.shape, 0)
    word = jnp.sum((head & 1) << row, axis=0, keepdims=True)
    scale = jnp.exp2((word - (128 + 14)).astype(f32))
    return code.astype(f32) * scale


def core_and_chip():
    place = lax.axis_index("cells")
    return lax.rem(place, CORES), lax.div(place, CORES)


def call(body, outs, in_specs, scratch=(), mib=32, flops=0, nbytes=0):
    return pl.pallas_call(
        body,
        out_shape=outs,
        in_specs=in_specs,
        out_specs=jax.tree.map(lambda _: VMEM, outs),
        scratch_shapes=list(scratch),
        compiler_params=pltpu.CompilerParams(vmem_limit_bytes=mib * MIB),
        cost_estimate=pl.CostEstimate(flops=flops, bytes_accessed=nbytes, transcendentals=0),
    )


def rows_of(turned, core, rows):
    span = rows * CORES
    at = [pl.multiple_of(i * span + core * rows, rows) for i in range(STREAMS)]
    return jnp.concatenate([turned[pl.ds(x, rows), :] for x in at], axis=0)


def dense_kernel(count, rows, cols, sketch, tiles, dense, turned, theirs, place, sketch_here, load_sems, sems):
    tile = tiles.shape[1]
    core, _ = core_and_chip()
    rows_place, cols_place = place
    loads = [
        pltpu.make_async_copy(src, dst, load_sems.at[i])
        for i, (src, dst) in enumerate(((rows, rows_place), (cols, cols_place), (sketch, sketch_here)))
    ]
    for load in loads:
        load.start()

    def clear(i, _):
        dense[pl.ds(pl.multiple_of(i * 16, 16), 16), :] = jnp.zeros((16, dense.shape[1]), bf16)
        return 0

    lax.fori_loop(0, dense.shape[0] // 16, clear, 0)
    for load in loads[:2]:
        load.wait()

    def copy(s):
        r = pl.multiple_of(rows_place[s] * tile, tile)
        c = pl.multiple_of(cols_place[s] * tile, tile)
        return pltpu.make_async_copy(tiles.at[s], dense.at[pl.ds(r, tile), pl.ds(c, tile)], sems.at[s])

    def start(s, _):
        copy(s).start()
        return 0

    def wait(s, _):
        copy(s).wait()
        return 0

    lax.fori_loop(0, count[0], start, 0)
    loads[2].wait()
    turned[...] = sketch_here[...].T
    lax.fori_loop(0, count[0], wait, 0)
    left = rows_of(turned, 1 - core, theirs.shape[0] // STREAMS)
    width = 512
    for j in range(dense.shape[1] // width):
        cut = pl.ds(j * width, width)
        encode(jnp.dot(left, dense[:, cut], preferred_element_type=f32), theirs.at[:, cut])


def own_kernel(turned, dense, mine):
    core, _ = core_and_chip()
    left = rows_of(turned, core, mine.shape[0] // STREAMS)
    mine[...] = jnp.dot(left, dense[...], preferred_element_type=f32)


def halve(total, bit, keep, send):
    _, chip = core_and_chip()
    width = keep.shape[1]
    ours = (chip >> bit) & 1
    low, high = total[:, :width], total[:, width:]
    keep[...] = jnp.where(ours == 0, low, high)
    encode(jnp.where(ours == 0, high, low), send)


def pair_kernel(halves, mine, got, *outs):
    total = mine[...] + decode(got[...])
    rows = total.shape[0] // STREAMS
    for i in range(STREAMS):
        part = total[i * rows : (i + 1) * rows]
        if halves:
            halve(part, 0, *outs[2 * i : 2 * i + 2])
        else:
            encode(part, outs[i])


def add_kernel(bit, keep, got, *outs):
    total = keep[...] + decode(got[...])
    if len(outs) == 2:
        halve(total, bit, *outs)
    else:
        encode(total, outs[0])


def cast_kernel(code, got, out):
    out[...] = (decode(code[...]) + decode(got[...])).astype(bf16)


def cell_kernel(masks, dense, *refs):
    ours, theirs = refs[: len(masks)], refs[len(masks) : 2 * len(masks)]
    outs, gene = refs[2 * len(masks) : -1], refs[-1]
    core, chip = core_and_chip()
    rows, width = ours[0].shape
    for k, mask in enumerate(masks):
        at, size = 0, gene.shape[1]
        for bit in range(len(masks).bit_length() - 1):
            size //= 2
            at = at + (((chip ^ mask) >> bit) & 1) * size
        cut = pl.ds(pl.multiple_of(at, width), width)
        gene[pl.ds(pl.multiple_of(core * rows, rows), rows), cut] = ours[k][...]
        gene[pl.ds(pl.multiple_of((1 - core) * rows, rows), rows), cut] = theirs[k][...]
    me = lax.axis_index("genes")
    height = outs[0].shape[0]
    for k, out in enumerate(outs):
        left = dense[pl.ds(pl.multiple_of((me ^ k) * height, height), height), :]
        part = lax.dot_general(left, gene[...], (((1,), (1,)), ((), ())), preferred_element_type=f32)
        if k == 0:
            out[...] = part
        else:
            encode(part, out)


def last_kernel(count, *refs):
    out = refs[-1]
    for i in range(STREAMS):
        own, *got = refs[i * count : (i + 1) * count]
        total = own[...]
        for ref in got:
            total = total + decode(ref[...])
        out[:, i * own.shape[1] : (i + 1) * own.shape[1]] = total


def local(n_cells, n_genes, sketch, tiles, tile_rows, tile_cols, tile_counts):
    cells, rank = sketch.shape
    slots, tile, _ = tiles.shape
    genes = GENE_BLOCKS * tile
    bits = (n_cells // CORES).bit_length() - 1
    span = rank // STREAMS
    rows = span // CORES
    share = rows * STREAMS
    height = cells // n_genes
    flops = 2 * cells * genes * rank
    shape = jax.ShapeDtypeStruct

    def to_core(x):
        return lax.ppermute(x, "cells", [(i, i ^ 1) for i in range(n_cells)])

    def to_chip(x, bit):
        return lax.ppermute(x, "cells", [(i, i ^ (CORES << bit)) for i in range(n_cells)])

    def to_gene(x, k):
        return lax.ppermute(x, "genes", [(i, i ^ k) for i in range(n_genes)])

    def halves(width):
        return shape((rows, width // 2), f32), shape((rows, width // 2), i16)

    dense, turned, theirs = call(
        dense_kernel,
        (shape((cells, genes), bf16), shape((rank, cells), bf16), shape((share, genes), i16)),
        [SMEM] + [HBM] * 4,
        scratch=[
            (pltpu.SMEM((slots,), i32), pltpu.SMEM((slots,), i32)),
            pltpu.VMEM((cells, rank), bf16),
            pltpu.SemaphoreType.DMA((3,)),
            pltpu.SemaphoreType.DMA((slots,)),
        ],
        flops=flops // 2,
        nbytes=8 * MIB,
    )(tile_counts, *(pltpu.with_memory_space_constraint(x, pltpu.HBM) for x in (tile_rows, tile_cols, sketch, tiles)))
    got = to_core(theirs)
    mine = call(own_kernel, shape((share, genes), f32), [VMEM, VMEM], flops=flops // 2, nbytes=5 * MIB)(turned, dense)
    cut = bits > 1
    one = halves(genes) if cut else (shape((rows, genes), i16),)
    pieces = call(functools.partial(pair_kernel, cut), one * STREAMS, [VMEM, VMEM], nbytes=2 * MIB)(mine, got)

    def gene_side(i):
        width = genes
        if cut:
            keep, send = pieces[2 * i : 2 * i + 2]
            for bit in range(bits - 1):
                width //= 2
                got = to_chip(send, bit)
                outs = halves(width) if bit < bits - 2 else (shape((rows, width), i16),)
                done = call(functools.partial(add_kernel, bit + 1), outs, [VMEM, VMEM], nbytes=MIB)(keep, got)
                keep, send = done[0], done[-1]
            code = send
        else:
            code = pieces[i]
        got = to_chip(code, bits - 1)
        held = [call(cast_kernel, shape((rows, width), bf16), [VMEM, VMEM], nbytes=MIB)(code, got)]
        masks = [0]
        for bit in reversed(range(bits - 1)):
            held += [to_chip(x, bit) for x in held]
            masks += [mask ^ (1 << bit) for mask in masks]
        return held, masks

    parts = []
    for i in range(STREAMS):
        held, masks = gene_side(i)
        partner = [to_core(x) for x in held]
        outs = call(
            functools.partial(cell_kernel, masks),
            (shape((height, span), f32),) + (shape((height, span), i16),) * (n_genes - 1),
            [VMEM] * (1 + 2 * len(held)),
            scratch=[pltpu.VMEM((span, genes), bf16)],
            flops=flops // STREAMS,
            nbytes=5 * MIB,
        )(dense, *held, *partner)
        parts += [outs[0]] + [to_gene(outs[k], k) for k in range(1, n_genes)]
    last = functools.partial(last_kernel, n_genes)
    return call(last, shape((height, rank), f32), [VMEM] * len(parts), nbytes=MIB)(*parts)


def solution(mesh):
    in_specs = (
        P("cells", None),
        P(("cells", "genes"), None, None),
        P(("cells", "genes")),
        P(("cells", "genes")),
        P(("cells", "genes")),
    )
    out_specs = P(("cells", "genes"), None)
    body = functools.partial(local, mesh.shape["cells"], mesh.shape["genes"])
    return jax.shard_map(body, mesh=mesh, in_specs=in_specs, out_specs=out_specs, check_vma=False)
```

```python
import functools

import jax
import jax.numpy as jnp
from jax import lax
from jax.experimental import pallas as pl
from jax.experimental.pallas import tpu as pltpu
from jax.sharding import PartitionSpec as P

GENE_BLOCKS = 16
CORES = 2
STREAMS = 2
MIB = 1 << 20

VMEM = pl.BlockSpec(memory_space=pltpu.VMEM)
SMEM = pl.BlockSpec(memory_space=pltpu.SMEM)
HBM = pl.BlockSpec(memory_space=pltpu.HBM)
f32, bf16, i16, i32 = jnp.float32, jnp.bfloat16, jnp.int16, jnp.int32


def encode(x, out, at=()):
    peak = jnp.max(jnp.abs(x), axis=0, keepdims=True)
    expo = jnp.ceil(jnp.log2(jnp.maximum(peak, 2.0**-100)))
    expo = jnp.clip(expo, -100.0, 126.0)
    code = jnp.round(x * jnp.exp2(14.0 - expo)).astype(i32)
    top = code[:16]
    row = lax.broadcasted_iota(i32, top.shape, 0)
    word = jnp.broadcast_to(expo.astype(i32) + 128, top.shape)
    marked = (top & ~1) | ((word >> jnp.minimum(row, 7)) & 1)
    top = jnp.where(row < 8, marked, top)
    out[at + (pl.ds(0, 16),)] = top.astype(i16)
    out[at + (pl.ds(16, x.shape[0] - 16),)] = code[16:].astype(i16)


def decode(code):
    code = code.astype(i32)
    head = code[:8]
    row = lax.broadcasted_iota(i32, head.shape, 0)
    word = jnp.sum((head & 1) << row, axis=0, keepdims=True)
    scale = jnp.exp2((word - (128 + 14)).astype(f32))
    return code.astype(f32) * scale


def core_and_chip():
    place = lax.axis_index("cells")
    return lax.rem(place, CORES), lax.div(place, CORES)


def call(body, outs, in_specs, scratch=(), mib=32, flops=0, nbytes=0):
    return pl.pallas_call(
        body,
        out_shape=outs,
        in_specs=in_specs,
        out_specs=jax.tree.map(lambda _: VMEM, outs),
        scratch_shapes=list(scratch),
        compiler_params=pltpu.CompilerParams(vmem_limit_bytes=mib * MIB),
        cost_estimate=pl.CostEstimate(flops=flops, bytes_accessed=nbytes, transcendentals=0),
    )


def rows_of(turned, core, rows):
    span = rows * CORES
    at = [pl.multiple_of(i * span + core * rows, rows) for i in range(STREAMS)]
    return jnp.concatenate([turned[pl.ds(x, rows), :] for x in at], axis=0)


def dense_kernel(count, rows, cols, sketch, tiles, dense, turned, theirs, place, sketch_here, load_sems, sems):
    tile = tiles.shape[1]
    core, _ = core_and_chip()
    rows_place, cols_place = place
    loads = [
        pltpu.make_async_copy(src, dst, load_sems.at[i])
        for i, (src, dst) in enumerate(((rows, rows_place), (cols, cols_place), (sketch, sketch_here)))
    ]
    for load in loads:
        load.start()

    def clear(i, _):
        dense[pl.ds(pl.multiple_of(i * 16, 16), 16), :] = jnp.zeros((16, dense.shape[1]), bf16)
        return 0

    lax.fori_loop(0, dense.shape[0] // 16, clear, 0)
    for load in loads[:2]:
        load.wait()

    def copy(s):
        r = pl.multiple_of(rows_place[s] * tile, tile)
        c = pl.multiple_of(cols_place[s] * tile, tile)
        return pltpu.make_async_copy(tiles.at[s], dense.at[pl.ds(r, tile), pl.ds(c, tile)], sems.at[s])

    def start(s, _):
        copy(s).start()
        return 0

    def wait(s, _):
        copy(s).wait()
        return 0

    lax.fori_loop(0, count[0], start, 0)
    loads[2].wait()
    turned[...] = sketch_here[...].T
    lax.fori_loop(0, count[0], wait, 0)
    left = rows_of(turned, 1 - core, theirs.shape[0] // STREAMS)
    width = 512
    for j in range(dense.shape[1] // width):
        cut = pl.ds(j * width, width)
        encode(jnp.dot(left, dense[:, cut], preferred_element_type=f32), theirs.at[:, cut])


def own_kernel(turned, dense, mine):
    core, _ = core_and_chip()
    left = rows_of(turned, core, mine.shape[0] // STREAMS)
    mine[...] = jnp.dot(left, dense[...], preferred_element_type=f32)


def halve(total, bit, keep, send):
    _, chip = core_and_chip()
    width = keep.shape[1]
    ours = (chip >> bit) & 1
    low, high = total[:, :width], total[:, width:]
    keep[...] = jnp.where(ours == 0, low, high)
    encode(jnp.where(ours == 0, high, low), send)


def pair_kernel(halves, mine, got, *outs):
    total = mine[...] + decode(got[...])
    rows = total.shape[0] // STREAMS
    for i in range(STREAMS):
        part = total[i * rows : (i + 1) * rows]
        if halves:
            halve(part, 0, *outs[2 * i : 2 * i + 2])
        else:
            encode(part, outs[i])


def add_kernel(bit, keep, got, *outs):
    total = keep[...] + decode(got[...])
    if len(outs) == 2:
        halve(total, bit, *outs)
    else:
        encode(total, outs[0])


def cast_kernel(code, got, out):
    out[...] = (decode(code[...]) + decode(got[...])).astype(bf16)


def cell_kernel(masks, dense, *refs):
    *pieces, gene = refs
    count = len(masks) * CORES * STREAMS
    pieces, outs = pieces[:count], pieces[count:]
    core, chip = core_and_chip()
    rows, width = pieces[0].shape
    for k, mask in enumerate(masks):
        at, size = 0, gene.shape[1]
        for bit in range(len(masks).bit_length() - 1):
            size //= 2
            at = at + (((chip ^ mask) >> bit) & 1) * size
        cut = pl.ds(pl.multiple_of(at, width), width)
        for i in range(STREAMS):
            for j, owner in enumerate((core, 1 - core)):
                row = pl.multiple_of((i * CORES + owner) * rows, rows)
                gene[pl.ds(row, rows), cut] = pieces[(i * CORES + j) * len(masks) + k][...]
    me = lax.axis_index("genes")
    height = outs[0].shape[0]
    for k, out in enumerate(outs):
        left = dense[pl.ds(pl.multiple_of((me ^ k) * height, height), height), :]
        part = lax.dot_general(left, gene[...], (((1,), (1,)), ((), ())), preferred_element_type=f32)
        if k == 0:
            out[...] = part
        else:
            encode(part, out)


def last_kernel(own, *refs):
    *got, out = refs
    total = own[...]
    for ref in got:
        total = total + decode(ref[...])
    out[...] = total


def local(n_cells, n_genes, sketch, tiles, tile_rows, tile_cols, tile_counts):
    cells, rank = sketch.shape
    slots, tile, _ = tiles.shape
    genes = GENE_BLOCKS * tile
    bits = (n_cells // CORES).bit_length() - 1
    span = rank // STREAMS
    rows = span // CORES
    share = rows * STREAMS
    height = cells // n_genes
    flops = 2 * cells * genes * rank
    shape = jax.ShapeDtypeStruct

    def to_core(x):
        return lax.ppermute(x, "cells", [(i, i ^ 1) for i in range(n_cells)])

    def to_chip(x, bit):
        return lax.ppermute(x, "cells", [(i, i ^ (CORES << bit)) for i in range(n_cells)])

    def to_gene(x, k):
        return lax.ppermute(x, "genes", [(i, i ^ k) for i in range(n_genes)])

    def halves(width):
        return shape((rows, width // 2), f32), shape((rows, width // 2), i16)

    dense, turned, theirs = call(
        dense_kernel,
        (shape((cells, genes), bf16), shape((rank, cells), bf16), shape((share, genes), i16)),
        [SMEM] + [HBM] * 4,
        scratch=[
            (pltpu.SMEM((slots,), i32), pltpu.SMEM((slots,), i32)),
            pltpu.VMEM((cells, rank), bf16),
            pltpu.SemaphoreType.DMA((3,)),
            pltpu.SemaphoreType.DMA((slots,)),
        ],
        flops=flops // 2,
        nbytes=8 * MIB,
    )(tile_counts, *(pltpu.with_memory_space_constraint(x, pltpu.HBM) for x in (tile_rows, tile_cols, sketch, tiles)))
    got = to_core(theirs)
    mine = call(own_kernel, shape((share, genes), f32), [VMEM, VMEM], flops=flops // 2, nbytes=5 * MIB)(turned, dense)
    cut = bits > 1
    one = halves(genes) if cut else (shape((rows, genes), i16),)
    pieces = call(functools.partial(pair_kernel, cut), one * STREAMS, [VMEM, VMEM], nbytes=2 * MIB)(mine, got)

    def add_step(bit, keep, got, width):
        outs = halves(width) if bit < bits - 2 else (shape((rows, width), i16),)
        return call(functools.partial(add_kernel, bit + 1), outs, [VMEM, VMEM], nbytes=MIB)(keep, got)

    streams = [pieces[i * len(one) : (i + 1) * len(one)] for i in range(STREAMS)]
    width = genes
    for bit in range(bits - 1):
        width //= 2
        before = None
        for i in range(STREAMS):
            keep, send = streams[i]
            if before is not None:
                send, before = lax.optimization_barrier((send, before))
            before = to_chip(send, bit)
            streams[i] = add_step(bit, keep, before, width)
    held = []
    for code in [x[-1] for x in streams]:
        got = to_chip(code, bits - 1)
        held.append([call(cast_kernel, shape((rows, width), bf16), [VMEM, VMEM], nbytes=MIB)(code, got)])
    masks = [0]
    for bit in reversed(range(bits - 1)):
        held = [pieces + [to_chip(x, bit) for x in pieces] for pieces in held]
        masks += [mask ^ (1 << bit) for mask in masks]
    whole = []
    for pieces in held:
        whole += pieces + [to_core(x) for x in pieces]
    parts = call(
        functools.partial(cell_kernel, masks),
        (shape((height, rank), f32),) + (shape((height, rank), i16),) * (n_genes - 1),
        [VMEM] * (1 + len(whole)),
        scratch=[pltpu.VMEM((rank, genes), bf16)],
        flops=flops,
        nbytes=6 * MIB,
    )(dense, *whole)
    got = [to_gene(parts[k], k) for k in reversed(range(1, n_genes))]
    return call(last_kernel, shape((height, rank), f32), [VMEM] * n_genes, nbytes=MIB)(parts[0], *got)


def solution(mesh):
    in_specs = (
        P("cells", None),
        P(("cells", "genes"), None, None),
        P(("cells", "genes")),
        P(("cells", "genes")),
        P(("cells", "genes")),
    )
    out_specs = P(("cells", "genes"), None)
    body = functools.partial(local, mesh.shape["cells"], mesh.shape["genes"])
    return jax.shard_map(body, mesh=mesh, in_specs=in_specs, out_specs=out_specs, check_vma=False)
```

```python
import functools

import jax
import jax.numpy as jnp
from jax import lax
from jax.experimental import pallas as pl
from jax.experimental.pallas import tpu as pltpu
from jax.sharding import PartitionSpec as P

GENE_BLOCKS = 16
CORES = 2
STREAMS = 2
MIB = 1 << 20

VMEM = pl.BlockSpec(memory_space=pltpu.VMEM)
SMEM = pl.BlockSpec(memory_space=pltpu.SMEM)
HBM = pl.BlockSpec(memory_space=pltpu.HBM)
f32, bf16, i16, i32 = jnp.float32, jnp.bfloat16, jnp.int16, jnp.int32


def encode(x, out, at=()):
    peak = jnp.max(jnp.abs(x), axis=0, keepdims=True)
    expo = jnp.ceil(jnp.log2(jnp.maximum(peak, 2.0**-100)))
    expo = jnp.clip(expo, -100.0, 126.0)
    code = jnp.round(x * jnp.exp2(14.0 - expo)).astype(i32)
    top = code[:16]
    row = lax.broadcasted_iota(i32, top.shape, 0)
    word = jnp.broadcast_to(expo.astype(i32) + 128, top.shape)
    marked = (top & ~1) | ((word >> jnp.minimum(row, 7)) & 1)
    top = jnp.where(row < 8, marked, top)
    out[at + (pl.ds(0, 16),)] = top.astype(i16)
    out[at + (pl.ds(16, x.shape[0] - 16),)] = code[16:].astype(i16)


def decode(code):
    code = code.astype(i32)
    head = code[:8]
    row = lax.broadcasted_iota(i32, head.shape, 0)
    word = jnp.sum((head & 1) << row, axis=0, keepdims=True)
    scale = jnp.exp2((word - (128 + 14)).astype(f32))
    return code.astype(f32) * scale


def core_and_chip():
    place = lax.axis_index("cells")
    return lax.rem(place, CORES), lax.div(place, CORES)


def call(body, outs, in_specs, scratch=(), mib=32, flops=0, nbytes=0):
    return pl.pallas_call(
        body,
        out_shape=outs,
        in_specs=in_specs,
        out_specs=jax.tree.map(lambda _: VMEM, outs),
        scratch_shapes=list(scratch),
        compiler_params=pltpu.CompilerParams(vmem_limit_bytes=mib * MIB),
        cost_estimate=pl.CostEstimate(flops=flops, bytes_accessed=nbytes, transcendentals=0),
    )


def rows_of(turned, core, rows):
    span = rows * CORES
    at = [pl.multiple_of(i * span + core * rows, rows) for i in range(STREAMS)]
    return jnp.concatenate([turned[pl.ds(x, rows), :] for x in at], axis=0)


def dense_kernel(count, rows, cols, sketch, tiles, dense, turned, theirs, place, sketch_here, load_sems, sems):
    tile = tiles.shape[1]
    core, _ = core_and_chip()
    rows_place, cols_place = place
    loads = [
        pltpu.make_async_copy(src, dst, load_sems.at[i])
        for i, (src, dst) in enumerate(((rows, rows_place), (cols, cols_place), (sketch, sketch_here)))
    ]
    for load in loads:
        load.start()

    def clear(i, _):
        dense[pl.ds(pl.multiple_of(i * 16, 16), 16), :] = jnp.zeros((16, dense.shape[1]), bf16)
        return 0

    lax.fori_loop(0, dense.shape[0] // 16, clear, 0)
    for load in loads[:2]:
        load.wait()

    def copy(s):
        r = pl.multiple_of(rows_place[s] * tile, tile)
        c = pl.multiple_of(cols_place[s] * tile, tile)
        return pltpu.make_async_copy(tiles.at[s], dense.at[pl.ds(r, tile), pl.ds(c, tile)], sems.at[s])

    def start(s, _):
        copy(s).start()
        return 0

    def wait(s, _):
        copy(s).wait()
        return 0

    lax.fori_loop(0, count[0], start, 0)
    loads[2].wait()
    turned[...] = sketch_here[...].T
    lax.fori_loop(0, count[0], wait, 0)
    left = rows_of(turned, 1 - core, theirs.shape[0] // STREAMS)
    width = 512
    for j in range(dense.shape[1] // width):
        cut = pl.ds(j * width, width)
        encode(jnp.dot(left, dense[:, cut], preferred_element_type=f32), theirs.at[:, cut])


def own_kernel(turned, dense, mine):
    core, _ = core_and_chip()
    left = rows_of(turned, core, mine.shape[0] // STREAMS)
    mine[...] = jnp.dot(left, dense[...], preferred_element_type=f32)


def halve(total, bit, keep, send):
    _, chip = core_and_chip()
    width = keep.shape[1]
    ours = (chip >> bit) & 1
    low, high = total[:, :width], total[:, width:]
    keep[...] = jnp.where(ours == 0, low, high)
    encode(jnp.where(ours == 0, high, low), send)


def pair_kernel(chips, mine, got, *refs):
    *outs, total = refs
    direct, rest = outs[:chips], outs[chips:]
    _, chip = core_and_chip()
    total[...] = mine[...] + decode(got[...])
    rows, width = direct[0].shape
    if len(rest) == 2:
        halve(total[rows:, :], 0, *rest)
    else:
        encode(total[rows:, :], rest[0])
    for k, out in enumerate(direct):
        part = total[:rows, pl.ds(pl.multiple_of((chip ^ k) * width, width), width)]
        if k == 0:
            out[...] = part
        else:
            encode(part, out)


def add_kernel(bit, keep, got, *outs):
    total = keep[...] + decode(got[...])
    if len(outs) == 2:
        halve(total, bit, *outs)
    else:
        encode(total, outs[0])


def cast_kernel(code, got, out):
    out[...] = (decode(code[...]) + decode(got[...])).astype(bf16)


def direct_cast_kernel(own, *refs):
    *got, out = refs
    total = own[...]
    for ref in got:
        total = total + decode(ref[...])
    out[...] = total.astype(bf16)


def join_kernel(*refs):
    *pieces, out = refs
    _, chip = core_and_chip()
    width = pieces[0].shape[1]
    for k, piece in enumerate(pieces):
        out[:, pl.ds(pl.multiple_of((chip ^ k) * width, width), width)] = piece[...]


def gene_kernel(masks, first, first_theirs, *refs):
    *pieces, gene = refs
    core, chip = core_and_chip()
    rows, width = pieces[0].shape

    def at(stream, owner):
        return pl.ds(pl.multiple_of((stream * CORES + owner) * rows, rows), rows)

    gene[at(0, core), :] = first[...]
    gene[at(0, 1 - core), :] = first_theirs[...]
    for k, mask in enumerate(masks):
        place, size = 0, gene.shape[1]
        for bit in range(len(masks).bit_length() - 1):
            size //= 2
            place = place + (((chip ^ mask) >> bit) & 1) * size
        cut = pl.ds(pl.multiple_of(place, width), width)
        gene[at(1, core), cut] = pieces[k][...]
        gene[at(1, 1 - core), cut] = pieces[len(masks) + k][...]


def cell_kernel(k, dense, gene, out):
    height = out.shape[0]
    me = lax.axis_index("genes")
    left = dense[pl.ds(pl.multiple_of((me ^ k) * height, height), height), :]
    part = lax.dot_general(left, gene[...], (((1,), (1,)), ((), ())), preferred_element_type=f32)
    if k == 0:
        out[...] = part
    else:
        encode(part, out)


def more_kernel(total, got, out):
    out[...] = total[...] + decode(got[...])


def local(n_cells, n_genes, sketch, tiles, tile_rows, tile_cols, tile_counts):
    cells, rank = sketch.shape
    slots, tile, _ = tiles.shape
    genes = GENE_BLOCKS * tile
    bits = (n_cells // CORES).bit_length() - 1
    span = rank // STREAMS
    rows = span // CORES
    share = rows * STREAMS
    height = cells // n_genes
    flops = 2 * cells * genes * rank
    shape = jax.ShapeDtypeStruct

    def to_core(x):
        return lax.ppermute(x, "cells", [(i, i ^ 1) for i in range(n_cells)])

    def to_chip(x, k):
        return lax.ppermute(x, "cells", [(i, i ^ (CORES * k)) for i in range(n_cells)])

    def to_gene(x, k):
        return lax.ppermute(x, "genes", [(i, i ^ k) for i in range(n_genes)])

    def halves(width):
        return shape((rows, width // 2), f32), shape((rows, width // 2), i16)

    dense, turned, theirs = call(
        dense_kernel,
        (shape((cells, genes), bf16), shape((rank, cells), bf16), shape((share, genes), i16)),
        [SMEM] + [HBM] * 4,
        scratch=[
            (pltpu.SMEM((slots,), i32), pltpu.SMEM((slots,), i32)),
            pltpu.VMEM((cells, rank), bf16),
            pltpu.SemaphoreType.DMA((3,)),
            pltpu.SemaphoreType.DMA((slots,)),
        ],
        flops=flops // 2,
        nbytes=8 * MIB,
    )(tile_counts, *(pltpu.with_memory_space_constraint(x, pltpu.HBM) for x in (tile_rows, tile_cols, sketch, tiles)))
    got = to_core(theirs)
    mine = call(own_kernel, shape((share, genes), f32), [VMEM, VMEM], flops=flops // 2, nbytes=5 * MIB)(turned, dense)
    chips = n_cells // CORES
    chunk = genes // chips
    one = halves(genes) if bits > 1 else (shape((rows, genes), i16),)
    pieces = call(
        functools.partial(pair_kernel, chips),
        (shape((rows, chunk), f32),) + (shape((rows, chunk), i16),) * (chips - 1) + one,
        [VMEM, VMEM],
        scratch=[pltpu.VMEM((share, genes), f32)],
        nbytes=3 * MIB,
    )(mine, got)
    direct, half = pieces[:chips], pieces[chips:]

    width = genes
    for bit in range(bits - 1):
        width //= 2
        outs = halves(width) if bit < bits - 2 else (shape((rows, width), i16),)
        half = call(functools.partial(add_kernel, bit + 1), outs, [VMEM, VMEM], nbytes=MIB)(
            half[0], to_chip(half[1], 1 << bit)
        )
    came = [to_chip(direct[k], k) for k in reversed(range(1, chips))]
    summed = call(direct_cast_kernel, shape((rows, chunk), bf16), [VMEM] * chips, nbytes=MIB)(direct[0], *came)
    crossed = to_chip(half[-1], chips // 2)
    spread = [to_chip(summed, k) for k in reversed(range(1, chips))][::-1]
    held = [call(cast_kernel, shape((rows, width), bf16), [VMEM, VMEM], nbytes=MIB)(half[-1], crossed)]
    *spread, _ = lax.optimization_barrier((*spread, held[0]))
    first = call(join_kernel, shape((rows, genes), bf16), [VMEM] * chips, nbytes=MIB)(summed, *spread)
    masks = [0]
    for bit in reversed(range(bits - 1)):
        held = held + [to_chip(x, 1 << bit) for x in held]
        masks += [mask ^ (1 << bit) for mask in masks]
    theirs = [to_core(x) for x in held]
    gene = call(
        functools.partial(gene_kernel, masks), shape((rank, genes), bf16), [VMEM] * (2 + 2 * len(held)), nbytes=2 * MIB
    )(first, to_core(first), *held, *theirs)

    def cell(k, gene):
        kind = f32 if k == 0 else i16
        return call(
            functools.partial(cell_kernel, k),
            shape((height, rank), kind),
            [VMEM, VMEM],
            flops=flops // n_genes,
            nbytes=3 * MIB,
        )(dense, gene)

    got = []
    for k in reversed(range(1, n_genes)):
        got.append(to_gene(cell(k, gene), k))
    total = cell(0, gene)
    for x in got:
        total = call(more_kernel, shape((height, rank), f32), [VMEM, VMEM], nbytes=16 * MIB)(total, x)
    return total


def solution(mesh):
    in_specs = (
        P("cells", None),
        P(("cells", "genes"), None, None),
        P(("cells", "genes")),
        P(("cells", "genes")),
        P(("cells", "genes")),
    )
    out_specs = P(("cells", "genes"), None)
    body = functools.partial(local, mesh.shape["cells"], mesh.shape["genes"])
    return jax.shard_map(body, mesh=mesh, in_specs=in_specs, out_specs=out_specs, check_vma=False)
```

```python
import functools

import jax
import jax.numpy as jnp
from jax import lax
from jax.experimental import pallas as pl
from jax.experimental.pallas import tpu as pltpu
from jax.sharding import PartitionSpec as P

GENE_BLOCKS = 16
CORES = 2
LANES = 128
PARTS = (1, 1, 1, 1)
MIB = 1 << 20

VMEM = pl.BlockSpec(memory_space=pltpu.VMEM)
SMEM = pl.BlockSpec(memory_space=pltpu.SMEM)
HBM = pl.BlockSpec(memory_space=pltpu.HBM)
f32, bf16, i16, i32 = jnp.float32, jnp.bfloat16, jnp.int16, jnp.int32


def encode(x, out, at=()):
    peak = jnp.max(jnp.abs(x), axis=0, keepdims=True)
    expo = jnp.ceil(jnp.log2(jnp.maximum(peak, 2.0**-100)))
    expo = jnp.clip(expo, -100.0, 126.0)
    code = jnp.round(x * jnp.exp2(14.0 - expo)).astype(i32)
    top = code[:16]
    row = lax.broadcasted_iota(i32, top.shape, 0)
    word = jnp.broadcast_to(expo.astype(i32) + 128, top.shape)
    marked = (top & ~1) | ((word >> jnp.minimum(row, 7)) & 1)
    top = jnp.where(row < 8, marked, top)
    out[at + (pl.ds(0, 16),)] = top.astype(i16)
    out[at + (pl.ds(16, x.shape[0] - 16),)] = code[16:].astype(i16)


def decode(code):
    code = code.astype(i32)
    head = code[:8]
    row = lax.broadcasted_iota(i32, head.shape, 0)
    word = jnp.sum((head & 1) << row, axis=0, keepdims=True)
    scale = jnp.exp2((word - (128 + 14)).astype(f32))
    return code.astype(f32) * scale


def core_and_chip():
    place = lax.axis_index("cells")
    return lax.rem(place, CORES), lax.div(place, CORES)


def call(body, outs, in_specs, scratch=(), mib=32, nbytes=0):
    return pl.pallas_call(
        body,
        out_shape=outs,
        in_specs=in_specs,
        out_specs=jax.tree.map(lambda _: VMEM, outs),
        scratch_shapes=list(scratch),
        compiler_params=pltpu.CompilerParams(vmem_limit_bytes=mib * MIB),
        cost_estimate=pl.CostEstimate(flops=0, bytes_accessed=nbytes, transcendentals=0),
    )


def block(index, size):
    return pl.ds(pl.multiple_of(index * size, size), size)


def dense_kernel(count, rows, cols, sketch, tiles, dense, turned, theirs, place, sketch_here, load_sems, sems):
    tile = tiles.shape[1]
    core, _ = core_and_chip()
    rows_place, cols_place = place
    loads = [
        pltpu.make_async_copy(src, dst, load_sems.at[i])
        for i, (src, dst) in enumerate(((rows, rows_place), (cols, cols_place), (sketch, sketch_here)))
    ]
    for load in loads:
        load.start()

    def clear(i, _):
        dense[block(i, 16), :] = jnp.zeros((16, dense.shape[1]), bf16)
        return 0

    lax.fori_loop(0, dense.shape[0] // 16, clear, 0)
    for load in loads[:2]:
        load.wait()

    def copy(s):
        to = dense.at[block(rows_place[s], tile), block(cols_place[s], tile)]
        return pltpu.make_async_copy(tiles.at[s], to, sems.at[s])

    def start(s, _):
        copy(s).start()
        return 0

    def wait(s, _):
        copy(s).wait()
        return 0

    lax.fori_loop(0, count[0], start, 0)
    loads[2].wait()
    turned[...] = sketch_here[...].T
    lax.fori_loop(0, count[0], wait, 0)
    half_kernel(1, 0, turned, dense, theirs)


def half_kernel(other, start, turned, dense, out):
    core, _ = core_and_chip()
    rows, width = out.shape
    left = turned[block(core ^ other, rows), :]
    step = min(width, 512)
    for j in range(0, width, step):
        part = jnp.dot(left, dense[:, start + j : start + j + step], preferred_element_type=f32)
        if other:
            encode(part, out.at[:, j : j + step])
        else:
            out[:, j : j + step] = part


def add_kernel(bit, mine, got, *outs):
    _, chip = core_and_chip()
    start = 0
    for keep, send in zip(outs[::2], outs[1::2]):
        width = keep.shape[1]
        ours = (chip >> bit) & 1
        cut = pl.ds(pl.multiple_of(start + (1 - ours) * width, width), width)
        encode(mine[:, cut] + decode(got[:, cut]), send)
        cut = pl.ds(pl.multiple_of(start + ours * width, width), width)
        keep[...] = mine[:, cut] + decode(got[:, cut])
        start += 2 * width


def code_kernel(mine, got, *outs):
    start = 0
    for out in outs:
        cut = slice(start, start + out.shape[1])
        encode(mine[:, cut] + decode(got[:, cut]), out)
        start += out.shape[1]


def cast_kernel(code, got, out):
    out[...] = (decode(code[...]) + decode(got[...])).astype(bf16)


def join(masks, pieces, gene):
    core, chip = core_and_chip()
    rows, width = pieces[0].shape
    for k, mask in enumerate(masks):
        place, size = 0, gene.shape[1]
        for bit in range(len(masks).bit_length() - 1):
            size //= 2
            place = place + (((chip ^ mask) >> bit) & 1) * size
        cut = pl.ds(pl.multiple_of(place, width), width)
        gene[block(core, rows), cut] = pieces[k][...]
        gene[block(1 - core, rows), cut] = pieces[len(masks) + k][...]


def gene_kernel(masks, *refs):
    join(masks, refs[:-1], refs[-1])


def product(left, gene):
    return lax.dot_general(left, gene, (((1,), (1,)), ((), ())), preferred_element_type=f32)


def part_kernel(masks, start, fresh, dense, *refs):
    *pieces, out, gene = refs
    if not fresh:
        before, *pieces = pieces
    join(masks, pieces, gene)
    step = 256
    for i in range(0, out.shape[0], step):
        part = product(dense[i : i + step, start : start + gene.shape[1]], gene[...])
        out[i : i + step, :] = part if fresh else before[i : i + step, :] + part


def cell_kernel(k, start, dense, gene, *refs):
    *before, out = refs
    cut = block(lax.axis_index("genes") ^ k, out.shape[0])
    part = product(dense[cut, start : start + gene.shape[1]], gene[...])
    if before:
        part = part + before[0][cut, :]
    if k == 0:
        out[...] = part
    else:
        encode(part, out)


def more_kernel(total, got, out):
    out[...] = total[...] + decode(got[...])


def cuts_of(genes, bits):
    for parts in (PARTS, (1, 1)):
        unit = genes // sum(parts)
        if unit >> max(bits - 1, 0) >= LANES:
            ends = [sum(parts[:i]) * unit for i in range(len(parts))]
            return tuple((at, p * unit) for at, p in zip(ends, parts))
    return ((0, genes),)


def local(n_cells, n_genes, sketch, tiles, tile_rows, tile_cols, tile_counts):
    cells, rank = sketch.shape
    slots, tile, _ = tiles.shape
    genes = GENE_BLOCKS * tile
    bits = (n_cells // CORES).bit_length() - 1
    rows = rank // CORES
    height = cells // n_genes
    shape = jax.ShapeDtypeStruct
    cuts = cuts_of(genes, bits)

    def to_core(x):
        return lax.ppermute(x, "cells", [(i, i ^ 1) for i in range(n_cells)])

    def to_chip(x, bit):
        return lax.ppermute(x, "cells", [(i, i ^ (CORES << bit)) for i in range(n_cells)])

    def to_gene(x, k):
        return lax.ppermute(x, "genes", [(i, i ^ k) for i in range(n_genes)])

    dense, turned, theirs = call(
        dense_kernel,
        (shape((cells, genes), bf16), shape((rank, cells), bf16), shape((rows, cuts[0][1]), i16)),
        [SMEM] + [HBM] * 4,
        scratch=[
            (pltpu.SMEM((slots,), i32), pltpu.SMEM((slots,), i32)),
            pltpu.VMEM((cells, rank), bf16),
            pltpu.SemaphoreType.DMA((3,)),
            pltpu.SemaphoreType.DMA((slots,)),
        ],

    )(tile_counts, *(pltpu.with_memory_space_constraint(x, pltpu.HBM) for x in (tile_rows, tile_cols, sketch, tiles)))

    def half_of(other, start, turned, width):
        body = functools.partial(half_kernel, other, start)
        return call(body, shape((rows, width), i16 if other else f32), [VMEM, VMEM])(turned, dense)

    def after(x, *others):
        return lax.optimization_barrier((x, *others))[0]

    def add_step(bit, kept, came, widths):
        if bit < bits - 1:
            outs = [shape((rows, width // 2), kind) for width in widths for kind in (f32, i16)]
            done = call(functools.partial(add_kernel, bit), tuple(outs), [VMEM, VMEM])(kept, came)
            return [done[i : i + 2] for i in range(0, len(done), 2)]
        done = call(code_kernel, tuple(shape((rows, width), i16) for width in widths), [VMEM, VMEM])(kept, came)
        return [done[i : i + 1] for i in range(len(done))]

    widths = [width for _, width in cuts]
    first, rest = widths[0], genes - widths[0]
    got = to_core(theirs)
    mine = half_of(0, 0, turned, first)
    if rest:
        got_rest = to_core(half_of(1, first, after(turned, mine), rest))
    sums = add_step(0, mine, got, widths[:1])
    if rest:
        sums += add_step(0, half_of(0, first, after(turned, *sums[0]), rest), got_rest, widths[1:])
    for bit in range(bits - 1):
        widths = [width // 2 for width in widths]
        came = [to_chip(code, bit) for _, code in sums]
        done = []
        for (kept, _), x, width in zip(sums, came, widths):
            done += add_step(bit + 1, kept, after(x, *done[-1]) if done else x, [width])
        sums = done
    held = []
    for (code,) in sums:
        came = to_chip(code, bits - 1)
        came = after(came, *held[-1]) if held else came
        held.append([call(cast_kernel, shape(code.shape, bf16), [VMEM, VMEM])(code, came)])
    masks = [0]
    for bit in reversed(range(bits - 1)):
        before = None
        for pieces in held:
            came = [to_chip(x, bit) for x in pieces]
            if before is not None:
                came = [after(x, before) for x in came]
            pieces += came
            before = came[-1]
        masks += [mask ^ (1 << bit) for mask in masks]
    sides = [pieces + [to_core(x) for x in pieces] for pieces in held]
    total = ()
    for (start, width), pieces in zip(cuts[:-1], sides):
        total = (
            call(
                functools.partial(part_kernel, masks, start, not total),
                shape((cells, rank), f32),
                [VMEM] * (1 + len(total) + len(pieces)),
                scratch=[pltpu.VMEM((rank, width), bf16)],
            )(dense, *total, *pieces),
        )
    (start, width), pieces = cuts[-1], sides[-1]
    gene = call(
        functools.partial(gene_kernel, masks), shape((rank, width), bf16), [VMEM] * len(pieces)
    )(*pieces)

    def cell(k):
        return call(
            functools.partial(cell_kernel, k, start),
            shape((height, rank), f32 if k == 0 else i16),
            [VMEM] * (2 + len(total)),
        )(dense, gene, *total)

    came = [to_gene(cell(k), k) for k in reversed(range(1, n_genes))]
    out = cell(0)
    for x in came:
        out = call(more_kernel, shape((height, rank), f32), [VMEM, VMEM], nbytes=16 * MIB)(out, x)
    return out


def solution(mesh):
    in_specs = (
        P("cells", None),
        P(("cells", "genes"), None, None),
        P(("cells", "genes")),
        P(("cells", "genes")),
        P(("cells", "genes")),
    )
    out_specs = P(("cells", "genes"), None)
    body = functools.partial(local, mesh.shape["cells"], mesh.shape["genes"])
    return jax.shard_map(body, mesh=mesh, in_specs=in_specs, out_specs=out_specs, check_vma=False)
```

```python
import functools

import jax
import jax.numpy as jnp
from jax import lax
from jax.experimental import pallas as pl
from jax.experimental.pallas import tpu as pltpu
from jax.sharding import PartitionSpec as P

GENE_BLOCKS = 16
CORES = 2
LANES = 128
PARTS = (1, 1, 1, 1)
MIB = 1 << 20

VMEM = pl.BlockSpec(memory_space=pltpu.VMEM)
SMEM = pl.BlockSpec(memory_space=pltpu.SMEM)
HBM = pl.BlockSpec(memory_space=pltpu.HBM)
f32, bf16, i16, i32 = jnp.float32, jnp.bfloat16, jnp.int16, jnp.int32


def encode(x, out, at=()):
    peak = jnp.max(jnp.abs(x), axis=0, keepdims=True)
    expo = jnp.ceil(jnp.log2(jnp.maximum(peak, 2.0**-100)))
    expo = jnp.clip(expo, -100.0, 126.0)
    code = jnp.round(x * jnp.exp2(14.0 - expo)).astype(i32)
    top = code[:16]
    row = lax.broadcasted_iota(i32, top.shape, 0)
    word = jnp.broadcast_to(expo.astype(i32) + 128, top.shape)
    marked = (top & ~1) | ((word >> jnp.minimum(row, 7)) & 1)
    top = jnp.where(row < 8, marked, top)
    out[at + (pl.ds(0, 16),)] = top.astype(i16)
    out[at + (pl.ds(16, x.shape[0] - 16),)] = code[16:].astype(i16)


def decode(code):
    code = code.astype(i32)
    head = code[:8]
    row = lax.broadcasted_iota(i32, head.shape, 0)
    word = jnp.sum((head & 1) << row, axis=0, keepdims=True)
    scale = jnp.exp2((word - (128 + 14)).astype(f32))
    return code.astype(f32) * scale


def core_and_chip():
    place = lax.axis_index("cells")
    return lax.rem(place, CORES), lax.div(place, CORES)


def call(body, outs, in_specs, scratch=(), mib=32, nbytes=0):
    return pl.pallas_call(
        body,
        out_shape=outs,
        in_specs=in_specs,
        out_specs=jax.tree.map(lambda _: VMEM, outs),
        scratch_shapes=list(scratch),
        compiler_params=pltpu.CompilerParams(vmem_limit_bytes=mib * MIB),
        cost_estimate=pl.CostEstimate(flops=0, bytes_accessed=nbytes, transcendentals=0),
    )


def block(index, size):
    return pl.ds(pl.multiple_of(index * size, size), size)


def dense_kernel(count, rows, cols, sketch, tiles, dense, turned, *refs):
    *outs, place, sketch_here, load_sems, sems = refs
    tile = tiles.shape[1]
    rows_place, cols_place = place
    loads = [
        pltpu.make_async_copy(src, dst, load_sems.at[i])
        for i, (src, dst) in enumerate(((rows, rows_place), (cols, cols_place), (sketch, sketch_here)))
    ]
    for load in loads:
        load.start()

    def clear(i, _):
        dense[block(i, 16), :] = jnp.zeros((16, dense.shape[1]), bf16)
        return 0

    lax.fori_loop(0, dense.shape[0] // 16, clear, 0)
    for load in loads[:2]:
        load.wait()

    def copy(s):
        to = dense.at[block(rows_place[s], tile), block(cols_place[s], tile)]
        return pltpu.make_async_copy(tiles.at[s], to, sems.at[s])

    def start(s, _):
        copy(s).start()
        return 0

    def wait(s, _):
        copy(s).wait()
        return 0

    lax.fori_loop(0, count[0], start, 0)
    loads[2].wait()
    turned[...] = sketch_here[...].T
    lax.fori_loop(0, count[0], wait, 0)
    start = 0
    for out in outs:
        half_kernel(1, start, turned, dense, out)
        start += out.shape[1]


def half_kernel(other, start, turned, dense, out):
    core, _ = core_and_chip()
    rows, width = out.shape
    left = turned[block(core ^ other, rows), :]
    step = min(width, 512)
    for j in range(0, width, step):
        part = jnp.dot(left, dense[:, start + j : start + j + step], preferred_element_type=f32)
        if other:
            encode(part, out.at[:, j : j + step])
        else:
            out[:, j : j + step] = part


def add_kernel(bit, mine, got, *outs):
    _, chip = core_and_chip()
    start = 0
    for keep, send in zip(outs[::2], outs[1::2]):
        width = keep.shape[1]
        ours = (chip >> bit) & 1
        cut = pl.ds(pl.multiple_of(start + (1 - ours) * width, width), width)
        encode(mine[:, cut] + decode(got[:, cut]), send)
        cut = pl.ds(pl.multiple_of(start + ours * width, width), width)
        keep[...] = mine[:, cut] + decode(got[:, cut])
        start += 2 * width


def code_kernel(mine, got, *outs):
    start = 0
    for out in outs:
        cut = slice(start, start + out.shape[1])
        encode(mine[:, cut] + decode(got[:, cut]), out)
        start += out.shape[1]


def both_kernel(mine, got, *outs):
    start = 0
    for keep, send in zip(outs[::2], outs[1::2]):
        cut = slice(start, start + keep.shape[1])
        total = mine[:, cut] + decode(got[:, cut])
        keep[...] = total
        encode(total, send)
        start += keep.shape[1]


def pick_kernel(cast, got, out):
    _, chip = core_and_chip()
    middle = (chip == 1) | (chip == 2)

    @pl.when(middle)
    def _():
        out[...] = cast[...]

    @pl.when(jnp.logical_not(middle))
    def _():
        out[...] = got[...]


def cast_kernel(code, got, out):
    out[...] = (decode(code[...]) + decode(got[...])).astype(bf16)


def join(masks, pieces, gene):
    core, chip = core_and_chip()
    rows, width = pieces[0].shape
    for k, mask in enumerate(masks):
        place, size = 0, gene.shape[1]
        for bit in range(len(masks).bit_length() - 1):
            size //= 2
            place = place + (((chip ^ mask) >> bit) & 1) * size
        cut = pl.ds(pl.multiple_of(place, width), width)
        gene[block(core, rows), cut] = pieces[k][...]
        gene[block(1 - core, rows), cut] = pieces[len(masks) + k][...]


def gene_kernel(masks, *refs):
    join(masks, refs[:-1], refs[-1])


def product(left, gene):
    return lax.dot_general(left, gene, (((1,), (1,)), ((), ())), preferred_element_type=f32)


def part_kernel(masks, start, fresh, dense, *refs):
    *pieces, out, gene = refs
    if not fresh:
        before, *pieces = pieces
    join(masks, pieces, gene)
    step = 256
    for i in range(0, out.shape[0], step):
        part = product(dense[i : i + step, start : start + gene.shape[1]], gene[...])
        out[i : i + step, :] = part if fresh else before[i : i + step, :] + part


def cell_kernel(k, start, dense, gene, *refs):
    *before, out = refs
    cut = block(lax.axis_index("genes") ^ k, out.shape[0])
    part = product(dense[cut, start : start + gene.shape[1]], gene[...])
    if before:
        part = part + before[0][cut, :]
    if k == 0:
        out[...] = part
    else:
        encode(part, out)


def more_kernel(total, got, out):
    out[...] = total[...] + decode(got[...])


def cuts_of(genes, bits):
    for parts in (PARTS, (1, 1)):
        unit = genes // sum(parts)
        if unit >> max(bits - 1, 0) >= LANES:
            ends = [sum(parts[:i]) * unit for i in range(len(parts))]
            return tuple((at, p * unit) for at, p in zip(ends, parts))
    return ((0, genes),)


def local(n_cells, n_genes, sketch, tiles, tile_rows, tile_cols, tile_counts):
    cells, rank = sketch.shape
    slots, tile, _ = tiles.shape
    genes = GENE_BLOCKS * tile
    bits = (n_cells // CORES).bit_length() - 1
    rows = rank // CORES
    height = cells // n_genes
    shape = jax.ShapeDtypeStruct
    chips = n_cells // CORES
    hub = chips == 4
    cuts = cuts_of(genes, bits)

    def to_core(x):
        return lax.ppermute(x, "cells", [(i, i ^ 1) for i in range(n_cells)])

    def to_chip(x, bit):
        return lax.ppermute(x, "cells", [(i, i ^ (CORES << bit)) for i in range(n_cells)])

    def to_gene(x, k):
        return lax.ppermute(x, "genes", [(i, i ^ k) for i in range(n_genes)])

    widths = [width for _, width in cuts]
    first, rest = widths[0], genes - widths[0]
    dense, turned, *theirs = call(
        dense_kernel,
        (shape((cells, genes), bf16), shape((rank, cells), bf16))
        + tuple(shape((rows, width), i16) for width in (first, rest) if width),
        [SMEM] + [HBM] * 4,
        scratch=[
            (pltpu.SMEM((slots,), i32), pltpu.SMEM((slots,), i32)),
            pltpu.VMEM((cells, rank), bf16),
            pltpu.SemaphoreType.DMA((3,)),
            pltpu.SemaphoreType.DMA((slots,)),
        ],
    )(tile_counts, *(pltpu.with_memory_space_constraint(x, pltpu.HBM) for x in (tile_rows, tile_cols, sketch, tiles)))

    def half_of(other, start, turned, width):
        body = functools.partial(half_kernel, other, start)
        return call(body, shape((rows, width), i16 if other else f32), [VMEM, VMEM])(turned, dense)

    def after(x, *others):
        return lax.optimization_barrier((x, *others))[0]

    def add_step(bit, kept, came, widths):
        if hub and bit == 0:
            outs = [shape((rows, width), kind) for width in widths for kind in (f32, i16)]
            done = call(both_kernel, tuple(outs), [VMEM, VMEM])(kept, came)
            return [done[i : i + 2] for i in range(0, len(done), 2)]
        if bit < bits - 1:
            outs = [shape((rows, width // 2), kind) for width in widths for kind in (f32, i16)]
            done = call(functools.partial(add_kernel, bit), tuple(outs), [VMEM, VMEM])(kept, came)
            return [done[i : i + 2] for i in range(0, len(done), 2)]
        done = call(code_kernel, tuple(shape((rows, width), i16) for width in widths), [VMEM, VMEM])(kept, came)
        return [done[i : i + 1] for i in range(len(done))]

    def through_hubs(sums):
        def move(x, pairs):
            return lax.ppermute(x, "cells", [(a * CORES + i, b * CORES + i) for a, b in pairs for i in range(CORES)])

        came = [move(code, ((0, 1), (3, 2))) for _, code in sums]
        codes = []
        for (kept, _), x in zip(sums, came):
            x = after(x, codes[-1]) if codes else x
            codes += call(code_kernel, (shape(x.shape, i16),), [VMEM, VMEM])(kept, x)
        came = [move(code, ((1, 2), (2, 1))) for code in codes]
        casts = []
        for code, x in zip(codes, came):
            x = after(x, casts[-1]) if casts else x
            casts.append(call(cast_kernel, shape(x.shape, bf16), [VMEM, VMEM])(code, x))
        came = [move(x, ((1, 0), (2, 3))) for x in casts]
        return [(casts[0], came[0])] + [(cast, after(x, casts[-1])) for cast, x in zip(casts[1:], came[1:])]

    def by_halving(sums):
        widths = [sum_[0].shape[1] for sum_ in sums]
        for bit in range(bits - 1):
            came = [to_chip(code, bit) for _, code in sums]
            done = []
            for (kept, _), x, width in zip(sums, came, widths):
                done += add_step(bit + 1, kept, after(x, *done[-1]) if done else x, [width])
            sums = done
            widths = [width // 2 for width in widths]
        held = []
        for (code,) in sums:
            came = to_chip(code, bits - 1)
            came = after(came, *held[-1]) if held else came
            held.append([call(cast_kernel, shape(code.shape, bf16), [VMEM, VMEM])(code, came)])
        masks = [0]
        for bit in reversed(range(bits - 1)):
            before = None
            for pieces in held:
                came = [to_chip(x, bit) for x in pieces]
                if before is not None:
                    came = [after(x, before) for x in came]
                pieces += came
                before = came[-1]
            masks += [mask ^ (1 << bit) for mask in masks]
        return masks, held

    got = [to_core(x) for x in theirs]
    sums = add_step(0, half_of(0, 0, turned, first), got[0], widths[:1])
    if rest:
        sums += add_step(0, half_of(0, first, after(turned, *sums[0]), rest), got[1], widths[1:])
    if hub:
        sides = through_hubs(sums)
        masks = [0]
    else:
        masks, sides = by_halving(sums)
    totals = []
    for i, ((start, width), pieces) in enumerate(zip(cuts, sides)):
        if i >= 2:
            pieces = [after(x, totals[i - 2]) for x in pieces]
        if hub:
            pieces = [call(pick_kernel, shape(pieces[0].shape, bf16), [VMEM, VMEM])(*pieces)]
        pieces = pieces + [to_core(x) for x in pieces]
        if i == len(cuts) - 1:
            break
        before = totals[-1:]
        totals.append(
            call(
                functools.partial(part_kernel, masks, start, not before),
                shape((cells, rank), f32),
                [VMEM] * (1 + len(before) + len(pieces)),
                scratch=[pltpu.VMEM((rank, width), bf16)],
            )(dense, *before, *pieces)
        )
    gene = call(
        functools.partial(gene_kernel, masks), shape((rank, width), bf16), [VMEM] * len(pieces)
    )(*pieces)

    def cell(k):
        return call(
            functools.partial(cell_kernel, k, start),
            shape((height, rank), f32 if k == 0 else i16),
            [VMEM] * (2 + len(totals[-1:])),
        )(dense, gene, *totals[-1:])

    came = [to_gene(cell(k), k) for k in reversed(range(1, n_genes))]
    out = cell(0)
    for x in came:
        out = call(more_kernel, shape((height, rank), f32), [VMEM, VMEM], nbytes=16 * MIB)(out, x)
    return out


def solution(mesh):
    in_specs = (
        P("cells", None),
        P(("cells", "genes"), None, None),
        P(("cells", "genes")),
        P(("cells", "genes")),
        P(("cells", "genes")),
    )
    out_specs = P(("cells", "genes"), None)
    body = functools.partial(local, mesh.shape["cells"], mesh.shape["genes"])
    return jax.shard_map(body, mesh=mesh, in_specs=in_specs, out_specs=out_specs, check_vma=False)
```

```python
import functools

import jax
import jax.numpy as jnp
from jax import lax
from jax.experimental import pallas as pl
from jax.experimental.pallas import tpu as pltpu
from jax.sharding import PartitionSpec as P

GENE_BLOCKS = 16
CORES = 2
LANES = 128
STREAMS = 2
MIB = 1 << 20

VMEM = pl.BlockSpec(memory_space=pltpu.VMEM)
SMEM = pl.BlockSpec(memory_space=pltpu.SMEM)
HBM = pl.BlockSpec(memory_space=pltpu.HBM)
f32, bf16, i16, i32 = jnp.float32, jnp.bfloat16, jnp.int16, jnp.int32


def encode(x, out, at=()):
    peak = jnp.max(jnp.abs(x), axis=0, keepdims=True)
    expo = jnp.ceil(jnp.log2(jnp.maximum(peak, 2.0**-100)))
    expo = jnp.clip(expo, -100.0, 126.0)
    code = jnp.round(x * jnp.exp2(14.0 - expo)).astype(i32)
    top = code[:16]
    row = lax.broadcasted_iota(i32, top.shape, 0)
    word = jnp.broadcast_to(expo.astype(i32) + 128, top.shape)
    marked = (top & ~1) | ((word >> jnp.minimum(row, 7)) & 1)
    top = jnp.where(row < 8, marked, top)
    out[at + (pl.ds(0, 16),)] = top.astype(i16)
    out[at + (pl.ds(16, x.shape[0] - 16),)] = code[16:].astype(i16)


def decode(code):
    code = code.astype(i32)
    head = code[:8]
    row = lax.broadcasted_iota(i32, head.shape, 0)
    word = jnp.sum((head & 1) << row, axis=0, keepdims=True)
    scale = jnp.exp2((word - (128 + 14)).astype(f32))
    return code.astype(f32) * scale


def core_and_chip():
    place = lax.axis_index("cells")
    return lax.rem(place, CORES), lax.div(place, CORES)


def call(body, outs, in_specs, scratch=(), mib=32, nbytes=0):
    return pl.pallas_call(
        body,
        out_shape=outs,
        in_specs=in_specs,
        out_specs=jax.tree.map(lambda _: VMEM, outs),
        scratch_shapes=list(scratch),
        compiler_params=pltpu.CompilerParams(vmem_limit_bytes=mib * MIB),
        cost_estimate=pl.CostEstimate(flops=0, bytes_accessed=nbytes, transcendentals=0),
    )


def block(index, size):
    return pl.ds(pl.multiple_of(index * size, size), size)


def dense_kernel(count, rows, cols, sketch, tiles, dense, turned, *refs):
    *outs, place, sketch_here, load_sems, sems = refs
    tile = tiles.shape[1]
    rows_place, cols_place = place
    loads = [
        pltpu.make_async_copy(src, dst, load_sems.at[i])
        for i, (src, dst) in enumerate(((rows, rows_place), (cols, cols_place), (sketch, sketch_here)))
    ]
    for load in loads:
        load.start()

    def clear(i, _):
        dense[block(i, 16), :] = jnp.zeros((16, dense.shape[1]), bf16)
        return 0

    lax.fori_loop(0, dense.shape[0] // 16, clear, 0)
    for load in loads[:2]:
        load.wait()

    def copy(s):
        to = dense.at[block(rows_place[s], tile), block(cols_place[s], tile)]
        return pltpu.make_async_copy(tiles.at[s], to, sems.at[s])

    def start(s, _):
        copy(s).start()
        return 0

    def wait(s, _):
        copy(s).wait()
        return 0

    lax.fori_loop(0, count[0], start, 0)
    loads[2].wait()
    turned[...] = sketch_here[...].T
    lax.fori_loop(0, count[0], wait, 0)
    start = 0
    for out in outs:
        half_kernel(1, start, turned, dense, out)
        start += out.shape[1]


def half_kernel(other, start, turned, dense, out):
    core, _ = core_and_chip()
    rows, width = out.shape
    left = turned[block(core ^ other, rows), :]
    step = min(width, 512)
    for j in range(0, width, step):
        part = jnp.dot(left, dense[:, start + j : start + j + step], preferred_element_type=f32)
        if other:
            encode(part, out.at[:, j : j + step])
        else:
            out[:, j : j + step] = part


def add_kernel(bit, mine, got, *outs):
    _, chip = core_and_chip()
    start = 0
    for keep, send in zip(outs[::2], outs[1::2]):
        width = keep.shape[1]
        ours = (chip >> bit) & 1
        cut = pl.ds(pl.multiple_of(start + (1 - ours) * width, width), width)
        encode(mine[:, cut] + decode(got[:, cut]), send)
        cut = pl.ds(pl.multiple_of(start + ours * width, width), width)
        keep[...] = mine[:, cut] + decode(got[:, cut])
        start += 2 * width


def code_kernel(mine, got, *outs):
    start = 0
    for out in outs:
        cut = slice(start, start + out.shape[1])
        encode(mine[:, cut] + decode(got[:, cut]), out)
        start += out.shape[1]


def place(chip, genes, count):
    at, size = 0, genes
    for bit in range(count.bit_length() - 1):
        size //= 2
        at = at + ((chip >> bit) & 1) * size
    return pl.ds(pl.multiple_of(at, size), size)


def deal_kernel(mine, got, *outs):
    _, chip = core_and_chip()
    count = len(outs) // STREAMS
    for i, out in enumerate(outs):
        stream, k = divmod(i, count)
        cut = place(chip ^ k, mine.shape[1] // STREAMS, count)
        cut = pl.ds(pl.multiple_of(stream * (mine.shape[1] // STREAMS) + cut.start, cut.size), cut.size)
        part = mine[:, cut] + decode(got[:, cut])
        if k == 0:
            out[...] = part
        else:
            encode(part, out)


def sum_kernel(own, *refs):
    *got, out = refs
    total = own[...]
    for ref in got:
        total = total + decode(ref[...])
    out[...] = total.astype(bf16)


def cast_kernel(code, got, out):
    out[...] = (decode(code[...]) + decode(got[...])).astype(bf16)


def join(masks, pieces, gene):
    core, chip = core_and_chip()
    rows = pieces[0].shape[0]
    for k, mask in enumerate(masks):
        cut = place(chip ^ mask, gene.shape[1], len(masks))
        gene[block(core, rows), cut] = pieces[k][...]
        gene[block(1 - core, rows), cut] = pieces[len(masks) + k][...]


def gene_kernel(masks, *refs):
    join(masks, refs[:-1], refs[-1])


def product(left, gene):
    return lax.dot_general(left, gene, (((1,), (1,)), ((), ())), preferred_element_type=f32)


def part_kernel(masks, start, fresh, dense, *refs):
    *pieces, out, gene = refs
    if not fresh:
        before, *pieces = pieces
    join(masks, pieces, gene)
    step = 256
    for i in range(0, out.shape[0], step):
        part = product(dense[i : i + step, start : start + gene.shape[1]], gene[...])
        out[i : i + step, :] = part if fresh else before[i : i + step, :] + part


def cell_kernel(k, start, dense, gene, *refs):
    *before, out = refs
    cut = block(lax.axis_index("genes") ^ k, out.shape[0])
    part = product(dense[cut, start : start + gene.shape[1]], gene[...])
    if before:
        part = part + before[0][cut, :]
    if k == 0:
        out[...] = part
    else:
        encode(part, out)


def more_kernel(total, got, out):
    out[...] = total[...] + decode(got[...])


def cuts_of(genes, bits):
    half = genes // 2
    if half >> max(bits - 1, 0) >= LANES:
        return ((0, half), (half, half))
    return ((0, genes),)


def local(n_cells, n_genes, sketch, tiles, tile_rows, tile_cols, tile_counts):
    cells, rank = sketch.shape
    slots, tile, _ = tiles.shape
    genes = GENE_BLOCKS * tile
    bits = (n_cells // CORES).bit_length() - 1
    rows = rank // CORES
    height = cells // n_genes
    shape = jax.ShapeDtypeStruct
    chips = n_cells // CORES
    cuts = cuts_of(genes, bits)

    def to_core(x):
        return lax.ppermute(x, "cells", [(i, i ^ 1) for i in range(n_cells)])

    def to_chip(x, bit):
        return lax.ppermute(x, "cells", [(i, i ^ (CORES << bit)) for i in range(n_cells)])

    def to_gene(x, k):
        return lax.ppermute(x, "genes", [(i, i ^ k) for i in range(n_genes)])

    widths = [width for _, width in cuts]
    first, rest = widths[0], genes - widths[0]
    direct = bits > 1 and rest > 0 and first // chips >= LANES
    dense, turned, *theirs = call(
        dense_kernel,
        (shape((cells, genes), bf16), shape((rank, cells), bf16))
        + tuple(shape((rows, width), i16) for width in ((genes,) if direct else (first, rest)) if width),
        [SMEM] + [HBM] * 4,
        scratch=[
            (pltpu.SMEM((slots,), i32), pltpu.SMEM((slots,), i32)),
            pltpu.VMEM((cells, rank), bf16),
            pltpu.SemaphoreType.DMA((3,)),
            pltpu.SemaphoreType.DMA((slots,)),
        ],
    )(tile_counts, *(pltpu.with_memory_space_constraint(x, pltpu.HBM) for x in (tile_rows, tile_cols, sketch, tiles)))

    def half_of(other, start, turned, width):
        body = functools.partial(half_kernel, other, start)
        return call(body, shape((rows, width), i16 if other else f32), [VMEM, VMEM])(turned, dense)

    def after(x, *others):
        return lax.optimization_barrier((x, *others))[0] if others else x

    def add_step(bit, kept, came, widths):
        if bit < bits - 1:
            outs = [shape((rows, width // 2), kind) for width in widths for kind in (f32, i16)]
            done = call(functools.partial(add_kernel, bit), tuple(outs), [VMEM, VMEM])(kept, came)
            return [done[i : i + 2] for i in range(0, len(done), 2)]
        done = call(code_kernel, tuple(shape((rows, width), i16) for width in widths), [VMEM, VMEM])(kept, came)
        return [done[i : i + 1] for i in range(len(done))]

    def to_chips(x, k):
        return lax.ppermute(x, "cells", [(i, i ^ (k * CORES)) for i in range(n_cells)])

    def by_halving(sums):
        widths = [sum_[0].shape[1] for sum_ in sums]
        for bit in range(bits - 1):
            came = [to_chip(code, bit) for _, code in sums]
            done = []
            for (kept, _), x, width in zip(sums, came, widths):
                done += add_step(bit + 1, kept, after(x, *(done[-1] if done else ())), [width])
            sums = done
            widths = [width // 2 for width in widths]
        held = []
        for (code,) in sums:
            came = to_chip(code, bits - 1)
            came = after(came, *held[-1]) if held else came
            held.append([call(cast_kernel, shape(code.shape, bf16), [VMEM, VMEM])(code, came)])
        masks = [0]
        for bit in reversed(range(bits - 1)):
            before = None
            for pieces in held:
                came = [to_chip(x, bit) for x in pieces]
                if before is not None:
                    came = [after(x, before) for x in came]
                pieces += came
                before = came[-1]
            masks += [mask ^ (1 << bit) for mask in masks]
        return masks, held

    got = [to_core(x) for x in theirs]
    if direct:
        width = first // chips
        dealt = ((shape((rows, width), f32),) + (shape((rows, width), i16),) * (chips - 1)) * STREAMS
        pieces = call(deal_kernel, dealt, [VMEM, VMEM])(half_of(0, 0, turned, genes), got[0])
        pieces = [pieces[i * chips : (i + 1) * chips] for i in range(STREAMS)]
        sides = []
        for own, *codes in pieces:
            came = [to_chips(codes[k - 1], k) for k in reversed(range(1, chips))]
            chunk = call(sum_kernel, shape(own.shape, bf16), [VMEM] * chips)(own, *came)
            came = [to_chips(chunk, k) for k in reversed(range(1, chips))][::-1]
            sides.append([chunk] + came)
        sides[0][1:] = [after(x, sides[1][0]) for x in sides[0][1:]]
        masks = [list(range(chips))] * STREAMS
    else:
        sums = add_step(0, half_of(0, 0, turned, first), got[0], [first])
        if rest:
            sums += add_step(0, half_of(0, first, after(turned, *sums[0]), rest), got[1], [rest])
        masks, sides = by_halving(sums)
        masks = [masks] * len(sides)
    totals = []
    for i, ((start, width), pieces) in enumerate(zip(cuts, sides)):
        pieces = pieces + [to_core(x) for x in pieces]
        if i == len(cuts) - 1:
            break
        before = totals[-1:]
        totals.append(
            call(
                functools.partial(part_kernel, masks[i], start, not before),
                shape((cells, rank), f32),
                [VMEM] * (1 + len(before) + len(pieces)),
                scratch=[pltpu.VMEM((rank, width), bf16)],
            )(dense, *before, *pieces)
        )
    gene = call(
        functools.partial(gene_kernel, masks[-1]), shape((rank, width), bf16), [VMEM] * len(pieces)
    )(*pieces)

    def cell(k):
        return call(
            functools.partial(cell_kernel, k, start),
            shape((height, rank), f32 if k == 0 else i16),
            [VMEM] * (2 + len(totals[-1:])),
        )(dense, gene, *totals[-1:])

    came = [to_gene(cell(k), k) for k in reversed(range(1, n_genes))]
    out = cell(0)
    for x in came:
        out = call(more_kernel, shape((height, rank), f32), [VMEM, VMEM], nbytes=16 * MIB)(out, x)
    return out


def solution(mesh):
    in_specs = (
        P("cells", None),
        P(("cells", "genes"), None, None),
        P(("cells", "genes")),
        P(("cells", "genes")),
        P(("cells", "genes")),
    )
    out_specs = P(("cells", "genes"), None)
    body = functools.partial(local, mesh.shape["cells"], mesh.shape["genes"])
    return jax.shard_map(body, mesh=mesh, in_specs=in_specs, out_specs=out_specs, check_vma=False)
```

```python
import functools

import jax
import jax.numpy as jnp
from jax import lax
from jax.experimental import pallas as pl
from jax.experimental.pallas import tpu as pltpu
from jax.sharding import PartitionSpec as P

GENE_BLOCKS = 16
CORES = 2
LANES = 128
PARTS = (1, 1, 1, 1)
MIB = 1 << 20

VMEM = pl.BlockSpec(memory_space=pltpu.VMEM)
SMEM = pl.BlockSpec(memory_space=pltpu.SMEM)
HBM = pl.BlockSpec(memory_space=pltpu.HBM)
f32, bf16, i16, i32 = jnp.float32, jnp.bfloat16, jnp.int16, jnp.int32


def encode(x, out, at=()):
    peak = jnp.max(jnp.abs(x), axis=0, keepdims=True)
    expo = jnp.ceil(jnp.log2(jnp.maximum(peak, 2.0**-100)))
    expo = jnp.clip(expo, -100.0, 126.0)
    code = jnp.round(x * jnp.exp2(14.0 - expo)).astype(i32)
    top = code[:16]
    row = lax.broadcasted_iota(i32, top.shape, 0)
    word = jnp.broadcast_to(expo.astype(i32) + 128, top.shape)
    marked = (top & ~1) | ((word >> jnp.minimum(row, 7)) & 1)
    top = jnp.where(row < 8, marked, top)
    out[at + (pl.ds(0, 16),)] = top.astype(i16)
    out[at + (pl.ds(16, x.shape[0] - 16),)] = code[16:].astype(i16)


def decode(code):
    code = code.astype(i32)
    head = code[:8]
    row = lax.broadcasted_iota(i32, head.shape, 0)
    word = jnp.sum((head & 1) << row, axis=0, keepdims=True)
    scale = jnp.exp2((word - (128 + 14)).astype(f32))
    return code.astype(f32) * scale


def core_and_chip():
    place = lax.axis_index("cells")
    return lax.rem(place, CORES), lax.div(place, CORES)


def call(body, outs, in_specs, scratch=(), mib=32, nbytes=0):
    return pl.pallas_call(
        body,
        out_shape=outs,
        in_specs=in_specs,
        out_specs=jax.tree.map(lambda _: VMEM, outs),
        scratch_shapes=list(scratch),
        compiler_params=pltpu.CompilerParams(vmem_limit_bytes=mib * MIB),
        cost_estimate=pl.CostEstimate(flops=0, bytes_accessed=nbytes, transcendentals=0),
    )


def block(index, size):
    return pl.ds(pl.multiple_of(index * size, size), size)


def dense_kernel(count, rows, cols, sketch, tiles, dense, turned, *refs):
    *outs, place, sketch_here, load_sems, sems = refs
    tile = tiles.shape[1]
    rows_place, cols_place = place
    loads = [
        pltpu.make_async_copy(src, dst, load_sems.at[i])
        for i, (src, dst) in enumerate(((rows, rows_place), (cols, cols_place), (sketch, sketch_here)))
    ]
    for load in loads:
        load.start()

    def clear(i, _):
        dense[block(i, 16), :] = jnp.zeros((16, dense.shape[1]), bf16)
        return 0

    lax.fori_loop(0, dense.shape[0] // 16, clear, 0)
    for load in loads[:2]:
        load.wait()

    def copy(s):
        to = dense.at[block(rows_place[s], tile), block(cols_place[s], tile)]
        return pltpu.make_async_copy(tiles.at[s], to, sems.at[s])

    def start(s, _):
        copy(s).start()
        return 0

    def wait(s, _):
        copy(s).wait()
        return 0

    lax.fori_loop(0, count[0], start, 0)
    loads[2].wait()
    turned[...] = sketch_here[...].T
    lax.fori_loop(0, count[0], wait, 0)
    start = 0
    for out in outs:
        half_kernel(1, start, turned, dense, out)
        start += out.shape[1]


def half_kernel(other, start, turned, dense, out):
    core, _ = core_and_chip()
    rows, width = out.shape
    left = turned[block(core ^ other, rows), :]
    step = min(width, 512)
    for j in range(0, width, step):
        part = jnp.dot(left, dense[:, start + j : start + j + step], preferred_element_type=f32)
        if other:
            encode(part, out.at[:, j : j + step])
        else:
            out[:, j : j + step] = part


def add_kernel(bit, mine, got, *outs):
    _, chip = core_and_chip()
    start = 0
    for keep, send in zip(outs[::2], outs[1::2]):
        width = keep.shape[1]
        ours = (chip >> bit) & 1
        cut = pl.ds(pl.multiple_of(start + (1 - ours) * width, width), width)
        encode(mine[:, cut] + decode(got[:, cut]), send)
        cut = pl.ds(pl.multiple_of(start + ours * width, width), width)
        keep[...] = mine[:, cut] + decode(got[:, cut])
        start += 2 * width


def code_kernel(mine, got, *outs):
    start = 0
    for out in outs:
        cut = slice(start, start + out.shape[1])
        encode(mine[:, cut] + decode(got[:, cut]), out)
        start += out.shape[1]


def both_kernel(mine, got, *outs):
    start = 0
    for keep, send in zip(outs[::2], outs[1::2]):
        cut = slice(start, start + keep.shape[1])
        total = mine[:, cut] + decode(got[:, cut])
        keep[...] = total
        encode(total, send)
        start += keep.shape[1]


def pick_kernel(cast, got, out):
    _, chip = core_and_chip()
    middle = (chip == 1) | (chip == 2)

    @pl.when(middle)
    def _():
        out[...] = cast[...]

    @pl.when(jnp.logical_not(middle))
    def _():
        out[...] = got[...]


def cast_kernel(code, got, out):
    out[...] = (decode(code[...]) + decode(got[...])).astype(bf16)


def join(masks, pieces, gene):
    core, chip = core_and_chip()
    rows, width = pieces[0].shape
    for k, mask in enumerate(masks):
        place, size = 0, gene.shape[1]
        for bit in range(len(masks).bit_length() - 1):
            size //= 2
            place = place + (((chip ^ mask) >> bit) & 1) * size
        cut = pl.ds(pl.multiple_of(place, width), width)
        gene[block(core, rows), cut] = pieces[k][...]
        gene[block(1 - core, rows), cut] = pieces[len(masks) + k][...]


def gene_kernel(masks, *refs):
    join(masks, refs[:-1], refs[-1])


def product(left, gene):
    return lax.dot_general(left, gene, (((1,), (1,)), ((), ())), preferred_element_type=f32)


def part_kernel(masks, start, fresh, dense, *refs):
    *pieces, out, gene = refs
    if not fresh:
        before, *pieces = pieces
    join(masks, pieces, gene)
    step = 256
    for i in range(0, out.shape[0], step):
        part = product(dense[i : i + step, start : start + gene.shape[1]], gene[...])
        out[i : i + step, :] = part if fresh else before[i : i + step, :] + part


def cell_kernel(k, start, dense, gene, *refs):
    *before, out = refs
    cut = block(lax.axis_index("genes") ^ k, out.shape[0])
    part = product(dense[cut, start : start + gene.shape[1]], gene[...])
    if before:
        part = part + before[0][cut, :]
    if k == 0:
        out[...] = part
    else:
        encode(part, out)


def more_kernel(total, got, out):
    out[...] = total[...] + decode(got[...])


def cuts_of(genes, bits):
    for parts in (PARTS, (1, 1)):
        unit = genes // sum(parts)
        if unit >> max(bits - 1, 0) >= LANES:
            ends = [sum(parts[:i]) * unit for i in range(len(parts))]
            return tuple((at, p * unit) for at, p in zip(ends, parts))
    return ((0, genes),)


def local(n_cells, n_genes, sketch, tiles, tile_rows, tile_cols, tile_counts):
    cells, rank = sketch.shape
    slots, tile, _ = tiles.shape
    genes = GENE_BLOCKS * tile
    bits = (n_cells // CORES).bit_length() - 1
    rows = rank // CORES
    height = cells // n_genes
    shape = jax.ShapeDtypeStruct
    chips = n_cells // CORES
    hub = chips == 4
    cuts = cuts_of(genes, bits)

    def to_core(x):
        return lax.ppermute(x, "cells", [(i, i ^ 1) for i in range(n_cells)])

    def to_chip(x, bit):
        return lax.ppermute(x, "cells", [(i, i ^ (CORES << bit)) for i in range(n_cells)])

    def to_gene(x, k):
        return lax.ppermute(x, "genes", [(i, i ^ k) for i in range(n_genes)])

    widths = [width for _, width in cuts]
    first, rest = widths[0], genes - widths[0]
    dense, turned, *theirs = call(
        dense_kernel,
        (shape((cells, genes), bf16), shape((rank, cells), bf16))
        + tuple(shape((rows, width), i16) for width in (first, rest) if width),
        [SMEM] + [HBM] * 4,
        scratch=[
            (pltpu.SMEM((slots,), i32), pltpu.SMEM((slots,), i32)),
            pltpu.VMEM((cells, rank), bf16),
            pltpu.SemaphoreType.DMA((3,)),
            pltpu.SemaphoreType.DMA((slots,)),
        ],
    )(tile_counts, *(pltpu.with_memory_space_constraint(x, pltpu.HBM) for x in (tile_rows, tile_cols, sketch, tiles)))

    def half_of(other, start, turned, width):
        body = functools.partial(half_kernel, other, start)
        return call(body, shape((rows, width), i16 if other else f32), [VMEM, VMEM])(turned, dense)

    def after(x, *others):
        return lax.optimization_barrier((x, *others))[0]

    def add_step(bit, kept, came, widths):
        if hub and bit == 0:
            outs = [shape((rows, width), kind) for width in widths for kind in (f32, i16)]
            done = call(both_kernel, tuple(outs), [VMEM, VMEM])(kept, came)
            return [done[i : i + 2] for i in range(0, len(done), 2)]
        if bit < bits - 1:
            outs = [shape((rows, width // 2), kind) for width in widths for kind in (f32, i16)]
            done = call(functools.partial(add_kernel, bit), tuple(outs), [VMEM, VMEM])(kept, came)
            return [done[i : i + 2] for i in range(0, len(done), 2)]
        done = call(code_kernel, tuple(shape((rows, width), i16) for width in widths), [VMEM, VMEM])(kept, came)
        return [done[i : i + 1] for i in range(len(done))]

    def through_hubs(sums):
        def move(x, to):
            return lax.ppermute(x, "cells", [(a * CORES + i, b * CORES + i) for a, b in enumerate(to) for i in range(CORES)])

        came = [move(code, (1, 0, 3, 2)) for _, code in sums]
        codes = []
        for (kept, _), x in zip(sums, came):
            x = after(x, codes[-1]) if codes else x
            codes += call(code_kernel, (shape(x.shape, i16),), [VMEM, VMEM])(kept, x)
        came = [move(code, (0, 2, 1, 3)) for code in codes]
        casts = []
        for code, x in zip(codes, came):
            x = after(x, casts[-1]) if casts else x
            casts.append(call(cast_kernel, shape(x.shape, bf16), [VMEM, VMEM])(code, x))
        came = [move(x, (1, 0, 3, 2)) for x in casts]
        return [(casts[0], came[0])] + [(cast, after(x, casts[-1])) for cast, x in zip(casts[1:], came[1:])]

    def by_halving(sums):
        widths = [sum_[0].shape[1] for sum_ in sums]
        for bit in range(bits - 1):
            came = [to_chip(code, bit) for _, code in sums]
            done = []
            for (kept, _), x, width in zip(sums, came, widths):
                done += add_step(bit + 1, kept, after(x, *done[-1]) if done else x, [width])
            sums = done
            widths = [width // 2 for width in widths]
        held = []
        for (code,) in sums:
            came = to_chip(code, bits - 1)
            came = after(came, *held[-1]) if held else came
            held.append([call(cast_kernel, shape(code.shape, bf16), [VMEM, VMEM])(code, came)])
        masks = [0]
        for bit in reversed(range(bits - 1)):
            before = None
            for pieces in held:
                came = [to_chip(x, bit) for x in pieces]
                if before is not None:
                    came = [after(x, before) for x in came]
                pieces += came
                before = came[-1]
            masks += [mask ^ (1 << bit) for mask in masks]
        return masks, held

    got = [to_core(x) for x in theirs]
    sums = add_step(0, half_of(0, 0, turned, first), got[0], widths[:1])
    if rest:
        sums += add_step(0, half_of(0, first, after(turned, *sums[0]), rest), got[1], widths[1:])
    if hub:
        sides = through_hubs(sums)
        masks = [0]
    else:
        masks, sides = by_halving(sums)
    totals = []
    for i, ((start, width), pieces) in enumerate(zip(cuts, sides)):
        if i >= 2:
            pieces = [after(x, totals[i - 2]) for x in pieces]
        if hub:
            pieces = [call(pick_kernel, shape(pieces[0].shape, bf16), [VMEM, VMEM])(*pieces)]
        pieces = pieces + [to_core(x) for x in pieces]
        if i == len(cuts) - 1:
            break
        before = totals[-1:]
        totals.append(
            call(
                functools.partial(part_kernel, masks, start, not before),
                shape((cells, rank), f32),
                [VMEM] * (1 + len(before) + len(pieces)),
                scratch=[pltpu.VMEM((rank, width), bf16)],
            )(dense, *before, *pieces)
        )
    gene = call(
        functools.partial(gene_kernel, masks), shape((rank, width), bf16), [VMEM] * len(pieces)
    )(*pieces)

    def cell(k):
        return call(
            functools.partial(cell_kernel, k, start),
            shape((height, rank), f32 if k == 0 else i16),
            [VMEM] * (2 + len(totals[-1:])),
        )(dense, gene, *totals[-1:])

    came = [to_gene(cell(k), k) for k in reversed(range(1, n_genes))]
    out = cell(0)
    for x in came:
        out = call(more_kernel, shape((height, rank), f32), [VMEM, VMEM], nbytes=16 * MIB)(out, x)
    return out


def solution(mesh):
    in_specs = (
        P("cells", None),
        P(("cells", "genes"), None, None),
        P(("cells", "genes")),
        P(("cells", "genes")),
        P(("cells", "genes")),
    )
    out_specs = P(("cells", "genes"), None)
    body = functools.partial(local, mesh.shape["cells"], mesh.shape["genes"])
    return jax.shard_map(body, mesh=mesh, in_specs=in_specs, out_specs=out_specs, check_vma=False)
```

```python
import functools

import jax
import jax.numpy as jnp
from jax import lax
from jax.experimental import pallas as pl
from jax.experimental.pallas import tpu as pltpu
from jax.sharding import PartitionSpec as P

GENE_BLOCKS = 16
CORES = 2
LANES = 128
PARTS = (3, 3, 2)
MIB = 1 << 20

VMEM = pl.BlockSpec(memory_space=pltpu.VMEM)
SMEM = pl.BlockSpec(memory_space=pltpu.SMEM)
HBM = pl.BlockSpec(memory_space=pltpu.HBM)
f32, bf16, i16, i32 = jnp.float32, jnp.bfloat16, jnp.int16, jnp.int32


def encode(x, out, at=()):
    peak = jnp.max(jnp.abs(x), axis=0, keepdims=True)
    expo = jnp.ceil(jnp.log2(jnp.maximum(peak, 2.0**-100)))
    expo = jnp.clip(expo, -100.0, 126.0)
    code = jnp.round(x * jnp.exp2(14.0 - expo)).astype(i32)
    top = code[:16]
    row = lax.broadcasted_iota(i32, top.shape, 0)
    word = jnp.broadcast_to(expo.astype(i32) + 128, top.shape)
    marked = (top & ~1) | ((word >> jnp.minimum(row, 7)) & 1)
    top = jnp.where(row < 8, marked, top)
    out[at + (pl.ds(0, 16),)] = top.astype(i16)
    out[at + (pl.ds(16, x.shape[0] - 16),)] = code[16:].astype(i16)


def decode(code):
    code = code.astype(i32)
    head = code[:8]
    row = lax.broadcasted_iota(i32, head.shape, 0)
    word = jnp.sum((head & 1) << row, axis=0, keepdims=True)
    scale = jnp.exp2((word - (128 + 14)).astype(f32))
    return code.astype(f32) * scale


def core_and_chip():
    place = lax.axis_index("cells")
    return lax.rem(place, CORES), lax.div(place, CORES)


def call(body, outs, in_specs, scratch=(), mib=32, nbytes=0):
    return pl.pallas_call(
        body,
        out_shape=outs,
        in_specs=in_specs,
        out_specs=jax.tree.map(lambda _: VMEM, outs),
        scratch_shapes=list(scratch),
        compiler_params=pltpu.CompilerParams(vmem_limit_bytes=mib * MIB),
        cost_estimate=pl.CostEstimate(flops=0, bytes_accessed=nbytes, transcendentals=0),
    )


def block(index, size):
    return pl.ds(pl.multiple_of(index * size, size), size)


def dense_kernel(count, rows, cols, sketch, tiles, dense, turned, *refs):
    *outs, place, sketch_here, load_sems, sems = refs
    tile = tiles.shape[1]
    rows_place, cols_place = place
    loads = [
        pltpu.make_async_copy(src, dst, load_sems.at[i])
        for i, (src, dst) in enumerate(((rows, rows_place), (cols, cols_place), (sketch, sketch_here)))
    ]
    for load in loads:
        load.start()

    def clear(i, _):
        dense[block(i, 16), :] = jnp.zeros((16, dense.shape[1]), bf16)
        return 0

    lax.fori_loop(0, dense.shape[0] // 16, clear, 0)
    for load in loads[:2]:
        load.wait()

    def copy(s):
        to = dense.at[block(rows_place[s], tile), block(cols_place[s], tile)]
        return pltpu.make_async_copy(tiles.at[s], to, sems.at[s])

    def start(s, _):
        copy(s).start()
        return 0

    def wait(s, _):
        copy(s).wait()
        return 0

    lax.fori_loop(0, count[0], start, 0)
    loads[2].wait()
    turned[...] = sketch_here[...].T
    lax.fori_loop(0, count[0], wait, 0)
    start = 0
    for out in outs:
        half_kernel(1, start, turned, dense, out)
        start += out.shape[1]


def half_kernel(other, start, turned, dense, out):
    core, _ = core_and_chip()
    rows, width = out.shape
    left = turned[block(core ^ other, rows), :]
    step = 512 if width % 512 == 0 else 256
    for j in range(0, width, step):
        part = jnp.dot(left, dense[:, start + j : start + j + step], preferred_element_type=f32)
        if other:
            encode(part, out.at[:, j : j + step])
        else:
            out[:, j : j + step] = part


def add_kernel(bit, mine, got, *outs):
    _, chip = core_and_chip()
    start = 0
    for keep, send in zip(outs[::2], outs[1::2]):
        width = keep.shape[1]
        ours = (chip >> bit) & 1
        cut = pl.ds(pl.multiple_of(start + (1 - ours) * width, width), width)
        encode(mine[:, cut] + decode(got[:, cut]), send)
        cut = pl.ds(pl.multiple_of(start + ours * width, width), width)
        keep[...] = mine[:, cut] + decode(got[:, cut])
        start += 2 * width


def code_kernel(mine, got, *outs):
    start = 0
    for out in outs:
        cut = slice(start, start + out.shape[1])
        encode(mine[:, cut] + decode(got[:, cut]), out)
        start += out.shape[1]


def cast_kernel(code, got, out):
    out[...] = (decode(code[...]) + decode(got[...])).astype(bf16)


def join(masks, pieces, gene):
    core, chip = core_and_chip()
    rows, width = pieces[0].shape
    for k, mask in enumerate(masks):
        place, size = 0, gene.shape[1]
        for bit in range(len(masks).bit_length() - 1):
            size //= 2
            place = place + (((chip ^ mask) >> bit) & 1) * size
        cut = pl.ds(pl.multiple_of(place, width), width)
        gene[block(core, rows), cut] = pieces[k][...]
        gene[block(1 - core, rows), cut] = pieces[len(masks) + k][...]


def gene_kernel(masks, *refs):
    join(masks, refs[:-1], refs[-1])


def product(left, gene):
    return lax.dot_general(left, gene, (((1,), (1,)), ((), ())), preferred_element_type=f32)


def part_kernel(masks, start, fresh, dense, *refs):
    *pieces, out, gene = refs
    if not fresh:
        before, *pieces = pieces
    join(masks, pieces, gene)
    step = 256
    for i in range(0, out.shape[0], step):
        part = product(dense[i : i + step, start : start + gene.shape[1]], gene[...])
        out[i : i + step, :] = part if fresh else before[i : i + step, :] + part


def cell_kernel(k, start, dense, gene, *refs):
    *before, out = refs
    cut = block(lax.axis_index("genes") ^ k, out.shape[0])
    part = product(dense[cut, start : start + gene.shape[1]], gene[...])
    if before:
        part = part + before[0][cut, :]
    if k == 0:
        out[...] = part
    else:
        encode(part, out)


def more_kernel(total, got, out):
    out[...] = total[...] + decode(got[...])


def cuts_of(genes, bits):
    for parts in (PARTS, (1, 1)):
        unit = genes // sum(parts)
        if unit >> max(bits - 1, 0) >= LANES:
            ends = [sum(parts[:i]) * unit for i in range(len(parts))]
            return tuple((at, p * unit) for at, p in zip(ends, parts))
    return ((0, genes),)


def local(n_cells, n_genes, sketch, tiles, tile_rows, tile_cols, tile_counts):
    cells, rank = sketch.shape
    slots, tile, _ = tiles.shape
    genes = GENE_BLOCKS * tile
    bits = (n_cells // CORES).bit_length() - 1
    rows = rank // CORES
    height = cells // n_genes
    shape = jax.ShapeDtypeStruct
    cuts = cuts_of(genes, bits)

    def to_core(x):
        return lax.ppermute(x, "cells", [(i, i ^ 1) for i in range(n_cells)])

    def to_chip(x, bit):
        return lax.ppermute(x, "cells", [(i, i ^ (CORES << bit)) for i in range(n_cells)])

    def to_gene(x, k):
        return lax.ppermute(x, "genes", [(i, i ^ k) for i in range(n_genes)])

    widths = [width for _, width in cuts]
    first, rest = widths[0], genes - widths[0]
    dense, turned, *theirs = call(
        dense_kernel,
        (shape((cells, genes), bf16), shape((rank, cells), bf16))
        + tuple(shape((rows, width), i16) for width in (first, rest) if width),
        [SMEM] + [HBM] * 4,
        scratch=[
            (pltpu.SMEM((slots,), i32), pltpu.SMEM((slots,), i32)),
            pltpu.VMEM((cells, rank), bf16),
            pltpu.SemaphoreType.DMA((3,)),
            pltpu.SemaphoreType.DMA((slots,)),
        ],
    )(tile_counts, *(pltpu.with_memory_space_constraint(x, pltpu.HBM) for x in (tile_rows, tile_cols, sketch, tiles)))

    def half_of(other, start, turned, width):
        body = functools.partial(half_kernel, other, start)
        return call(body, shape((rows, width), i16 if other else f32), [VMEM, VMEM])(turned, dense)

    def after(x, *others):
        return lax.optimization_barrier((x, *others))[0]

    def add_step(bit, kept, came, widths):
        if bit < bits - 1:
            outs = [shape((rows, width // 2), kind) for width in widths for kind in (f32, i16)]
            done = call(functools.partial(add_kernel, bit), tuple(outs), [VMEM, VMEM])(kept, came)
            return [done[i : i + 2] for i in range(0, len(done), 2)]
        done = call(code_kernel, tuple(shape((rows, width), i16) for width in widths), [VMEM, VMEM])(kept, came)
        return [done[i : i + 1] for i in range(len(done))]

    def by_halving(sums):
        widths = [sum_[0].shape[1] for sum_ in sums]
        for bit in range(bits - 1):
            came = [to_chip(code, bit) for _, code in sums]
            done = []
            for (kept, _), x, width in zip(sums, came, widths):
                done += add_step(bit + 1, kept, after(x, *done[-1]) if done else x, [width])
            sums = done
            widths = [width // 2 for width in widths]
        held = []
        for (code,) in sums:
            came = to_chip(code, bits - 1)
            came = after(came, *held[-1]) if held else came
            held.append([call(cast_kernel, shape(code.shape, bf16), [VMEM, VMEM])(code, came)])
        masks = [0]
        for bit in reversed(range(bits - 1)):
            before = None
            for pieces in held:
                came = [to_chip(x, bit) for x in pieces]
                if before is not None:
                    came = [after(x, before) for x in came]
                pieces += came
                before = came[-1]
            masks += [mask ^ (1 << bit) for mask in masks]
        return masks, held

    got = [to_core(x) for x in theirs]
    sums = add_step(0, half_of(0, 0, turned, first), got[0], widths[:1])
    if rest:
        sums += add_step(0, half_of(0, first, after(turned, *sums[0]), rest), got[1], widths[1:])
    masks, sides = by_halving(sums)
    totals = []
    for i, ((start, width), pieces) in enumerate(zip(cuts, sides)):
        if i >= 2:
            pieces = [after(x, totals[i - 2]) for x in pieces]
        pieces = pieces + [to_core(x) for x in pieces]
        if i == len(cuts) - 1:
            break
        before = totals[-1:]
        totals.append(
            call(
                functools.partial(part_kernel, masks, start, not before),
                shape((cells, rank), f32),
                [VMEM] * (1 + len(before) + len(pieces)),
                scratch=[pltpu.VMEM((rank, width), bf16)],
            )(dense, *before, *pieces)
        )
    gene = call(
        functools.partial(gene_kernel, masks), shape((rank, width), bf16), [VMEM] * len(pieces)
    )(*pieces)

    def cell(k):
        return call(
            functools.partial(cell_kernel, k, start),
            shape((height, rank), f32 if k == 0 else i16),
            [VMEM] * (2 + len(totals[-1:])),
        )(dense, gene, *totals[-1:])

    came = [to_gene(cell(k), k) for k in reversed(range(1, n_genes))]
    out = cell(0)
    for x in came:
        out = call(more_kernel, shape((height, rank), f32), [VMEM, VMEM], nbytes=16 * MIB)(out, x)
    return out


def solution(mesh):
    in_specs = (
        P("cells", None),
        P(("cells", "genes"), None, None),
        P(("cells", "genes")),
        P(("cells", "genes")),
        P(("cells", "genes")),
    )
    out_specs = P(("cells", "genes"), None)
    body = functools.partial(local, mesh.shape["cells"], mesh.shape["genes"])
    return jax.shard_map(body, mesh=mesh, in_specs=in_specs, out_specs=out_specs, check_vma=False)
```

```python
import functools

import jax
import jax.numpy as jnp
from jax import lax
from jax.experimental import pallas as pl
from jax.experimental.pallas import tpu as pltpu
from jax.sharding import PartitionSpec as P

GENE_BLOCKS = 16
CORES = 2
LANES = 128
PARTS = (3, 5)
MIB = 1 << 20

VMEM = pl.BlockSpec(memory_space=pltpu.VMEM)
SMEM = pl.BlockSpec(memory_space=pltpu.SMEM)
HBM = pl.BlockSpec(memory_space=pltpu.HBM)
f32, bf16, i16, i32 = jnp.float32, jnp.bfloat16, jnp.int16, jnp.int32


def encode(x, out, at=()):
    peak = jnp.max(jnp.abs(x), axis=0, keepdims=True)
    expo = jnp.ceil(jnp.log2(jnp.maximum(peak, 2.0**-100)))
    expo = jnp.clip(expo, -100.0, 126.0)
    code = jnp.round(x * jnp.exp2(14.0 - expo)).astype(i32)
    top = code[:16]
    row = lax.broadcasted_iota(i32, top.shape, 0)
    word = jnp.broadcast_to(expo.astype(i32) + 128, top.shape)
    marked = (top & ~1) | ((word >> jnp.minimum(row, 7)) & 1)
    top = jnp.where(row < 8, marked, top)
    out[at + (pl.ds(0, 16),)] = top.astype(i16)
    out[at + (pl.ds(16, x.shape[0] - 16),)] = code[16:].astype(i16)


def decode(code):
    code = code.astype(i32)
    head = code[:8]
    row = lax.broadcasted_iota(i32, head.shape, 0)
    word = jnp.sum((head & 1) << row, axis=0, keepdims=True)
    scale = jnp.exp2((word - (128 + 14)).astype(f32))
    return code.astype(f32) * scale


def core_and_chip():
    place = lax.axis_index("cells")
    return lax.rem(place, CORES), lax.div(place, CORES)


def call(body, outs, in_specs, scratch=(), mib=32, nbytes=0):
    return pl.pallas_call(
        body,
        out_shape=outs,
        in_specs=in_specs,
        out_specs=jax.tree.map(lambda _: VMEM, outs),
        scratch_shapes=list(scratch),
        compiler_params=pltpu.CompilerParams(vmem_limit_bytes=mib * MIB),
        cost_estimate=pl.CostEstimate(flops=0, bytes_accessed=nbytes, transcendentals=0),
    )


def block(index, size):
    return pl.ds(pl.multiple_of(index * size, size), size)


def dense_kernel(count, rows, cols, sketch, tiles, dense, turned, *refs):
    *outs, place, sketch_here, load_sems, sems = refs
    tile = tiles.shape[1]
    rows_place, cols_place = place
    loads = [
        pltpu.make_async_copy(src, dst, load_sems.at[i])
        for i, (src, dst) in enumerate(((rows, rows_place), (cols, cols_place), (sketch, sketch_here)))
    ]
    for load in loads:
        load.start()

    def clear(i, _):
        dense[block(i, 16), :] = jnp.zeros((16, dense.shape[1]), bf16)
        return 0

    lax.fori_loop(0, dense.shape[0] // 16, clear, 0)
    for load in loads[:2]:
        load.wait()

    def copy(s):
        to = dense.at[block(rows_place[s], tile), block(cols_place[s], tile)]
        return pltpu.make_async_copy(tiles.at[s], to, sems.at[s])

    def start(s, _):
        copy(s).start()
        return 0

    def wait(s, _):
        copy(s).wait()
        return 0

    lax.fori_loop(0, count[0], start, 0)
    loads[2].wait()
    turned[...] = sketch_here[...].T
    lax.fori_loop(0, count[0], wait, 0)
    start = 0
    for out in outs:
        half_kernel(1, start, turned, dense, out)
        start += out.shape[1]


def half_kernel(other, start, turned, dense, out):
    core, _ = core_and_chip()
    rows, width = out.shape
    left = turned[block(core ^ other, rows), :]
    step = 512 if width % 512 == 0 else 256
    for j in range(0, width, step):
        part = jnp.dot(left, dense[:, start + j : start + j + step], preferred_element_type=f32)
        if other:
            encode(part, out.at[:, j : j + step])
        else:
            out[:, j : j + step] = part


def add_kernel(bit, mine, got, *outs):
    _, chip = core_and_chip()
    start = 0
    for keep, send in zip(outs[::2], outs[1::2]):
        width = keep.shape[1]
        ours = (chip >> bit) & 1
        cut = pl.ds(pl.multiple_of(start + (1 - ours) * width, width), width)
        encode(mine[:, cut] + decode(got[:, cut]), send)
        cut = pl.ds(pl.multiple_of(start + ours * width, width), width)
        keep[...] = mine[:, cut] + decode(got[:, cut])
        start += 2 * width


def code_kernel(mine, got, *outs):
    start = 0
    for out in outs:
        cut = slice(start, start + out.shape[1])
        encode(mine[:, cut] + decode(got[:, cut]), out)
        start += out.shape[1]


def again_kernel(code, got, out):
    encode(decode(code[...]) + decode(got[...]), out)


def cast_kernel(code, got, out):
    out[...] = (decode(code[...]) + decode(got[...])).astype(bf16)


def join(masks, pieces, gene):
    core, chip = core_and_chip()
    rows, width = pieces[0].shape
    for k, mask in enumerate(masks):
        place, size = 0, gene.shape[1]
        for bit in range(len(masks).bit_length() - 1):
            size //= 2
            place = place + (((chip ^ mask) >> bit) & 1) * size
        cut = pl.ds(pl.multiple_of(place, width), width)
        gene[block(core, rows), cut] = pieces[k][...]
        gene[block(1 - core, rows), cut] = pieces[len(masks) + k][...]


def gene_kernel(masks, *refs):
    join(masks, refs[:-1], refs[-1])


def product(left, gene):
    return lax.dot_general(left, gene, (((1,), (1,)), ((), ())), preferred_element_type=f32)


def part_kernel(masks, start, fresh, dense, *refs):
    *pieces, out, gene = refs
    if not fresh:
        before, *pieces = pieces
    join(masks, pieces, gene)
    step = 256
    for i in range(0, out.shape[0], step):
        part = product(dense[i : i + step, start : start + gene.shape[1]], gene[...])
        out[i : i + step, :] = part if fresh else before[i : i + step, :] + part


def cell_kernel(k, start, dense, gene, *refs):
    *before, out = refs
    cut = block(lax.axis_index("genes") ^ k, out.shape[0])
    part = product(dense[cut, start : start + gene.shape[1]], gene[...])
    if before:
        part = part + before[0][cut, :]
    if k == 0:
        out[...] = part
    else:
        encode(part, out)


def more_kernel(total, got, out):
    out[...] = total[...] + decode(got[...])


def cuts_of(genes, bits):
    for parts in (PARTS, (1, 1)):
        unit = genes // sum(parts)
        if unit * parts[1] % (LANES << max(bits - 1, 0)) == 0:
            return ((0, parts[0] * unit), (parts[0] * unit, parts[1] * unit))
    return ((0, genes),)


def local(n_cells, n_genes, sketch, tiles, tile_rows, tile_cols, tile_counts):
    cells, rank = sketch.shape
    slots, tile, _ = tiles.shape
    genes = GENE_BLOCKS * tile
    bits = (n_cells // CORES).bit_length() - 1
    rows = rank // CORES
    height = cells // n_genes
    shape = jax.ShapeDtypeStruct
    cuts = cuts_of(genes, bits)

    def to_core(x):
        return lax.ppermute(x, "cells", [(i, i ^ 1) for i in range(n_cells)])

    def to_chip(x, bit):
        return lax.ppermute(x, "cells", [(i, i ^ (CORES << bit)) for i in range(n_cells)])

    def to_gene(x, k):
        return lax.ppermute(x, "genes", [(i, i ^ k) for i in range(n_genes)])

    widths = [width for _, width in cuts]
    first, rest = widths[0], genes - widths[0]
    dense, turned, *theirs = call(
        dense_kernel,
        (shape((cells, genes), bf16), shape((rank, cells), bf16))
        + tuple(shape((rows, width), i16) for width in (first, rest) if width),
        [SMEM] + [HBM] * 4,
        scratch=[
            (pltpu.SMEM((slots,), i32), pltpu.SMEM((slots,), i32)),
            pltpu.VMEM((cells, rank), bf16),
            pltpu.SemaphoreType.DMA((3,)),
            pltpu.SemaphoreType.DMA((slots,)),
        ],
    )(tile_counts, *(pltpu.with_memory_space_constraint(x, pltpu.HBM) for x in (tile_rows, tile_cols, sketch, tiles)))

    def half_of(other, start, turned, width):
        body = functools.partial(half_kernel, other, start)
        return call(body, shape((rows, width), i16 if other else f32), [VMEM, VMEM])(turned, dense)

    def after(x, *others):
        return lax.optimization_barrier((x, *others))[0]

    def add_step(bit, kept, came, widths):
        if bit < bits - 1:
            outs = [shape((rows, width // 2), kind) for width in widths for kind in (f32, i16)]
            done = call(functools.partial(add_kernel, bit), tuple(outs), [VMEM, VMEM])(kept, came)
            return [done[i : i + 2] for i in range(0, len(done), 2)]
        done = call(code_kernel, tuple(shape((rows, width), i16) for width in widths), [VMEM, VMEM])(kept, came)
        return [done[i : i + 1] for i in range(len(done))]

    def by_halving(sums):
        widths = [sum_[0].shape[1] for sum_ in sums]
        for bit in range(bits - 1):
            came = [to_chip(code, bit) for _, code in sums]
            done = []
            for (kept, _), x, width in zip(sums, came, widths):
                done += add_step(bit + 1, kept, after(x, *done[-1]) if done else x, [width])
            sums = done
            widths = [width // 2 for width in widths]
        held = []
        for (code,) in sums:
            came = to_chip(code, bits - 1)
            came = after(came, *held[-1]) if held else came
            held.append([call(cast_kernel, shape(code.shape, bf16), [VMEM, VMEM])(code, came)])
        masks = [0]
        for bit in reversed(range(bits - 1)):
            before = None
            for pieces in held:
                came = [to_chip(x, bit) for x in pieces]
                if before is not None:
                    came = [after(x, before) for x in came]
                pieces += came
                before = came[-1]
            masks += [mask ^ (1 << bit) for mask in masks]
        return masks, held, code

    def by_doubling(code, *others):
        for bit in reversed(range(bits)):
            came = after(to_chip(code, bit), *others)
            others = ()
            body, kind = (again_kernel, i16) if bit else (cast_kernel, bf16)
            code = call(body, shape(code.shape, kind), [VMEM, VMEM])(code, came)
        return [code]

    got = [to_core(x) for x in theirs]
    mine = half_of(0, 0, turned, first)
    if rest:
        (code,) = call(code_kernel, (shape((rows, first), i16),), [VMEM, VMEM])(mine, got[0])
        sums = add_step(0, half_of(0, first, after(turned, code), rest), got[1], [rest])
        masks, sides, *crossing = by_halving(sums)
        sides = [by_doubling(code, *crossing)] + sides
        masks = [[0], masks]
    else:
        masks, sides, _ = by_halving(add_step(0, mine, got[0], [first]))
        masks = [masks]
    totals = []
    for i, ((start, width), pieces) in enumerate(zip(cuts, sides)):
        pieces = pieces + [to_core(x) for x in pieces]
        if i == len(cuts) - 1:
            break
        before = totals[-1:]
        totals.append(
            call(
                functools.partial(part_kernel, masks[i], start, not before),
                shape((cells, rank), f32),
                [VMEM] * (1 + len(before) + len(pieces)),
                scratch=[pltpu.VMEM((rank, width), bf16)],
            )(dense, *before, *pieces)
        )
    gene = call(
        functools.partial(gene_kernel, masks[-1]), shape((rank, width), bf16), [VMEM] * len(pieces)
    )(*pieces)

    def cell(k):
        return call(
            functools.partial(cell_kernel, k, start),
            shape((height, rank), f32 if k == 0 else i16),
            [VMEM] * (2 + len(totals[-1:])),
        )(dense, gene, *totals[-1:])

    came = [to_gene(cell(k), k) for k in reversed(range(1, n_genes))]
    out = cell(0)
    for x in came:
        out = call(more_kernel, shape((height, rank), f32), [VMEM, VMEM], nbytes=16 * MIB)(out, x)
    return out


def solution(mesh):
    in_specs = (
        P("cells", None),
        P(("cells", "genes"), None, None),
        P(("cells", "genes")),
        P(("cells", "genes")),
        P(("cells", "genes")),
    )
    out_specs = P(("cells", "genes"), None)
    body = functools.partial(local, mesh.shape["cells"], mesh.shape["genes"])
    return jax.shard_map(body, mesh=mesh, in_specs=in_specs, out_specs=out_specs, check_vma=False)
```

```python
import functools

import jax
import jax.numpy as jnp
from jax import lax
from jax.experimental import pallas as pl
from jax.experimental.pallas import tpu as pltpu
from jax.sharding import PartitionSpec as P

GENE_BLOCKS = 16
CORES = 2
LANES = 128
PARTS = (1, 1, 1, 1)
MIB = 1 << 20

VMEM = pl.BlockSpec(memory_space=pltpu.VMEM)
SMEM = pl.BlockSpec(memory_space=pltpu.SMEM)
HBM = pl.BlockSpec(memory_space=pltpu.HBM)
f32, bf16, i16, i32 = jnp.float32, jnp.bfloat16, jnp.int16, jnp.int32


def encode(x, out, at=()):
    peak = jnp.max(jnp.abs(x), axis=0, keepdims=True)
    expo = jnp.ceil(jnp.log2(jnp.maximum(peak, 2.0**-100)))
    expo = jnp.clip(expo, -100.0, 126.0)
    code = jnp.round(x * jnp.exp2(14.0 - expo)).astype(i32)
    top = code[:16]
    row = lax.broadcasted_iota(i32, top.shape, 0)
    word = jnp.broadcast_to(expo.astype(i32) + 128, top.shape)
    marked = (top & ~1) | ((word >> jnp.minimum(row, 7)) & 1)
    top = jnp.where(row < 8, marked, top)
    out[at + (pl.ds(0, 16),)] = top.astype(i16)
    out[at + (pl.ds(16, x.shape[0] - 16),)] = code[16:].astype(i16)


def decode(code):
    code = code.astype(i32)
    head = code[:8]
    row = lax.broadcasted_iota(i32, head.shape, 0)
    word = jnp.sum((head & 1) << row, axis=0, keepdims=True)
    scale = jnp.exp2((word - (128 + 14)).astype(f32))
    return code.astype(f32) * scale


def core_and_chip():
    place = lax.axis_index("cells")
    return lax.rem(place, CORES), lax.div(place, CORES)


def call(body, outs, in_specs, scratch=(), mib=32, nbytes=0):
    return pl.pallas_call(
        body,
        out_shape=outs,
        in_specs=in_specs,
        out_specs=jax.tree.map(lambda _: VMEM, outs),
        scratch_shapes=list(scratch),
        compiler_params=pltpu.CompilerParams(vmem_limit_bytes=mib * MIB),
        cost_estimate=pl.CostEstimate(flops=0, bytes_accessed=nbytes, transcendentals=0),
    )


def block(index, size):
    return pl.ds(pl.multiple_of(index * size, size), size)


def dense_kernel(count, rows, cols, sketch, tiles, dense, turned, *refs):
    *outs, place, sketch_here, load_sems, sems = refs
    tile = tiles.shape[1]
    rows_place, cols_place = place
    loads = [
        pltpu.make_async_copy(src, dst, load_sems.at[i])
        for i, (src, dst) in enumerate(((rows, rows_place), (cols, cols_place), (sketch, sketch_here)))
    ]
    for load in loads:
        load.start()

    def clear(i, _):
        dense[block(i, 16), :] = jnp.zeros((16, dense.shape[1]), bf16)
        return 0

    lax.fori_loop(0, dense.shape[0] // 16, clear, 0)
    for load in loads[:2]:
        load.wait()

    def copy(s):
        to = dense.at[block(rows_place[s], tile), block(cols_place[s], tile)]
        return pltpu.make_async_copy(tiles.at[s], to, sems.at[s])

    def start(s, _):
        copy(s).start()
        return 0

    def wait(s, _):
        copy(s).wait()
        return 0

    lax.fori_loop(0, count[0], start, 0)
    loads[2].wait()
    turned[...] = sketch_here[...].T
    lax.fori_loop(0, count[0], wait, 0)
    start = 0
    for out in outs:
        half_kernel(1, start, turned, dense, out)
        start += out.shape[1]


def half_kernel(other, start, turned, dense, out):
    core, _ = core_and_chip()
    rows, width = out.shape
    left = turned[block(core ^ other, rows), :]
    step = 512 if width % 512 == 0 else 256
    for j in range(0, width, step):
        part = jnp.dot(left, dense[:, start + j : start + j + step], preferred_element_type=f32)
        if other:
            encode(part, out.at[:, j : j + step])
        else:
            out[:, j : j + step] = part


def add_kernel(bit, mine, got, *outs):
    _, chip = core_and_chip()
    start = 0
    for keep, send in zip(outs[::2], outs[1::2]):
        width = keep.shape[1]
        ours = (chip >> bit) & 1
        cut = pl.ds(pl.multiple_of(start + (1 - ours) * width, width), width)
        encode(mine[:, cut] + decode(got[:, cut]), send)
        cut = pl.ds(pl.multiple_of(start + ours * width, width), width)
        keep[...] = mine[:, cut] + decode(got[:, cut])
        start += 2 * width


def code_kernel(mine, got, *outs):
    start = 0
    for out in outs:
        cut = slice(start, start + out.shape[1])
        encode(mine[:, cut] + decode(got[:, cut]), out)
        start += out.shape[1]


def cast_kernel(code, got, out):
    out[...] = (decode(code[...]) + decode(got[...])).astype(bf16)


def join(masks, pieces, gene):
    core, chip = core_and_chip()
    rows, width = pieces[0].shape
    for k, mask in enumerate(masks):
        place, size = 0, gene.shape[1]
        for bit in range(len(masks).bit_length() - 1):
            size //= 2
            place = place + (((chip ^ mask) >> bit) & 1) * size
        cut = pl.ds(pl.multiple_of(place, width), width)
        gene[block(core, rows), cut] = pieces[k][...]
        gene[block(1 - core, rows), cut] = pieces[len(masks) + k][...]


def gene_kernel(masks, *refs):
    join(masks, refs[:-1], refs[-1])


def product(left, gene):
    return lax.dot_general(left, gene, (((1,), (1,)), ((), ())), preferred_element_type=f32)


def part_kernel(masks, start, fresh, dense, *refs):
    *pieces, out, gene = refs
    if not fresh:
        before, *pieces = pieces
    join(masks, pieces, gene)
    step = 256
    for i in range(0, out.shape[0], step):
        part = product(dense[i : i + step, start : start + gene.shape[1]], gene[...])
        out[i : i + step, :] = part if fresh else before[i : i + step, :] + part


def cell_kernel(k, start, dense, gene, *refs):
    *before, out = refs
    cut = block(lax.axis_index("genes") ^ k, out.shape[0])
    part = product(dense[cut, start : start + gene.shape[1]], gene[...])
    if before:
        part = part + before[0][cut, :]
    if k == 0:
        out[...] = part
    else:
        encode(part, out)


def more_kernel(total, got, out):
    out[...] = total[...] + decode(got[...])


def cuts_of(genes, bits):
    for parts in (PARTS, (1, 1)):
        unit = genes // sum(parts)
        if unit >> max(bits - 1, 0) >= LANES:
            ends = [sum(parts[:i]) * unit for i in range(len(parts))]
            return tuple((at, p * unit) for at, p in zip(ends, parts))
    return ((0, genes),)


def local(n_cells, n_genes, sketch, tiles, tile_rows, tile_cols, tile_counts):
    cells, rank = sketch.shape
    slots, tile, _ = tiles.shape
    genes = GENE_BLOCKS * tile
    bits = (n_cells // CORES).bit_length() - 1
    rows = rank // CORES
    height = cells // n_genes
    shape = jax.ShapeDtypeStruct
    cuts = cuts_of(genes, bits)

    def to_core(x):
        return lax.ppermute(x, "cells", [(i, i ^ 1) for i in range(n_cells)])

    def to_chip(x, bit):
        return lax.ppermute(x, "cells", [(i, i ^ (CORES << bit)) for i in range(n_cells)])

    def to_gene(x, k):
        return lax.ppermute(x, "genes", [(i, i ^ k) for i in range(n_genes)])

    widths = [width for _, width in cuts]
    first, rest = widths[0], genes - widths[0]
    dense, turned, *theirs = call(
        dense_kernel,
        (shape((cells, genes), bf16), shape((rank, cells), bf16))
        + tuple(shape((rows, width), i16) for width in (first, rest) if width),
        [SMEM] + [HBM] * 4,
        scratch=[
            (pltpu.SMEM((slots,), i32), pltpu.SMEM((slots,), i32)),
            pltpu.VMEM((cells, rank), bf16),
            pltpu.SemaphoreType.DMA((3,)),
            pltpu.SemaphoreType.DMA((slots,)),
        ],
    )(tile_counts, *(pltpu.with_memory_space_constraint(x, pltpu.HBM) for x in (tile_rows, tile_cols, sketch, tiles)))

    def half_of(other, start, turned, width):
        body = functools.partial(half_kernel, other, start)
        return call(body, shape((rows, width), i16 if other else f32), [VMEM, VMEM])(turned, dense)

    def after(x, *others):
        return lax.optimization_barrier((x, *others))[0]

    def add_step(bit, kept, came, widths):
        if bit < bits - 1:
            outs = [shape((rows, width // 2), kind) for width in widths for kind in (f32, i16)]
            done = call(functools.partial(add_kernel, bit), tuple(outs), [VMEM, VMEM])(kept, came)
            return [done[i : i + 2] for i in range(0, len(done), 2)]
        done = call(code_kernel, tuple(shape((rows, width), i16) for width in widths), [VMEM, VMEM])(kept, came)
        return [done[i : i + 1] for i in range(len(done))]

    def by_halving(sums):
        widths = [sum_[0].shape[1] for sum_ in sums]
        for bit in range(bits - 1):
            came = [to_chip(code, bit) for _, code in sums]
            done = []
            for (kept, _), x, width in zip(sums, came, widths):
                done += add_step(bit + 1, kept, after(x, *done[-1]) if done else x, [width])
            sums = done
            widths = [width // 2 for width in widths]
        held = []
        for (code,) in sums:
            came = to_chip(code, bits - 1)
            came = after(came, *held[-1]) if held else came
            held.append([call(cast_kernel, shape(code.shape, bf16), [VMEM, VMEM])(code, came)])
        masks = [0]
        for bit in reversed(range(bits - 1)):
            before = None
            for pieces in held:
                came = [to_chip(x, bit) for x in pieces]
                if before is not None:
                    came = [after(x, before) for x in came]
                pieces += came
                before = came[-1]
            masks += [mask ^ (1 << bit) for mask in masks]
        return masks, held

    got = [to_core(x) for x in theirs]
    sums = add_step(0, half_of(0, 0, turned, first), got[0], widths[:1])
    if rest:
        sums += add_step(0, half_of(0, first, after(turned, *sums[0]), rest), got[1], widths[1:])
    masks, sides = by_halving(sums)
    totals = []
    for i, ((start, width), pieces) in enumerate(zip(cuts, sides)):
        if i >= 2:
            pieces = [after(x, totals[i - 2]) for x in pieces]
        pieces = pieces + [to_core(x) for x in pieces]
        if i == len(cuts) - 1:
            break
        before = totals[-1:]
        totals.append(
            call(
                functools.partial(part_kernel, masks, start, not before),
                shape((cells, rank), f32),
                [VMEM] * (1 + len(before) + len(pieces)),
                scratch=[pltpu.VMEM((rank, width), bf16)],
            )(dense, *before, *pieces)
        )
    gene = call(
        functools.partial(gene_kernel, masks), shape((rank, width), bf16), [VMEM] * len(pieces)
    )(*pieces)

    def cell(k):
        return call(
            functools.partial(cell_kernel, k, start),
            shape((height, rank), f32 if k == 0 else i16),
            [VMEM] * (2 + len(totals[-1:])),
        )(dense, gene, *totals[-1:])

    came = [to_gene(cell(k), k) for k in reversed(range(1, n_genes))]
    out = cell(0)
    for x in came:
        out = call(more_kernel, shape((height, rank), f32), [VMEM, VMEM], nbytes=16 * MIB)(out, x)
    return out


def solution(mesh):
    in_specs = (
        P("cells", None),
        P(("cells", "genes"), None, None),
        P(("cells", "genes")),
        P(("cells", "genes")),
        P(("cells", "genes")),
    )
    out_specs = P(("cells", "genes"), None)
    body = functools.partial(local, mesh.shape["cells"], mesh.shape["genes"])
    return jax.shard_map(body, mesh=mesh, in_specs=in_specs, out_specs=out_specs, check_vma=False)
```

```python
import functools

import jax
import jax.numpy as jnp
from jax import lax
from jax.experimental import pallas as pl
from jax.experimental.pallas import tpu as pltpu
from jax.sharding import PartitionSpec as P

GENE_BLOCKS = 16
CORES = 2
STREAMS = 2
MIB = 1 << 20

VMEM = pl.BlockSpec(memory_space=pltpu.VMEM)
SMEM = pl.BlockSpec(memory_space=pltpu.SMEM)
HBM = pl.BlockSpec(memory_space=pltpu.HBM)
f32, bf16, i16, i32 = jnp.float32, jnp.bfloat16, jnp.int16, jnp.int32


def encode(x, out, at=()):
    peak = jnp.max(jnp.abs(x), axis=0, keepdims=True)
    expo = jnp.ceil(jnp.log2(jnp.maximum(peak, 2.0**-100)))
    expo = jnp.clip(expo, -100.0, 126.0)
    code = jnp.round(x * jnp.exp2(14.0 - expo)).astype(i32)
    top = code[:16]
    row = lax.broadcasted_iota(i32, top.shape, 0)
    word = jnp.broadcast_to(expo.astype(i32) + 128, top.shape)
    marked = (top & ~1) | ((word >> jnp.minimum(row, 7)) & 1)
    top = jnp.where(row < 8, marked, top)
    out[at + (pl.ds(0, 16),)] = top.astype(i16)
    out[at + (pl.ds(16, x.shape[0] - 16),)] = code[16:].astype(i16)


def decode(code):
    code = code.astype(i32)
    head = code[:8]
    row = lax.broadcasted_iota(i32, head.shape, 0)
    word = jnp.sum((head & 1) << row, axis=0, keepdims=True)
    scale = jnp.exp2((word - (128 + 14)).astype(f32))
    return code.astype(f32) * scale


def core_and_chip():
    place = lax.axis_index("cells")
    return lax.rem(place, CORES), lax.div(place, CORES)


def call(body, outs, in_specs, scratch=(), mib=32, flops=0, nbytes=0):
    return pl.pallas_call(
        body,
        out_shape=outs,
        in_specs=in_specs,
        out_specs=jax.tree.map(lambda _: VMEM, outs),
        scratch_shapes=list(scratch),
        compiler_params=pltpu.CompilerParams(vmem_limit_bytes=mib * MIB),
        cost_estimate=pl.CostEstimate(flops=flops, bytes_accessed=nbytes, transcendentals=0),
    )


def rows_of(turned, core, rows):
    span = rows * CORES
    at = [pl.multiple_of(i * span + core * rows, rows) for i in range(STREAMS)]
    return jnp.concatenate([turned[pl.ds(x, rows), :] for x in at], axis=0)


def dense_kernel(count, rows, cols, sketch, tiles, dense, turned, theirs, place, stage, sketch_here, load_sems, sems):
    slots, tile, _ = tiles.shape
    core, _ = core_and_chip()
    live = count[0]
    rows_place, cols_place = place
    groups = sems.shape[0]
    size = slots // groups
    loads = [
        pltpu.make_async_copy(src, dst, load_sems.at[i])
        for i, (src, dst) in enumerate(((rows, rows_place), (cols, cols_place), (sketch, sketch_here)))
    ]

    def group(i):
        cut = pl.ds(i * size, size)
        return pltpu.make_async_copy(tiles.at[cut], stage.at[cut], sems.at[i])

    for load in loads:
        load.start()
    for i in range(groups):
        pl.when(live > i * size)(lambda i=i: group(i).start())

    def clear(i, _):
        dense[pl.ds(pl.multiple_of(i * 16, 16), 16), :] = jnp.zeros((16, dense.shape[1]), bf16)
        return 0

    lax.fori_loop(0, dense.shape[0] // 16, clear, 0)
    loads[2].wait()
    turned[...] = sketch_here[...].T
    for load in loads[:2]:
        load.wait()

    def put(s):
        r = pl.multiple_of(rows_place[s] * tile, tile)
        c = pl.multiple_of(cols_place[s] * tile, tile)
        dense[pl.ds(r, tile), pl.ds(c, tile)] = stage[s]

    def put_one(s, _):
        put(s)
        return 0

    for i in range(groups):

        @pl.when(live > i * size)
        def _(i=i):
            group(i).wait()

            @pl.when(live >= (i + 1) * size)
            def _():
                for s in range(i * size, (i + 1) * size):
                    put(s)

            @pl.when(live < (i + 1) * size)
            def _():
                lax.fori_loop(i * size, live, put_one, 0)

    left = rows_of(turned, 1 - core, theirs.shape[0] // STREAMS)
    width = 512
    for j in range(dense.shape[1] // width):
        cut = pl.ds(j * width, width)
        encode(jnp.dot(left, dense[:, cut], preferred_element_type=f32), theirs.at[:, cut])


def own_kernel(turned, dense, mine):
    core, _ = core_and_chip()
    left = rows_of(turned, core, mine.shape[0] // STREAMS)
    mine[...] = jnp.dot(left, dense[...], preferred_element_type=f32)


def halve(total, bit, keep, send):
    _, chip = core_and_chip()
    width = keep.shape[1]
    ours = (chip >> bit) & 1
    low, high = total[:, :width], total[:, width:]
    keep[...] = jnp.where(ours == 0, low, high)
    encode(jnp.where(ours == 0, high, low), send)


def pair_kernel(chips, mine, got, *refs):
    *outs, total = refs
    direct, rest = outs[:chips], outs[chips:]
    _, chip = core_and_chip()
    total[...] = mine[...] + decode(got[...])
    rows, width = direct[0].shape
    if len(rest) == 2:
        halve(total[rows:, :], 0, *rest)
    else:
        encode(total[rows:, :], rest[0])
    for k, out in enumerate(direct):
        part = total[:rows, pl.ds(pl.multiple_of((chip ^ k) * width, width), width)]
        if k == 0:
            out[...] = part
        else:
            encode(part, out)


def add_kernel(bit, keep, got, *outs):
    total = keep[...] + decode(got[...])
    if len(outs) == 2:
        halve(total, bit, *outs)
    else:
        encode(total, outs[0])


def cast_kernel(code, got, out):
    out[...] = (decode(code[...]) + decode(got[...])).astype(bf16)


def direct_cast_kernel(own, *refs):
    *got, out = refs
    total = own[...]
    for ref in got:
        total = total + decode(ref[...])
    out[...] = total.astype(bf16)


def join_kernel(*refs):
    *pieces, out = refs
    _, chip = core_and_chip()
    width = pieces[0].shape[1]
    for k, piece in enumerate(pieces):
        out[:, pl.ds(pl.multiple_of((chip ^ k) * width, width), width)] = piece[...]


def gene_kernel(masks, first, first_theirs, *refs):
    *pieces, gene = refs
    core, chip = core_and_chip()
    rows, width = pieces[0].shape

    def at(stream, owner):
        return pl.ds(pl.multiple_of((stream * CORES + owner) * rows, rows), rows)

    gene[at(0, core), :] = first[...]
    gene[at(0, 1 - core), :] = first_theirs[...]
    for k, mask in enumerate(masks):
        place, size = 0, gene.shape[1]
        for bit in range(len(masks).bit_length() - 1):
            size //= 2
            place = place + (((chip ^ mask) >> bit) & 1) * size
        cut = pl.ds(pl.multiple_of(place, width), width)
        gene[at(1, core), cut] = pieces[k][...]
        gene[at(1, 1 - core), cut] = pieces[len(masks) + k][...]


def cell_kernel(k, dense, gene, out):
    height = out.shape[0]
    me = lax.axis_index("genes")
    left = dense[pl.ds(pl.multiple_of((me ^ k) * height, height), height), :]
    part = lax.dot_general(left, gene[...], (((1,), (1,)), ((), ())), preferred_element_type=f32)
    if k == 0:
        out[...] = part
    else:
        encode(part, out)


def more_kernel(total, got, out):
    out[...] = total[...] + decode(got[...])


def local(n_cells, n_genes, sketch, tiles, tile_rows, tile_cols, tile_counts):
    cells, rank = sketch.shape
    slots, tile, _ = tiles.shape
    genes = GENE_BLOCKS * tile
    bits = (n_cells // CORES).bit_length() - 1
    span = rank // STREAMS
    rows = span // CORES
    share = rows * STREAMS
    height = cells // n_genes
    flops = 2 * cells * genes * rank
    shape = jax.ShapeDtypeStruct

    def to_core(x):
        return lax.ppermute(x, "cells", [(i, i ^ 1) for i in range(n_cells)])

    def to_chip(x, k):
        return lax.ppermute(x, "cells", [(i, i ^ (CORES * k)) for i in range(n_cells)])

    def to_gene(x, k):
        return lax.ppermute(x, "genes", [(i, i ^ k) for i in range(n_genes)])

    def halves(width):
        return shape((rows, width // 2), f32), shape((rows, width // 2), i16)

    dense, turned, theirs = call(
        dense_kernel,
        (shape((cells, genes), bf16), shape((rank, cells), bf16), shape((share, genes), i16)),
        [SMEM] + [HBM] * 4,
        scratch=[
            (pltpu.SMEM((slots,), i32), pltpu.SMEM((slots,), i32)),
            pltpu.VMEM((slots, tile, tile), bf16),
            pltpu.VMEM((cells, rank), bf16),
            pltpu.SemaphoreType.DMA((3,)),
            pltpu.SemaphoreType.DMA((slots // 16 if slots % 16 == 0 else 1,)),
        ],
        flops=flops // 2,
        nbytes=8 * MIB,
    )(tile_counts, *(pltpu.with_memory_space_constraint(x, pltpu.HBM) for x in (tile_rows, tile_cols, sketch, tiles)))
    got = to_core(theirs)
    mine = call(own_kernel, shape((share, genes), f32), [VMEM, VMEM], flops=flops // 2, nbytes=5 * MIB)(turned, dense)
    chips = n_cells // CORES
    chunk = genes // chips
    one = halves(genes) if bits > 1 else (shape((rows, genes), i16),)
    pieces = call(
        functools.partial(pair_kernel, chips),
        (shape((rows, chunk), f32),) + (shape((rows, chunk), i16),) * (chips - 1) + one,
        [VMEM, VMEM],
        scratch=[pltpu.VMEM((share, genes), f32)],
        nbytes=3 * MIB,
    )(mine, got)
    direct, half = pieces[:chips], pieces[chips:]

    width = genes
    for bit in range(bits - 1):
        width //= 2
        outs = halves(width) if bit < bits - 2 else (shape((rows, width), i16),)
        half = call(functools.partial(add_kernel, bit + 1), outs, [VMEM, VMEM], nbytes=MIB)(
            half[0], to_chip(half[1], 1 << bit)
        )
    came = [to_chip(direct[k], k) for k in reversed(range(1, chips))]
    summed = call(direct_cast_kernel, shape((rows, chunk), bf16), [VMEM] * chips, nbytes=MIB)(direct[0], *came)
    crossed = to_chip(half[-1], chips // 2)
    spread = [to_chip(summed, k) for k in reversed(range(1, chips))][::-1]
    held = [call(cast_kernel, shape((rows, width), bf16), [VMEM, VMEM], nbytes=MIB)(half[-1], crossed)]
    *spread, _ = lax.optimization_barrier((*spread, held[0]))
    first = call(join_kernel, shape((rows, genes), bf16), [VMEM] * chips, nbytes=MIB)(summed, *spread)
    masks = [0]
    for bit in reversed(range(bits - 1)):
        held = held + [to_chip(x, 1 << bit) for x in held]
        masks += [mask ^ (1 << bit) for mask in masks]
    theirs = [to_core(x) for x in held]
    gene = call(
        functools.partial(gene_kernel, masks), shape((rank, genes), bf16), [VMEM] * (2 + 2 * len(held)), nbytes=2 * MIB
    )(first, to_core(first), *held, *theirs)

    def cell(k, gene):
        kind = f32 if k == 0 else i16
        return call(
            functools.partial(cell_kernel, k),
            shape((height, rank), kind),
            [VMEM, VMEM],
        )(dense, gene)

    got = []
    for k in reversed(range(1, n_genes)):
        got.append(to_gene(cell(k, gene), k))
    total = cell(0, gene)
    for x in got:
        total = call(more_kernel, shape((height, rank), f32), [VMEM, VMEM], nbytes=16 * MIB)(total, x)
    return total


def solution(mesh):
    in_specs = (
        P("cells", None),
        P(("cells", "genes"), None, None),
        P(("cells", "genes")),
        P(("cells", "genes")),
        P(("cells", "genes")),
    )
    out_specs = P(("cells", "genes"), None)
    body = functools.partial(local, mesh.shape["cells"], mesh.shape["genes"])
    return jax.shard_map(body, mesh=mesh, in_specs=in_specs, out_specs=out_specs, check_vma=False)
```

```python
import functools

import jax
import jax.numpy as jnp
from jax import lax
from jax.experimental import pallas as pl
from jax.experimental.pallas import tpu as pltpu
from jax.sharding import PartitionSpec as P

GENE_BLOCKS = 16
CORES = 2
DIRECT = (1, 2)
MIB = 1 << 20

VMEM = pl.BlockSpec(memory_space=pltpu.VMEM)
SMEM = pl.BlockSpec(memory_space=pltpu.SMEM)
HBM = pl.BlockSpec(memory_space=pltpu.HBM)
f32, bf16, i16, i32 = jnp.float32, jnp.bfloat16, jnp.int16, jnp.int32


def encode(x, out, at=()):
    peak = jnp.max(jnp.abs(x), axis=0, keepdims=True)
    expo = jnp.ceil(jnp.log2(jnp.maximum(peak, 2.0**-100)))
    expo = jnp.clip(expo, -100.0, 126.0)
    code = jnp.round(x * jnp.exp2(14.0 - expo)).astype(i32)
    top = code[:16]
    row = lax.broadcasted_iota(i32, top.shape, 0)
    word = jnp.broadcast_to(expo.astype(i32) + 128, top.shape)
    marked = (top & ~1) | ((word >> jnp.minimum(row, 7)) & 1)
    top = jnp.where(row < 8, marked, top)
    out[at + (pl.ds(0, 16),)] = top.astype(i16)
    out[at + (pl.ds(16, x.shape[0] - 16),)] = code[16:].astype(i16)


def scale_of(head):
    head = head.astype(i32)
    row = lax.broadcasted_iota(i32, head.shape, 0)
    word = jnp.sum((head & 1) << row, axis=0, keepdims=True)
    return jnp.exp2((word - (128 + 14)).astype(f32))


def decode(code):
    return code.astype(f32) * scale_of(code[:8])


def core_and_chip():
    place = lax.axis_index("cells")
    return lax.rem(place, CORES), lax.div(place, CORES)


def call(body, outs, in_specs, scratch=(), mib=32, flops=0, nbytes=0):
    return pl.pallas_call(
        body,
        out_shape=outs,
        in_specs=in_specs,
        out_specs=jax.tree.map(lambda _: VMEM, outs),
        scratch_shapes=list(scratch),
        compiler_params=pltpu.CompilerParams(vmem_limit_bytes=mib * MIB),
        cost_estimate=pl.CostEstimate(flops=flops, bytes_accessed=nbytes, transcendentals=0),
    )


def rows_of(turned, core, rows):
    return turned[pl.ds(pl.multiple_of(core * rows, rows), rows), :]


def dense_kernel(count, rows, cols, sketch, tiles, dense, turned, theirs, place, stage, sketch_here, load_sems, sems):
    slots, tile, _ = tiles.shape
    core, _ = core_and_chip()
    live = count[0]
    rows_place, cols_place = place
    groups = sems.shape[0]
    size = slots // groups
    loads = [
        pltpu.make_async_copy(src, dst, load_sems.at[i])
        for i, (src, dst) in enumerate(((rows, rows_place), (cols, cols_place), (sketch, sketch_here)))
    ]

    def group(i):
        cut = pl.ds(i * size, size)
        return pltpu.make_async_copy(tiles.at[cut], stage.at[cut], sems.at[i])

    for load in loads:
        load.start()
    for i in range(groups):
        pl.when(live > i * size)(lambda i=i: group(i).start())

    def clear(i, _):
        dense[pl.ds(pl.multiple_of(i * 16, 16), 16), :] = jnp.zeros((16, dense.shape[1]), bf16)
        return 0

    lax.fori_loop(0, dense.shape[0] // 16, clear, 0)
    loads[2].wait()
    turned[...] = sketch_here[...].T
    for load in loads[:2]:
        load.wait()

    def put(s):
        r = pl.multiple_of(rows_place[s] * tile, tile)
        c = pl.multiple_of(cols_place[s] * tile, tile)
        dense[pl.ds(r, tile), pl.ds(c, tile)] = stage[s]

    def put_one(s, _):
        put(s)
        return 0

    for i in range(groups):

        @pl.when(live > i * size)
        def _(i=i):
            group(i).wait()

            @pl.when(live >= (i + 1) * size)
            def _():
                for s in range(i * size, (i + 1) * size):
                    put(s)

            @pl.when(live < (i + 1) * size)
            def _():
                lax.fori_loop(i * size, live, put_one, 0)

    left = rows_of(turned, 1 - core, theirs.shape[0])
    width = 512
    for j in range(dense.shape[1] // width):
        cut = pl.ds(j * width, width)
        encode(jnp.dot(left, dense[:, cut], preferred_element_type=f32), theirs.at[:, cut])


def own_kernel(turned, dense, mine):
    core, _ = core_and_chip()
    left = rows_of(turned, core, mine.shape[0])
    mine[...] = jnp.dot(left, dense[...], preferred_element_type=f32)


def halve(total, bit, keep, send):
    _, chip = core_and_chip()
    width = keep.shape[1]
    ours = (chip >> bit) & 1
    low, high = total[:, :width], total[:, width:]
    keep[...] = jnp.where(ours == 0, low, high)
    encode(jnp.where(ours == 0, high, low), send)


def pair_kernel(chips, mine, got, *outs):
    direct, rest = outs[:chips], outs[chips:]
    _, chip = core_and_chip()
    lead = direct[0].shape[0]
    share, genes = mine.shape

    def total(rows, index, width):
        cut = pl.ds(pl.multiple_of(index * width, width), width)
        return mine[rows, cut] + got[rows, cut].astype(f32) * scale_of(got[:16, cut][:8])

    if len(rest) == 2:
        ours = chip & 1
        keep, send = rest
        encode(total(slice(lead, share), 1 - ours, genes // 2), send)
        keep[...] = total(slice(lead, share), ours, genes // 2)
    else:
        encode(total(slice(lead, share), 0, genes), rest[0])
    for k, out in enumerate(direct):
        part = total(slice(0, lead), chip ^ k, out.shape[1])
        if k == 0:
            out[...] = part
        else:
            encode(part, out)


def add_kernel(bit, keep, got, *outs):
    total = keep[...] + decode(got[...])
    if len(outs) == 2:
        halve(total, bit, *outs)
    else:
        encode(total, outs[0])


def cast_kernel(code, got, out):
    out[...] = (decode(code[...]) + decode(got[...])).astype(bf16)


def direct_cast_kernel(own, *refs):
    *got, out = refs
    total = own[...]
    for ref in got:
        total = total + decode(ref[...])
    out[...] = total.astype(bf16)


def join_kernel(*refs):
    *pieces, out = refs
    _, chip = core_and_chip()
    width = pieces[0].shape[1]
    for k, piece in enumerate(pieces):
        out[:, pl.ds(pl.multiple_of((chip ^ k) * width, width), width)] = piece[...]


def gene_kernel(masks, first, first_theirs, *refs):
    *pieces, gene = refs
    core, chip = core_and_chip()
    rows, width = pieces[0].shape
    lead = first.shape[0]

    def at(stream, owner):
        start = owner * (lead + rows) + stream * lead
        return pl.ds(pl.multiple_of(start, 16), rows if stream else lead)

    gene[at(0, core), :] = first[...]
    gene[at(0, 1 - core), :] = first_theirs[...]
    for k, mask in enumerate(masks):
        place, size = 0, gene.shape[1]
        for bit in range(len(masks).bit_length() - 1):
            size //= 2
            place = place + (((chip ^ mask) >> bit) & 1) * size
        cut = pl.ds(pl.multiple_of(place, width), width)
        gene[at(1, core), cut] = pieces[k][...]
        gene[at(1, 1 - core), cut] = pieces[len(masks) + k][...]


def cell_kernel(k, dense, gene, out):
    height = out.shape[0]
    me = lax.axis_index("genes")
    left = dense[pl.ds(pl.multiple_of((me ^ k) * height, height), height), :]
    part = lax.dot_general(left, gene[...], (((1,), (1,)), ((), ())), preferred_element_type=f32)
    if k == 0:
        out[...] = part
    else:
        encode(part, out)


def more_kernel(total, got, out):
    out[...] = total[...] + decode(got[...])


def local(n_cells, n_genes, sketch, tiles, tile_rows, tile_cols, tile_counts):
    cells, rank = sketch.shape
    slots, tile, _ = tiles.shape
    genes = GENE_BLOCKS * tile
    bits = (n_cells // CORES).bit_length() - 1
    share = rank // CORES
    lead = share * DIRECT[0] // DIRECT[1] // 16 * 16
    rows = share - lead
    height = cells // n_genes
    flops = 2 * cells * genes * rank
    shape = jax.ShapeDtypeStruct

    def to_core(x):
        return lax.ppermute(x, "cells", [(i, i ^ 1) for i in range(n_cells)])

    def to_chip(x, k):
        return lax.ppermute(x, "cells", [(i, i ^ (CORES * k)) for i in range(n_cells)])

    def to_gene(x, k):
        return lax.ppermute(x, "genes", [(i, i ^ k) for i in range(n_genes)])

    def halves(width):
        return shape((rows, width // 2), f32), shape((rows, width // 2), i16)

    dense, turned, theirs = call(
        dense_kernel,
        (shape((cells, genes), bf16), shape((rank, cells), bf16), shape((share, genes), i16)),
        [SMEM] + [HBM] * 4,
        scratch=[
            (pltpu.SMEM((slots,), i32), pltpu.SMEM((slots,), i32)),
            pltpu.VMEM((slots, tile, tile), bf16),
            pltpu.VMEM((cells, rank), bf16),
            pltpu.SemaphoreType.DMA((3,)),
            pltpu.SemaphoreType.DMA((slots // 16 if slots % 16 == 0 else 1,)),
        ],
        flops=flops // 2,
        nbytes=8 * MIB,
    )(tile_counts, *(pltpu.with_memory_space_constraint(x, pltpu.HBM) for x in (tile_rows, tile_cols, sketch, tiles)))
    got = to_core(theirs)
    mine = call(own_kernel, shape((share, genes), f32), [VMEM, VMEM], flops=flops // 2, nbytes=5 * MIB)(turned, dense)
    chips = n_cells // CORES
    chunk = genes // chips
    one = halves(genes) if bits > 1 else (shape((rows, genes), i16),)
    pieces = call(
        functools.partial(pair_kernel, chips),
        (shape((lead, chunk), f32),) + (shape((lead, chunk), i16),) * (chips - 1) + one,
        [VMEM, VMEM],
        nbytes=3 * MIB,
    )(mine, got)
    direct, half = pieces[:chips], pieces[chips:]

    width = genes
    for bit in range(bits - 1):
        width //= 2
        outs = halves(width) if bit < bits - 2 else (shape((rows, width), i16),)
        half = call(functools.partial(add_kernel, bit + 1), outs, [VMEM, VMEM], nbytes=MIB)(
            half[0], to_chip(half[1], 1 << bit)
        )
    came = [to_chip(direct[k], k) for k in reversed(range(1, chips))]
    summed = call(direct_cast_kernel, shape((lead, chunk), bf16), [VMEM] * chips, nbytes=MIB)(direct[0], *came)
    crossed = to_chip(half[-1], chips // 2)
    spread = [to_chip(summed, k) for k in reversed(range(1, chips))][::-1]
    held = [call(cast_kernel, shape((rows, width), bf16), [VMEM, VMEM], nbytes=MIB)(half[-1], crossed)]
    *spread, _ = lax.optimization_barrier((*spread, held[0]))
    first = call(join_kernel, shape((lead, genes), bf16), [VMEM] * chips, nbytes=MIB)(summed, *spread)
    masks = [0]
    for bit in reversed(range(bits - 1)):
        held = held + [to_chip(x, 1 << bit) for x in held]
        masks += [mask ^ (1 << bit) for mask in masks]
    theirs = [to_core(x) for x in held]
    gene = call(
        functools.partial(gene_kernel, masks), shape((rank, genes), bf16), [VMEM] * (2 + 2 * len(held)), nbytes=2 * MIB
    )(first, to_core(first), *held, *theirs)

    def cell(k, gene):
        kind = f32 if k == 0 else i16
        return call(
            functools.partial(cell_kernel, k),
            shape((height, rank), kind),
            [VMEM, VMEM],
        )(dense, gene)

    got = []
    for k in reversed(range(1, n_genes)):
        got.append(to_gene(cell(k, gene), k))
    total = cell(0, gene)
    for x in got:
        total = call(more_kernel, shape((height, rank), f32), [VMEM, VMEM], nbytes=16 * MIB)(total, x)
    return total


def solution(mesh):
    in_specs = (
        P("cells", None),
        P(("cells", "genes"), None, None),
        P(("cells", "genes")),
        P(("cells", "genes")),
        P(("cells", "genes")),
    )
    out_specs = P(("cells", "genes"), None)
    body = functools.partial(local, mesh.shape["cells"], mesh.shape["genes"])
    return jax.shard_map(body, mesh=mesh, in_specs=in_specs, out_specs=out_specs, check_vma=False)
```

```python
import functools

import jax
import jax.numpy as jnp
from jax import lax
from jax.experimental import pallas as pl
from jax.experimental.pallas import tpu as pltpu
from jax.sharding import PartitionSpec as P

GENE_BLOCKS = 16
CORES = 2
DIRECT = (1, 2)
MIB = 1 << 20

VMEM = pl.BlockSpec(memory_space=pltpu.VMEM)
SMEM = pl.BlockSpec(memory_space=pltpu.SMEM)
HBM = pl.BlockSpec(memory_space=pltpu.HBM)
f32, bf16, i16, i32 = jnp.float32, jnp.bfloat16, jnp.int16, jnp.int32


def encode(x, out, at=()):
    peak = jnp.max(jnp.abs(x), axis=0, keepdims=True)
    expo = jnp.ceil(jnp.log2(jnp.maximum(peak, 2.0**-100)))
    expo = jnp.clip(expo, -100.0, 126.0)
    code = jnp.round(x * jnp.exp2(14.0 - expo)).astype(i32)
    top = code[:16]
    row = lax.broadcasted_iota(i32, top.shape, 0)
    word = jnp.broadcast_to(expo.astype(i32) + 128, top.shape)
    marked = (top & ~1) | ((word >> jnp.minimum(row, 7)) & 1)
    top = jnp.where(row < 8, marked, top)
    out[at + (pl.ds(0, 16),)] = top.astype(i16)
    out[at + (pl.ds(16, x.shape[0] - 16),)] = code[16:].astype(i16)


def decode(code):
    code = code.astype(i32)
    head = code[:8]
    row = lax.broadcasted_iota(i32, head.shape, 0)
    word = jnp.sum((head & 1) << row, axis=0, keepdims=True)
    scale = jnp.exp2((word - (128 + 14)).astype(f32))
    return code.astype(f32) * scale


def core_and_chip():
    place = lax.axis_index("cells")
    return lax.rem(place, CORES), lax.div(place, CORES)


def call(body, outs, in_specs, scratch=(), mib=32, flops=0, nbytes=0):
    return pl.pallas_call(
        body,
        out_shape=outs,
        in_specs=in_specs,
        out_specs=jax.tree.map(lambda _: VMEM, outs),
        scratch_shapes=list(scratch),
        compiler_params=pltpu.CompilerParams(vmem_limit_bytes=mib * MIB),
        cost_estimate=pl.CostEstimate(flops=flops, bytes_accessed=nbytes, transcendentals=0),
    )


def rows_of(turned, core, rows):
    return turned[pl.ds(pl.multiple_of(core * rows, rows), rows), :]


def dense_kernel(count, rows, cols, sketch, tiles, dense, turned, theirs, place, stage, sketch_here, load_sems, sems):
    slots, tile, _ = tiles.shape
    core, _ = core_and_chip()
    live = count[0]
    rows_place, cols_place = place
    groups = sems.shape[0]
    size = slots // groups
    loads = [
        pltpu.make_async_copy(src, dst, load_sems.at[i])
        for i, (src, dst) in enumerate(((rows, rows_place), (cols, cols_place), (sketch, sketch_here)))
    ]

    def group(i):
        cut = pl.ds(i * size, size)
        return pltpu.make_async_copy(tiles.at[cut], stage.at[cut], sems.at[i])

    for load in loads:
        load.start()
    for i in range(groups):
        pl.when(live > i * size)(lambda i=i: group(i).start())

    def clear(i, _):
        dense[pl.ds(pl.multiple_of(i * 16, 16), 16), :] = jnp.zeros((16, dense.shape[1]), bf16)
        return 0

    lax.fori_loop(0, dense.shape[0] // 16, clear, 0)
    loads[2].wait()
    turned[...] = sketch_here[...].T
    for load in loads[:2]:
        load.wait()

    def put(s):
        r = pl.multiple_of(rows_place[s] * tile, tile)
        c = pl.multiple_of(cols_place[s] * tile, tile)
        dense[pl.ds(r, tile), pl.ds(c, tile)] = stage[s]

    def put_one(s, _):
        put(s)
        return 0

    for i in range(groups):

        @pl.when(live > i * size)
        def _(i=i):
            group(i).wait()

            @pl.when(live >= (i + 1) * size)
            def _():
                for s in range(i * size, (i + 1) * size):
                    put(s)

            @pl.when(live < (i + 1) * size)
            def _():
                lax.fori_loop(i * size, live, put_one, 0)

    left = rows_of(turned, 1 - core, theirs.shape[0])
    width = 512
    for j in range(dense.shape[1] // width):
        cut = pl.ds(j * width, width)
        encode(jnp.dot(left, dense[:, cut], preferred_element_type=f32), theirs.at[:, cut])


def own_kernel(turned, dense, mine):
    core, _ = core_and_chip()
    left = rows_of(turned, core, mine.shape[0])
    mine[...] = jnp.dot(left, dense[...], preferred_element_type=f32)


def halve(total, bit, keep, send):
    _, chip = core_and_chip()
    width = keep.shape[1]
    ours = (chip >> bit) & 1
    low, high = total[:, :width], total[:, width:]
    keep[...] = jnp.where(ours == 0, low, high)
    encode(jnp.where(ours == 0, high, low), send)


def pair_kernel(chips, mine, got, *refs):
    *outs, total = refs
    direct, rest = outs[:chips], outs[chips:]
    _, chip = core_and_chip()
    total[...] = mine[...] + decode(got[...])
    rows, width = direct[0].shape
    if len(rest) == 2:
        halve(total[rows:, :], 0, *rest)
    else:
        encode(total[rows:, :], rest[0])
    for k, out in enumerate(direct):
        part = total[:rows, pl.ds(pl.multiple_of((chip ^ k) * width, width), width)]
        if k == 0:
            out[...] = part
        else:
            encode(part, out)


def add_kernel(bit, keep, got, *outs):
    total = keep[...] + decode(got[...])
    if len(outs) == 2:
        halve(total, bit, *outs)
    else:
        encode(total, outs[0])


def cast_kernel(code, got, out):
    out[...] = (decode(code[...]) + decode(got[...])).astype(bf16)


def direct_cast_kernel(own, *refs):
    *got, out = refs
    total = own[...]
    for ref in got:
        total = total + decode(ref[...])
    out[...] = total.astype(bf16)


def join_kernel(*refs):
    *pieces, out = refs
    _, chip = core_and_chip()
    width = pieces[0].shape[1]
    for k, piece in enumerate(pieces):
        out[:, pl.ds(pl.multiple_of((chip ^ k) * width, width), width)] = piece[...]


def tail_kernel(code, got, chunk, out):
    lead = chunk.shape[1]
    out[:, :lead] = chunk[...]
    out[:, lead:] = (decode(code[...]) + decode(got[...])).astype(bf16)


def far_kernel(*refs):
    *pieces, out = refs
    width = pieces[0].shape[1]
    for k, piece in enumerate(pieces):
        out[:, k * width : (k + 1) * width] = piece[...]


def tails_gene_kernel(*refs):
    *pieces, gene = refs
    core, chip = core_and_chip()
    count = len(pieces) // CORES
    for j, owner in enumerate((core, 1 - core)):
        here, near, both = pieces[j * count : (j + 1) * count]
        lead = both.shape[0]
        chunk = both.shape[1] // 2
        far = (both[:, :chunk], both[:, chunk:])
        rows, width = here.shape[0], here.shape[1] - chunk
        at = pl.ds(pl.multiple_of(owner * (lead + rows), 16), lead)
        after = pl.ds(pl.multiple_of(owner * (lead + rows) + lead, 16), rows)
        for k, piece in enumerate((here, near, *far)):
            cut = pl.ds(pl.multiple_of((chip ^ k) * chunk, chunk), chunk)
            gene[at, cut] = piece[:, :chunk]
        for k, piece in enumerate((here, near)):
            half = pl.ds(pl.multiple_of(((chip ^ k) & 1) * width, width), width)
            gene[after, half] = piece[:, chunk:]


def gene_kernel(masks, first, first_theirs, *refs):
    *pieces, gene = refs
    core, chip = core_and_chip()
    rows, width = pieces[0].shape
    lead = first.shape[0]

    def at(stream, owner):
        start = owner * (lead + rows) + stream * lead
        return pl.ds(pl.multiple_of(start, 16), rows if stream else lead)

    gene[at(0, core), :] = first[...]
    gene[at(0, 1 - core), :] = first_theirs[...]
    for k, mask in enumerate(masks):
        place, size = 0, gene.shape[1]
        for bit in range(len(masks).bit_length() - 1):
            size //= 2
            place = place + (((chip ^ mask) >> bit) & 1) * size
        cut = pl.ds(pl.multiple_of(place, width), width)
        gene[at(1, core), cut] = pieces[k][...]
        gene[at(1, 1 - core), cut] = pieces[len(masks) + k][...]


def cell_kernel(k, dense, gene, out):
    height = out.shape[0]
    me = lax.axis_index("genes")
    left = dense[pl.ds(pl.multiple_of((me ^ k) * height, height), height), :]
    part = lax.dot_general(left, gene[...], (((1,), (1,)), ((), ())), preferred_element_type=f32)
    if k == 0:
        out[...] = part
    else:
        encode(part, out)


def more_kernel(total, got, out):
    out[...] = total[...] + decode(got[...])


def local(n_cells, n_genes, sketch, tiles, tile_rows, tile_cols, tile_counts):
    cells, rank = sketch.shape
    slots, tile, _ = tiles.shape
    genes = GENE_BLOCKS * tile
    bits = (n_cells // CORES).bit_length() - 1
    share = rank // CORES
    lead = share * DIRECT[0] // DIRECT[1] // 16 * 16
    rows = share - lead
    height = cells // n_genes
    flops = 2 * cells * genes * rank
    shape = jax.ShapeDtypeStruct

    def to_core(x):
        return lax.ppermute(x, "cells", [(i, i ^ 1) for i in range(n_cells)])

    def to_chip(x, k):
        return lax.ppermute(x, "cells", [(i, i ^ (CORES * k)) for i in range(n_cells)])

    def to_gene(x, k):
        return lax.ppermute(x, "genes", [(i, i ^ k) for i in range(n_genes)])

    def halves(width):
        return shape((rows, width // 2), f32), shape((rows, width // 2), i16)

    dense, turned, theirs = call(
        dense_kernel,
        (shape((cells, genes), bf16), shape((rank, cells), bf16), shape((share, genes), i16)),
        [SMEM] + [HBM] * 4,
        scratch=[
            (pltpu.SMEM((slots,), i32), pltpu.SMEM((slots,), i32)),
            pltpu.VMEM((slots, tile, tile), bf16),
            pltpu.VMEM((cells, rank), bf16),
            pltpu.SemaphoreType.DMA((3,)),
            pltpu.SemaphoreType.DMA((slots // 16 if slots % 16 == 0 else 1,)),
        ],
        flops=flops // 2,
        nbytes=8 * MIB,
    )(tile_counts, *(pltpu.with_memory_space_constraint(x, pltpu.HBM) for x in (tile_rows, tile_cols, sketch, tiles)))
    got = to_core(theirs)
    mine = call(own_kernel, shape((share, genes), f32), [VMEM, VMEM], flops=flops // 2, nbytes=5 * MIB)(turned, dense)
    chips = n_cells // CORES
    chunk = genes // chips
    one = halves(genes) if bits > 1 else (shape((rows, genes), i16),)
    pieces = call(
        functools.partial(pair_kernel, chips),
        (shape((lead, chunk), f32),) + (shape((lead, chunk), i16),) * (chips - 1) + one,
        [VMEM, VMEM],
        scratch=[pltpu.VMEM((share, genes), f32)],
        nbytes=3 * MIB,
    )(mine, got)
    direct, half = pieces[:chips], pieces[chips:]

    width = genes
    for bit in range(bits - 1):
        width //= 2
        outs = halves(width) if bit < bits - 2 else (shape((rows, width), i16),)
        half = call(functools.partial(add_kernel, bit + 1), outs, [VMEM, VMEM], nbytes=MIB)(
            half[0], to_chip(half[1], 1 << bit)
        )
    came = [to_chip(direct[k], k) for k in reversed(range(1, chips))]
    summed = call(direct_cast_kernel, shape((lead, chunk), bf16), [VMEM] * chips, flops=30000000000)(direct[0], *came)
    crossed = to_chip(half[-1], chips // 2)
    if bits == 2 and lead == rows:
        far = [to_chip(summed, k) for k in reversed(range(2, chips))][::-1]
        tail = call(tail_kernel, shape((rows, chunk + width), bf16), [VMEM] * 3, nbytes=MIB)(half[-1], crossed, summed)
        far = call(far_kernel, shape((lead, 2 * chunk), bf16), [VMEM] * 2, flops=30000000000, nbytes=MIB)(*far)
        near, _ = lax.optimization_barrier((to_chip(tail, 1), far))
        whole = [tail, near, far]
        whole += [to_core(x) for x in whole]
        gene = call(tails_gene_kernel, shape((rank, genes), bf16), [VMEM] * len(whole), nbytes=2 * MIB)(*whole)
    else:
        spread = [to_chip(summed, k) for k in reversed(range(1, chips))][::-1]
        held = [call(cast_kernel, shape((rows, width), bf16), [VMEM, VMEM], nbytes=MIB)(half[-1], crossed)]
        *spread, _ = lax.optimization_barrier((*spread, held[0]))
        first = call(join_kernel, shape((lead, genes), bf16), [VMEM] * chips, nbytes=MIB)(summed, *spread)
        masks = [0]
        for bit in reversed(range(bits - 1)):
            held = held + [to_chip(x, 1 << bit) for x in held]
            masks += [mask ^ (1 << bit) for mask in masks]
        theirs = [to_core(x) for x in held]
        gene = call(
            functools.partial(gene_kernel, masks), shape((rank, genes), bf16), [VMEM] * (2 + 2 * len(held)), nbytes=2 * MIB
        )(first, to_core(first), *held, *theirs)

    def cell(k, gene):
        kind = f32 if k == 0 else i16
        return call(
            functools.partial(cell_kernel, k),
            shape((height, rank), kind),
            [VMEM, VMEM],
        )(dense, gene)

    got = []
    for k in reversed(range(1, n_genes)):
        got.append(to_gene(cell(k, gene), k))
    total = cell(0, gene)
    for x in got:
        total = call(more_kernel, shape((height, rank), f32), [VMEM, VMEM], nbytes=16 * MIB)(total, x)
    return total


def solution(mesh):
    in_specs = (
        P("cells", None),
        P(("cells", "genes"), None, None),
        P(("cells", "genes")),
        P(("cells", "genes")),
        P(("cells", "genes")),
    )
    out_specs = P(("cells", "genes"), None)
    body = functools.partial(local, mesh.shape["cells"], mesh.shape["genes"])
    return jax.shard_map(body, mesh=mesh, in_specs=in_specs, out_specs=out_specs, check_vma=False)
```

```python
import functools

import jax
import jax.numpy as jnp
from jax import lax
from jax.experimental import pallas as pl
from jax.experimental.pallas import tpu as pltpu
from jax.sharding import PartitionSpec as P

GENE_BLOCKS = 16
CORES = 2
DIRECT = (1, 2)
MIB = 1 << 20

VMEM = pl.BlockSpec(memory_space=pltpu.VMEM)
SMEM = pl.BlockSpec(memory_space=pltpu.SMEM)
HBM = pl.BlockSpec(memory_space=pltpu.HBM)
f32, bf16, i16, i32 = jnp.float32, jnp.bfloat16, jnp.int16, jnp.int32


def encode(x, out, at=()):
    peak = jnp.max(jnp.abs(x), axis=0, keepdims=True)
    expo = jnp.ceil(jnp.log2(jnp.maximum(peak, 2.0**-100)))
    expo = jnp.clip(expo, -100.0, 126.0)
    code = jnp.round(x * jnp.exp2(14.0 - expo)).astype(i32)
    top = code[:16]
    row = lax.broadcasted_iota(i32, top.shape, 0)
    word = jnp.broadcast_to(expo.astype(i32) + 128, top.shape)
    marked = (top & ~1) | ((word >> jnp.minimum(row, 7)) & 1)
    top = jnp.where(row < 8, marked, top)
    out[at + (pl.ds(0, 16),)] = top.astype(i16)
    out[at + (pl.ds(16, x.shape[0] - 16),)] = code[16:].astype(i16)


def scale_of(head):
    head = head.astype(i32)
    row = lax.broadcasted_iota(i32, head.shape, 0)
    word = jnp.sum((head & 1) << row, axis=0, keepdims=True)
    return jnp.exp2((word - (128 + 14)).astype(f32))


def decode(code):
    return code.astype(f32) * scale_of(code[:8])


def core_and_chip():
    place = lax.axis_index("cells")
    return lax.rem(place, CORES), lax.div(place, CORES)


def call(body, outs, in_specs, scratch=(), mib=32, flops=0, nbytes=0):
    return pl.pallas_call(
        body,
        out_shape=outs,
        in_specs=in_specs,
        out_specs=jax.tree.map(lambda _: VMEM, outs),
        scratch_shapes=list(scratch),
        compiler_params=pltpu.CompilerParams(vmem_limit_bytes=mib * MIB),
        cost_estimate=pl.CostEstimate(flops=flops, bytes_accessed=nbytes, transcendentals=0),
    )


def rows_of(turned, core, rows):
    return turned[pl.ds(pl.multiple_of(core * rows, rows), rows), :]


def dense_kernel(count, rows, cols, sketch, tiles, dense, turned, theirs, place, stage, sketch_here, load_sems, sems):
    slots, tile, _ = tiles.shape
    core, _ = core_and_chip()
    live = count[0]
    rows_place, cols_place = place
    groups = sems.shape[0]
    size = slots // groups
    loads = [
        pltpu.make_async_copy(src, dst, load_sems.at[i])
        for i, (src, dst) in enumerate(((rows, rows_place), (cols, cols_place), (sketch, sketch_here)))
    ]

    def group(i):
        cut = pl.ds(i * size, size)
        return pltpu.make_async_copy(tiles.at[cut], stage.at[cut], sems.at[i])

    for load in loads:
        load.start()
    for i in range(groups):
        pl.when(live > i * size)(lambda i=i: group(i).start())

    def clear(i, _):
        dense[pl.ds(pl.multiple_of(i * 16, 16), 16), :] = jnp.zeros((16, dense.shape[1]), bf16)
        return 0

    lax.fori_loop(0, dense.shape[0] // 16, clear, 0)
    loads[2].wait()
    turned[...] = sketch_here[...].T
    for load in loads[:2]:
        load.wait()

    def put(s):
        r = pl.multiple_of(rows_place[s] * tile, tile)
        c = pl.multiple_of(cols_place[s] * tile, tile)
        dense[pl.ds(r, tile), pl.ds(c, tile)] = stage[s]

    def put_one(s, _):
        put(s)
        return 0

    for i in range(groups):

        @pl.when(live > i * size)
        def _(i=i):
            group(i).wait()

            @pl.when(live >= (i + 1) * size)
            def _():
                for s in range(i * size, (i + 1) * size):
                    put(s)

            @pl.when(live < (i + 1) * size)
            def _():
                lax.fori_loop(i * size, live, put_one, 0)

    left = rows_of(turned, 1 - core, theirs.shape[0])
    width = 512
    for j in range(dense.shape[1] // width):
        cut = pl.ds(j * width, width)
        encode(jnp.dot(left, dense[:, cut], preferred_element_type=f32), theirs.at[:, cut])


def own_kernel(turned, dense, mine):
    core, _ = core_and_chip()
    left = rows_of(turned, core, mine.shape[0])
    mine[...] = jnp.dot(left, dense[...], preferred_element_type=f32)


def halve(total, bit, keep, send):
    _, chip = core_and_chip()
    width = keep.shape[1]
    ours = (chip >> bit) & 1
    low, high = total[:, :width], total[:, width:]
    keep[...] = jnp.where(ours == 0, low, high)
    encode(jnp.where(ours == 0, high, low), send)


def pair_kernel(chips, mine, got, *outs):
    direct, rest = outs[:chips], outs[chips:]
    _, chip = core_and_chip()
    lead = direct[0].shape[0]
    share, genes = mine.shape

    def total(rows, index, width):
        cut = pl.ds(pl.multiple_of(index * width, width), width)
        return mine[rows, cut] + got[rows, cut].astype(f32) * scale_of(got[:16, cut][:8])

    if len(rest) == 2:
        ours = chip & 1
        keep, send = rest
        encode(total(slice(lead, share), 1 - ours, genes // 2), send)
        keep[...] = total(slice(lead, share), ours, genes // 2)
    else:
        encode(total(slice(lead, share), 0, genes), rest[0])
    for k, out in enumerate(direct):
        part = total(slice(0, lead), chip ^ k, out.shape[1])
        if k == 0:
            out[...] = part
        else:
            encode(part, out)


def add_kernel(bit, keep, got, *outs):
    total = keep[...] + decode(got[...])
    if len(outs) == 2:
        halve(total, bit, *outs)
    else:
        encode(total, outs[0])


def cast_kernel(code, got, out):
    out[...] = (decode(code[...]) + decode(got[...])).astype(bf16)


def direct_cast_kernel(own, *refs):
    *got, out = refs
    total = own[...]
    for ref in got:
        total = total + decode(ref[...])
    out[...] = total.astype(bf16)


def join_kernel(*refs):
    *pieces, out = refs
    _, chip = core_and_chip()
    width = pieces[0].shape[1]
    for k, piece in enumerate(pieces):
        out[:, pl.ds(pl.multiple_of((chip ^ k) * width, width), width)] = piece[...]


def gene_kernel(masks, first, first_theirs, *refs):
    *pieces, out, gene = refs
    core, chip = core_and_chip()
    rows, width = pieces[0].shape
    lead = first.shape[0]

    def at(stream, owner):
        start = owner * (lead + rows) + stream * lead
        return pl.ds(pl.multiple_of(start, 16), rows if stream else lead)

    gene[at(0, core), :] = first[...]
    gene[at(0, 1 - core), :] = first_theirs[...]
    for k, mask in enumerate(masks):
        place, size = 0, gene.shape[1]
        for bit in range(len(masks).bit_length() - 1):
            size //= 2
            place = place + (((chip ^ mask) >> bit) & 1) * size
        cut = pl.ds(pl.multiple_of(place, width), width)
        gene[at(1, core), cut] = pieces[k][...]
        gene[at(1, 1 - core), cut] = pieces[len(masks) + k][...]
    out[...] = gene[...].T


def cell_kernel(k, dense, gene, out):
    height = out.shape[0]
    me = lax.axis_index("genes")
    left = dense[pl.ds(pl.multiple_of((me ^ k) * height, height), height), :]
    part = jnp.dot(left, gene[...], preferred_element_type=f32)
    if k == 0:
        out[...] = part
    else:
        encode(part, out)


def more_kernel(total, got, out):
    out[...] = total[...] + decode(got[...])


def local(n_cells, n_genes, sketch, tiles, tile_rows, tile_cols, tile_counts):
    cells, rank = sketch.shape
    slots, tile, _ = tiles.shape
    genes = GENE_BLOCKS * tile
    bits = (n_cells // CORES).bit_length() - 1
    share = rank // CORES
    lead = share * DIRECT[0] // DIRECT[1] // 16 * 16
    rows = share - lead
    height = cells // n_genes
    flops = 2 * cells * genes * rank
    shape = jax.ShapeDtypeStruct

    def to_core(x):
        return lax.ppermute(x, "cells", [(i, i ^ 1) for i in range(n_cells)])

    def to_chip(x, k):
        return lax.ppermute(x, "cells", [(i, i ^ (CORES * k)) for i in range(n_cells)])

    def to_gene(x, k):
        return lax.ppermute(x, "genes", [(i, i ^ k) for i in range(n_genes)])

    def halves(width):
        return shape((rows, width // 2), f32), shape((rows, width // 2), i16)

    dense, turned, theirs = call(
        dense_kernel,
        (shape((cells, genes), bf16), shape((rank, cells), bf16), shape((share, genes), i16)),
        [SMEM] + [HBM] * 4,
        scratch=[
            (pltpu.SMEM((slots,), i32), pltpu.SMEM((slots,), i32)),
            pltpu.VMEM((slots, tile, tile), bf16),
            pltpu.VMEM((cells, rank), bf16),
            pltpu.SemaphoreType.DMA((3,)),
            pltpu.SemaphoreType.DMA((slots // 8 if slots % 8 == 0 else 1,)),
        ],
        flops=flops // 2,
        nbytes=8 * MIB,
    )(tile_counts, *(pltpu.with_memory_space_constraint(x, pltpu.HBM) for x in (tile_rows, tile_cols, sketch, tiles)))
    got = to_core(theirs)
    mine = call(own_kernel, shape((share, genes), f32), [VMEM, VMEM], flops=flops // 2, nbytes=5 * MIB)(turned, dense)
    chips = n_cells // CORES
    chunk = genes // chips
    one = halves(genes) if bits > 1 else (shape((rows, genes), i16),)
    pieces = call(
        functools.partial(pair_kernel, chips),
        (shape((lead, chunk), f32),) + (shape((lead, chunk), i16),) * (chips - 1) + one,
        [VMEM, VMEM],
        nbytes=3 * MIB,
    )(mine, got)
    direct, half = pieces[:chips], pieces[chips:]

    width = genes
    for bit in range(bits - 1):
        width //= 2
        outs = halves(width) if bit < bits - 2 else (shape((rows, width), i16),)
        half = call(functools.partial(add_kernel, bit + 1), outs, [VMEM, VMEM], nbytes=MIB)(
            half[0], to_chip(half[1], 1 << bit)
        )
    came = [to_chip(direct[k], k) for k in reversed(range(1, chips))]
    summed = call(direct_cast_kernel, shape((lead, chunk), bf16), [VMEM] * chips, nbytes=MIB)(direct[0], *came)
    crossed = to_chip(half[-1], chips // 2)
    spread = [to_chip(summed, k) for k in reversed(range(1, chips))][::-1]
    held = [call(cast_kernel, shape((rows, width), bf16), [VMEM, VMEM], nbytes=MIB)(half[-1], crossed)]
    *spread, _ = lax.optimization_barrier((*spread, held[0]))
    first = call(join_kernel, shape((lead, genes), bf16), [VMEM] * chips, nbytes=MIB)(summed, *spread)
    masks = [0]
    for bit in reversed(range(bits - 1)):
        held = held + [to_chip(x, 1 << bit) for x in held]
        masks += [mask ^ (1 << bit) for mask in masks]
    theirs = [to_core(x) for x in held]
    gene = call(
        functools.partial(gene_kernel, masks),
        shape((genes, rank), bf16),
        [VMEM] * (2 + 2 * len(held)),
        scratch=[pltpu.VMEM((rank, genes), bf16)],
        nbytes=2 * MIB,
    )(first, to_core(first), *held, *theirs)

    def cell(k, gene):
        kind = f32 if k == 0 else i16
        return call(
            functools.partial(cell_kernel, k),
            shape((height, rank), kind),
            [VMEM, VMEM],
        )(dense, gene)

    got = []
    for k in reversed(range(1, n_genes)):
        got.append(to_gene(cell(k, gene), k))
    total = cell(0, gene)
    for x in got:
        total = call(more_kernel, shape((height, rank), f32), [VMEM, VMEM], nbytes=16 * MIB)(total, x)
    return total


def solution(mesh):
    in_specs = (
        P("cells", None),
        P(("cells", "genes"), None, None),
        P(("cells", "genes")),
        P(("cells", "genes")),
        P(("cells", "genes")),
    )
    out_specs = P(("cells", "genes"), None)
    body = functools.partial(local, mesh.shape["cells"], mesh.shape["genes"])
    return jax.shard_map(body, mesh=mesh, in_specs=in_specs, out_specs=out_specs, check_vma=False)
```

```python
import functools

import jax
import jax.numpy as jnp
from jax import lax
from jax.experimental import pallas as pl
from jax.experimental.pallas import tpu as pltpu
from jax.sharding import PartitionSpec as P

GENE_BLOCKS = 16
CORES = 2
DIRECT = (1, 2)
MIB = 1 << 20

VMEM = pl.BlockSpec(memory_space=pltpu.VMEM)
SMEM = pl.BlockSpec(memory_space=pltpu.SMEM)
HBM = pl.BlockSpec(memory_space=pltpu.HBM)
f32, bf16, i16, i32 = jnp.float32, jnp.bfloat16, jnp.int16, jnp.int32


def encode(x, out, at=()):
    peak = jnp.max(jnp.abs(x), axis=0, keepdims=True)
    expo = jnp.ceil(jnp.log2(jnp.maximum(peak, 2.0**-100)))
    expo = jnp.clip(expo, -100.0, 126.0)
    code = jnp.round(x * jnp.exp2(14.0 - expo)).astype(i32)
    top = code[:16]
    row = lax.broadcasted_iota(i32, top.shape, 0)
    word = jnp.broadcast_to(expo.astype(i32) + 128, top.shape)
    marked = (top & ~1) | ((word >> jnp.minimum(row, 7)) & 1)
    top = jnp.where(row < 8, marked, top)
    out[at + (pl.ds(0, 16),)] = top.astype(i16)
    out[at + (pl.ds(16, x.shape[0] - 16),)] = code[16:].astype(i16)


def scale_of(head):
    head = head.astype(i32)
    row = lax.broadcasted_iota(i32, head.shape, 0)
    word = jnp.sum((head & 1) << row, axis=0, keepdims=True)
    return jnp.exp2((word - (128 + 14)).astype(f32))


def decode(code):
    return code.astype(f32) * scale_of(code[:8])


def core_and_chip():
    place = lax.axis_index("cells")
    return lax.rem(place, CORES), lax.div(place, CORES)


def call(body, outs, in_specs, scratch=(), mib=32, flops=0, nbytes=0):
    return pl.pallas_call(
        body,
        out_shape=outs,
        in_specs=in_specs,
        out_specs=jax.tree.map(lambda _: VMEM, outs),
        scratch_shapes=list(scratch),
        compiler_params=pltpu.CompilerParams(vmem_limit_bytes=mib * MIB),
        cost_estimate=pl.CostEstimate(flops=flops, bytes_accessed=nbytes, transcendentals=0),
    )


def rows_of(turned, core, rows):
    return turned[pl.ds(pl.multiple_of(core * rows, rows), rows), :]


def dense_kernel(count, rows, cols, sketch, tiles, dense, turned, theirs, place, stage, sketch_here, load_sems, sems):
    slots, tile, _ = tiles.shape
    core, _ = core_and_chip()
    live = count[0]
    rows_place, cols_place = place
    groups = sems.shape[0]
    size = slots // groups
    loads = [
        pltpu.make_async_copy(src, dst, load_sems.at[i])
        for i, (src, dst) in enumerate(((rows, rows_place), (cols, cols_place), (sketch, sketch_here)))
    ]

    def group(i):
        cut = pl.ds(i * size, size)
        return pltpu.make_async_copy(tiles.at[cut], stage.at[cut], sems.at[i])

    for load in loads:
        load.start()
    for i in range(groups):
        pl.when(live > i * size)(lambda i=i: group(i).start())

    def clear(i, _):
        dense[pl.ds(pl.multiple_of(i * 64, 64), 64), :] = jnp.zeros((64, dense.shape[1]), bf16)
        return 0

    lax.fori_loop(0, dense.shape[0] // 64, clear, 0)
    loads[2].wait()
    turned[...] = sketch_here[...].T
    for load in loads[:2]:
        load.wait()

    def put(s):
        r = pl.multiple_of(rows_place[s] * tile, tile)
        c = pl.multiple_of(cols_place[s] * tile, tile)
        dense[pl.ds(r, tile), pl.ds(c, tile)] = stage[s]

    def put_one(s, _):
        put(s)
        return 0

    for i in range(groups):

        @pl.when(live > i * size)
        def _(i=i):
            group(i).wait()

            @pl.when(live >= (i + 1) * size)
            def _():
                for s in range(i * size, (i + 1) * size):
                    put(s)

            @pl.when(live < (i + 1) * size)
            def _():
                lax.fori_loop(i * size, live, put_one, 0)

    left = rows_of(turned, 1 - core, theirs.shape[0])
    width = 1024
    for j in range(dense.shape[1] // width):
        cut = pl.ds(j * width, width)
        encode(jnp.dot(left, dense[:, cut], preferred_element_type=f32), theirs.at[:, cut])


def own_kernel(turned, dense, mine):
    core, _ = core_and_chip()
    left = rows_of(turned, core, mine.shape[0])
    mine[...] = jnp.dot(left, dense[...], preferred_element_type=f32)


def halve(total, bit, keep, send):
    _, chip = core_and_chip()
    width = keep.shape[1]
    ours = (chip >> bit) & 1
    low, high = total[:, :width], total[:, width:]
    keep[...] = jnp.where(ours == 0, low, high)
    encode(jnp.where(ours == 0, high, low), send)


def pair_kernel(chips, mine, got, *outs):
    direct, rest = outs[:chips], outs[chips:]
    _, chip = core_and_chip()
    lead = direct[0].shape[0]
    share, genes = mine.shape

    def total(rows, index, width):
        cut = pl.ds(pl.multiple_of(index * width, width), width)
        return mine[rows, cut] + got[rows, cut].astype(f32) * scale_of(got[:16, cut][:8])

    if len(rest) == 2:
        ours = chip & 1
        keep, send = rest
        encode(total(slice(lead, share), 1 - ours, genes // 2), send)
        keep[...] = total(slice(lead, share), ours, genes // 2)
    else:
        encode(total(slice(lead, share), 0, genes), rest[0])
    for k, out in enumerate(direct):
        part = total(slice(0, lead), chip ^ k, out.shape[1])
        if k == 0:
            out[...] = part
        else:
            encode(part, out)


def add_kernel(bit, keep, got, *outs):
    total = keep[...] + decode(got[...])
    if len(outs) == 2:
        halve(total, bit, *outs)
    else:
        encode(total, outs[0])


def cast_kernel(code, got, out):
    out[...] = (decode(code[...]) + decode(got[...])).astype(bf16)


def direct_cast_kernel(own, *refs):
    *got, out = refs
    total = own[...]
    for ref in got:
        total = total + decode(ref[...])
    out[...] = total.astype(bf16)


def join_kernel(*refs):
    *pieces, out = refs
    _, chip = core_and_chip()
    width = pieces[0].shape[1]
    for k, piece in enumerate(pieces):
        out[:, pl.ds(pl.multiple_of((chip ^ k) * width, width), width)] = piece[...]


def gene_kernel(masks, first, first_theirs, *refs):
    *pieces, gene = refs
    core, chip = core_and_chip()
    rows, width = pieces[0].shape
    lead = first.shape[0]

    def at(stream, owner):
        start = owner * (lead + rows) + stream * lead
        return pl.ds(pl.multiple_of(start, 16), rows if stream else lead)

    gene[at(0, core), :] = first[...]
    gene[at(0, 1 - core), :] = first_theirs[...]
    for k, mask in enumerate(masks):
        place, size = 0, gene.shape[1]
        for bit in range(len(masks).bit_length() - 1):
            size //= 2
            place = place + (((chip ^ mask) >> bit) & 1) * size
        cut = pl.ds(pl.multiple_of(place, width), width)
        gene[at(1, core), cut] = pieces[k][...]
        gene[at(1, 1 - core), cut] = pieces[len(masks) + k][...]


def cell_kernel(k, dense, gene, out):
    height = out.shape[0]
    me = lax.axis_index("genes")
    left = dense[pl.ds(pl.multiple_of((me ^ k) * height, height), height), :]
    part = lax.dot_general(left, gene[...], (((1,), (1,)), ((), ())), preferred_element_type=f32)
    if k == 0:
        out[...] = part
    else:
        encode(part, out)


def more_kernel(total, got, out):
    out[...] = total[...] + decode(got[...])


def local(n_cells, n_genes, sketch, tiles, tile_rows, tile_cols, tile_counts):
    cells, rank = sketch.shape
    slots, tile, _ = tiles.shape
    genes = GENE_BLOCKS * tile
    bits = (n_cells // CORES).bit_length() - 1
    share = rank // CORES
    lead = share * DIRECT[0] // DIRECT[1] // 16 * 16
    rows = share - lead
    height = cells // n_genes
    flops = 2 * cells * genes * rank
    shape = jax.ShapeDtypeStruct

    def to_core(x):
        return lax.ppermute(x, "cells", [(i, i ^ 1) for i in range(n_cells)])

    def to_chip(x, k):
        return lax.ppermute(x, "cells", [(i, i ^ (CORES * k)) for i in range(n_cells)])

    def to_gene(x, k):
        return lax.ppermute(x, "genes", [(i, i ^ k) for i in range(n_genes)])

    def halves(width):
        return shape((rows, width // 2), f32), shape((rows, width // 2), i16)

    dense, turned, theirs = call(
        dense_kernel,
        (shape((cells, genes), bf16), shape((rank, cells), bf16), shape((share, genes), i16)),
        [SMEM] + [HBM] * 4,
        scratch=[
            (pltpu.SMEM((slots,), i32), pltpu.SMEM((slots,), i32)),
            pltpu.VMEM((slots, tile, tile), bf16),
            pltpu.VMEM((cells, rank), bf16),
            pltpu.SemaphoreType.DMA((3,)),
            pltpu.SemaphoreType.DMA((slots // 16 if slots % 16 == 0 else 1,)),
        ],
        flops=flops // 2,
        nbytes=8 * MIB,
    )(tile_counts, *(pltpu.with_memory_space_constraint(x, pltpu.HBM) for x in (tile_rows, tile_cols, sketch, tiles)))
    got = to_core(theirs)
    mine = call(own_kernel, shape((share, genes), f32), [VMEM, VMEM], flops=flops // 2, nbytes=5 * MIB)(turned, dense)
    chips = n_cells // CORES
    chunk = genes // chips
    one = halves(genes) if bits > 1 else (shape((rows, genes), i16),)
    pieces = call(
        functools.partial(pair_kernel, chips),
        (shape((lead, chunk), f32),) + (shape((lead, chunk), i16),) * (chips - 1) + one,
        [VMEM, VMEM],
        nbytes=3 * MIB,
    )(mine, got)
    direct, half = pieces[:chips], pieces[chips:]

    width = genes
    for bit in range(bits - 1):
        width //= 2
        outs = halves(width) if bit < bits - 2 else (shape((rows, width), i16),)
        half = call(functools.partial(add_kernel, bit + 1), outs, [VMEM, VMEM], nbytes=MIB)(
            half[0], to_chip(half[1], 1 << bit)
        )
    came = [to_chip(direct[k], k) for k in reversed(range(1, chips))]
    summed = call(direct_cast_kernel, shape((lead, chunk), bf16), [VMEM] * chips, nbytes=MIB)(direct[0], *came)
    crossed = to_chip(half[-1], chips // 2)
    spread = [to_chip(summed, k) for k in reversed(range(1, chips))][::-1]
    held = [call(cast_kernel, shape((rows, width), bf16), [VMEM, VMEM], nbytes=MIB)(half[-1], crossed)]
    *spread, _ = lax.optimization_barrier((*spread, held[0]))
    first = call(join_kernel, shape((lead, genes), bf16), [VMEM] * chips, nbytes=MIB)(summed, *spread)
    masks = [0]
    for bit in reversed(range(bits - 1)):
        held = held + [to_chip(x, 1 << bit) for x in held]
        masks += [mask ^ (1 << bit) for mask in masks]
    theirs = [to_core(x) for x in held]
    gene = call(
        functools.partial(gene_kernel, masks), shape((rank, genes), bf16), [VMEM] * (2 + 2 * len(held)), nbytes=2 * MIB
    )(first, to_core(first), *held, *theirs)

    def cell(k, gene):
        kind = f32 if k == 0 else i16
        return call(
            functools.partial(cell_kernel, k),
            shape((height, rank), kind),
            [VMEM, VMEM],
        )(dense, gene)

    got = []
    for k in reversed(range(1, n_genes)):
        got.append(to_gene(cell(k, gene), k))
    total = cell(0, gene)
    for x in got:
        total = call(more_kernel, shape((height, rank), f32), [VMEM, VMEM], nbytes=16 * MIB)(total, x)
    return total


def solution(mesh):
    in_specs = (
        P("cells", None),
        P(("cells", "genes"), None, None),
        P(("cells", "genes")),
        P(("cells", "genes")),
        P(("cells", "genes")),
    )
    out_specs = P(("cells", "genes"), None)
    body = functools.partial(local, mesh.shape["cells"], mesh.shape["genes"])
    return jax.shard_map(body, mesh=mesh, in_specs=in_specs, out_specs=out_specs, check_vma=False)
```

```python
import functools

import jax
import jax.numpy as jnp
from jax import lax
from jax.experimental import pallas as pl
from jax.experimental.pallas import tpu as pltpu
from jax.sharding import PartitionSpec as P

GENE_BLOCKS = 16
CORES = 2
DIRECT = (1, 2)
MIB = 1 << 20

VMEM = pl.BlockSpec(memory_space=pltpu.VMEM)
SMEM = pl.BlockSpec(memory_space=pltpu.SMEM)
HBM = pl.BlockSpec(memory_space=pltpu.HBM)
f32, bf16, i16, i32 = jnp.float32, jnp.bfloat16, jnp.int16, jnp.int32


def encode(x, out, at=()):
    peak = jnp.max(jnp.abs(x), axis=0, keepdims=True)
    expo = jnp.ceil(jnp.log2(jnp.maximum(peak, 2.0**-100)))
    expo = jnp.clip(expo, -100.0, 126.0)
    code = jnp.round(x * jnp.exp2(14.0 - expo)).astype(i32)
    top = code[:16]
    row = lax.broadcasted_iota(i32, top.shape, 0)
    word = jnp.broadcast_to(expo.astype(i32) + 128, top.shape)
    marked = (top & ~1) | ((word >> jnp.minimum(row, 7)) & 1)
    top = jnp.where(row < 8, marked, top)
    out[at + (pl.ds(0, 16),)] = top.astype(i16)
    out[at + (pl.ds(16, x.shape[0] - 16),)] = code[16:].astype(i16)


def scale_of(head):
    head = head.astype(i32)
    row = lax.broadcasted_iota(i32, head.shape, 0)
    word = jnp.sum((head & 1) << row, axis=0, keepdims=True)
    return jnp.exp2((word - (128 + 14)).astype(f32))


def decode(code):
    return code.astype(f32) * scale_of(code[:8])


def core_and_chip():
    place = lax.axis_index("cells")
    return lax.rem(place, CORES), lax.div(place, CORES)


def call(body, outs, in_specs, scratch=(), mib=32, flops=0, nbytes=0):
    return pl.pallas_call(
        body,
        out_shape=outs,
        in_specs=in_specs,
        out_specs=jax.tree.map(lambda _: VMEM, outs),
        scratch_shapes=list(scratch),
        compiler_params=pltpu.CompilerParams(vmem_limit_bytes=mib * MIB),
        cost_estimate=pl.CostEstimate(flops=flops, bytes_accessed=nbytes, transcendentals=0),
    )


def rows_of(turned, core, rows):
    return turned[pl.ds(pl.multiple_of(core * rows, rows), rows), :]


def dense_kernel(count, rows, cols, sketch, tiles, dense, turned, theirs, place, stage, sketch_here, load_sems, sems):
    slots, tile, _ = tiles.shape
    core, _ = core_and_chip()
    live = count[0]
    rows_place, cols_place = place
    groups = sems.shape[0]
    size = slots // groups
    loads = [
        pltpu.make_async_copy(src, dst, load_sems.at[i])
        for i, (src, dst) in enumerate(((rows, rows_place), (cols, cols_place), (sketch, sketch_here)))
    ]

    def group(i):
        cut = pl.ds(i * size, size)
        return pltpu.make_async_copy(tiles.at[cut], stage.at[cut], sems.at[i])

    for load in loads:
        load.start()
    for i in range(groups):
        pl.when(live > i * size)(lambda i=i: group(i).start())

    def clear(i, _):
        dense[pl.ds(pl.multiple_of(i * 16, 16), 16), :] = jnp.zeros((16, dense.shape[1]), bf16)
        return 0

    lax.fori_loop(0, dense.shape[0] // 16, clear, 0)
    loads[2].wait()
    turned[...] = sketch_here[...].T
    for load in loads[:2]:
        load.wait()

    def put(s):
        r = pl.multiple_of(rows_place[s] * tile, tile)
        c = pl.multiple_of(cols_place[s] * tile, tile)
        dense[pl.ds(r, tile), pl.ds(c, tile)] = stage[s]

    def put_one(s, _):
        put(s)
        return 0

    for i in range(groups):

        @pl.when(live > i * size)
        def _(i=i):
            group(i).wait()

            @pl.when(live >= (i + 1) * size)
            def _():
                for s in range(i * size, (i + 1) * size):
                    put(s)

            @pl.when(live < (i + 1) * size)
            def _():
                lax.fori_loop(i * size, live, put_one, 0)

    left = rows_of(turned, 1 - core, theirs.shape[0])
    width = 512
    for j in range(dense.shape[1] // width):
        cut = pl.ds(j * width, width)
        encode(jnp.dot(left, dense[:, cut], preferred_element_type=f32), theirs.at[:, cut])


def own_kernel(turned, dense, mine):
    core, _ = core_and_chip()
    left = rows_of(turned, core, mine.shape[0])
    mine[...] = jnp.dot(left, dense[...], preferred_element_type=f32)


def halve(total, bit, keep, send):
    _, chip = core_and_chip()
    width = keep.shape[1]
    ours = (chip >> bit) & 1
    low, high = total[:, :width], total[:, width:]
    keep[...] = jnp.where(ours == 0, low, high)
    encode(jnp.where(ours == 0, high, low), send)


def pair_kernel(chips, mine, got, *outs):
    direct, rest = outs[:chips], outs[chips:]
    _, chip = core_and_chip()
    lead = direct[0].shape[0]
    share, genes = mine.shape

    def total(rows, index, width):
        cut = pl.ds(pl.multiple_of(index * width, width), width)
        return mine[rows, cut] + got[rows, cut].astype(f32) * scale_of(got[:16, cut][:8])

    if len(rest) == 2:
        ours = chip & 1
        keep, send = rest
        encode(total(slice(lead, share), 1 - ours, genes // 2), send)
        keep[...] = total(slice(lead, share), ours, genes // 2)
    else:
        encode(total(slice(lead, share), 0, genes), rest[0])
    for k, out in enumerate(direct):
        part = total(slice(0, lead), chip ^ k, out.shape[1])
        if k == 0:
            out[...] = part
        else:
            encode(part, out)


def add_kernel(bit, keep, got, *outs):
    total = keep[...] + decode(got[...])
    if len(outs) == 2:
        halve(total, bit, *outs)
    else:
        encode(total, outs[0])


def cast_kernel(code, got, out):
    out[...] = (decode(code[...]) + decode(got[...])).astype(bf16)


def direct_cast_kernel(own, *refs):
    *got, out = refs
    total = own[...]
    for ref in got:
        total = total + decode(ref[...])
    out[...] = total.astype(bf16)


def join_kernel(*refs):
    *pieces, out = refs
    _, chip = core_and_chip()
    width = pieces[0].shape[1]
    for k, piece in enumerate(pieces):
        out[:, pl.ds(pl.multiple_of((chip ^ k) * width, width), width)] = piece[...]


def gene_kernel(masks, first, first_theirs, *refs):
    *pieces, gene = refs
    core, chip = core_and_chip()
    rows, width = pieces[0].shape
    lead = first.shape[0]

    def at(stream, owner):
        start = owner * (lead + rows) + stream * lead
        return pl.ds(pl.multiple_of(start, 16), rows if stream else lead)

    gene[at(0, core), :] = first[...]
    gene[at(0, 1 - core), :] = first_theirs[...]
    for k, mask in enumerate(masks):
        place, size = 0, gene.shape[1]
        for bit in range(len(masks).bit_length() - 1):
            size //= 2
            place = place + (((chip ^ mask) >> bit) & 1) * size
        cut = pl.ds(pl.multiple_of(place, width), width)
        gene[at(1, core), cut] = pieces[k][...]
        gene[at(1, 1 - core), cut] = pieces[len(masks) + k][...]


def cell_kernel(k, dense, gene, out):
    height = out.shape[0]
    me = lax.axis_index("genes")
    left = dense[pl.ds(pl.multiple_of((me ^ k) * height, height), height), :]
    part = lax.dot_general(left, gene[...], (((1,), (1,)), ((), ())), preferred_element_type=f32)
    if k == 0:
        out[...] = part
    else:
        encode(part, out)


def more_kernel(total, got, out):
    out[...] = total[...] + decode(got[...])


def local(n_cells, n_genes, sketch, tiles, tile_rows, tile_cols, tile_counts):
    cells, rank = sketch.shape
    slots, tile, _ = tiles.shape
    genes = GENE_BLOCKS * tile
    bits = (n_cells // CORES).bit_length() - 1
    share = rank // CORES
    lead = share * DIRECT[0] // DIRECT[1] // 16 * 16
    rows = share - lead
    height = cells // n_genes
    flops = 2 * cells * genes * rank
    shape = jax.ShapeDtypeStruct

    def to_core(x):
        return lax.ppermute(x, "cells", [(i, i ^ 1) for i in range(n_cells)])

    def to_chip(x, k):
        return lax.ppermute(x, "cells", [(i, i ^ (CORES * k)) for i in range(n_cells)])

    def to_gene(x, k):
        return lax.ppermute(x, "genes", [(i, i ^ k) for i in range(n_genes)])

    def halves(width):
        return shape((rows, width // 2), f32), shape((rows, width // 2), i16)

    dense, turned, theirs = call(
        dense_kernel,
        (shape((cells, genes), bf16), shape((rank, cells), bf16), shape((share, genes), i16)),
        [SMEM] + [HBM] * 4,
        scratch=[
            (pltpu.SMEM((slots,), i32), pltpu.SMEM((slots,), i32)),
            pltpu.VMEM((slots, tile, tile), bf16),
            pltpu.VMEM((cells, rank), bf16),
            pltpu.SemaphoreType.DMA((3,)),
            pltpu.SemaphoreType.DMA((slots // 16 if slots % 16 == 0 else 1,)),
        ],
        flops=flops // 2,
        nbytes=8 * MIB,
    )(tile_counts, *(pltpu.with_memory_space_constraint(x, pltpu.HBM) for x in (tile_rows, tile_cols, sketch, tiles)))
    got = to_core(theirs)
    mine = call(own_kernel, shape((share, genes), f32), [VMEM, VMEM], flops=flops // 2, nbytes=5 * MIB)(turned, dense)
    chips = n_cells // CORES
    chunk = genes // chips
    one = halves(genes) if bits > 1 else (shape((rows, genes), i16),)
    pieces = call(
        functools.partial(pair_kernel, chips),
        (shape((lead, chunk), f32),) + (shape((lead, chunk), i16),) * (chips - 1) + one,
        [VMEM, VMEM],
        nbytes=3 * MIB,
    )(mine, got)
    direct, half = pieces[:chips], pieces[chips:]

    width = genes
    for bit in range(bits - 1):
        width //= 2
        outs = halves(width) if bit < bits - 2 else (shape((rows, width), i16),)
        half = call(functools.partial(add_kernel, bit + 1), outs, [VMEM, VMEM], nbytes=MIB)(
            half[0], to_chip(half[1], 1 << bit)
        )
    came = [to_chip(direct[k], k) for k in reversed(range(1, chips))]
    summed = call(direct_cast_kernel, shape((lead, chunk), bf16), [VMEM] * chips, nbytes=MIB)(direct[0], *came)
    crossed = to_chip(half[-1], chips // 2)
    spread = [to_chip(summed, k) for k in reversed(range(1, chips))][::-1]
    held = [call(cast_kernel, shape((rows, width), bf16), [VMEM, VMEM], nbytes=MIB)(half[-1], crossed)]
    *spread, _ = lax.optimization_barrier((*spread, held[0]))
    first = call(join_kernel, shape((lead, genes), bf16), [VMEM] * chips, nbytes=MIB)(summed, *spread)
    masks = [0]
    for bit in reversed(range(bits - 1)):
        held = held + [to_chip(x, 1 << bit) for x in held]
        masks += [mask ^ (1 << bit) for mask in masks]
    theirs = [to_core(x) for x in held]
    gene = call(
        functools.partial(gene_kernel, masks), shape((rank, genes), bf16), [VMEM] * (2 + 2 * len(held)), nbytes=2 * MIB
    )(first, to_core(first), *held, *theirs)

    def cell(k, gene):
        kind = f32 if k == 0 else i16
        return call(
            functools.partial(cell_kernel, k),
            shape((height, rank), kind),
            [VMEM, VMEM],
        )(dense, gene)

    got = []
    for k in (n_genes - 1, *range(1, n_genes - 1)):
        got.append(to_gene(cell(k, gene), k))
    total = cell(0, gene)
    for x in got:
        total = call(more_kernel, shape((height, rank), f32), [VMEM, VMEM], nbytes=16 * MIB)(total, x)
    return total


def solution(mesh):
    in_specs = (
        P("cells", None),
        P(("cells", "genes"), None, None),
        P(("cells", "genes")),
        P(("cells", "genes")),
        P(("cells", "genes")),
    )
    out_specs = P(("cells", "genes"), None)
    body = functools.partial(local, mesh.shape["cells"], mesh.shape["genes"])
    return jax.shard_map(body, mesh=mesh, in_specs=in_specs, out_specs=out_specs, check_vma=False)
```
